32 devices in a mesh: tm: 32 (over z, y, x, core).
Axes of the slice: x: 2, y: 2, z: 4, core: 2. Of those that a mesh axis runs over, the one named last changes fastest.
Arguments:
- inputs: float32 [16, 2048, 512], P(None, 'tm'), may hold values from -39 to 39
- lengths: int32 [16], replicated, may hold values from 1024 to 2048, as said below
- cotangent: float32 [16, 2048, 512], P(None, 'tm'), may hold values from -6 to 6
- bn_gain: float32 [2, 512], replicated, may hold values from 0.5 to 1.5
- bn_bias: float32 [2, 512], replicated, may hold values from -2.5 to 2.5
- running: float32 [2, 2, 512], replicated, may hold values from 0.5 to 1.5
- w_in: bfloat16 [2, 512, 512], replicated, may hold values from -0.25 to 0.25
- nu_log: float32 [2, 256], replicated, as said below
- phase: float32 [2, 256], replicated, may hold values from 0.01 to 3
- w_out: bfloat16 [2, 512, 512], replicated, may hold values from -0.25 to 0.25
- skip: float32 [2, 512], replicated, may hold values from -3 to 3
- w_glu: bfloat16 [2, 512, 1024], replicated, may hold values from -0.25 to 0.25
Outputs:
- output: float32 [16, 2048, 512], P(None, 'tm')
- grad_x: float32 [16, 2048, 512], P(None, 'tm')
- g_bn_gain: float32 [2, 512], replicated
- g_bn_bias: float32 [2, 512], replicated
- g_w_in: float32 [2, 512, 512], replicated
- g_nu_log: float32 [2, 256], replicated
- g_phase: float32 [2, 256], replicated
- g_w_out: float32 [2, 512, 512], replicated
- g_skip: float32 [2, 512], replicated
- g_w_glu: float32 [2, 512, 1024], replicated
- running_out: float32 [2, 2, 512], replicated
The draws below stay inside these ranges and needn't reach their ends.
Inputs may be any that keep to these rules, and one draw needn't show every extreme that they name: `lengths`: each sequence's valid steps come first; in every draw one sequence has exactly 2048 valid steps. exp(nu_log) lies between 0.1 / 2048 and 1 / 30.
All inputs are finite; a program needn't handle non-finite values.
Results may differ from the reference program's by a relative error of at most 0.015.
Values sent between devices are 32-bit elements; how exact they have to be, the bound alone decides.
No kernel may reach another device: no remote copies, remote signals or barrier semaphores. Data moves between devices by JAX's collectives and lax.ppermute only.
A program may use at most 192 MiB of HBM per device.

```python
import math
import jax
import jax.numpy as jnp
from jax import lax

D = 512
STATES = 256
SPAN = 64
SEQS = 16
SEQ = 2048


def draw_inputs(key, part):
    key = jax.random.fold_in(key, 11)
    key_offset, key_scale, key_noise = jax.random.split(key, 3)
    ramp = 1.0 + 2.0 * jnp.arange(SEQ, dtype=jnp.float32)[None, :, None] / SEQ
    scales = jnp.exp(jax.random.uniform(key_scale, (1, 1, D), jnp.float32, math.log(0.3), math.log(3.0)))
    offsets = jnp.clip(0.5 * jax.random.normal(key_offset, (1, 1, D), jnp.float32), -3.0, 3.0)
    noise = jnp.clip(jax.random.normal(key_noise, (SEQS, SEQ, D), jnp.float32), -4.0, 4.0)
    return offsets + scales * ramp * noise


def draw_lengths(key, part):
    key = jax.random.fold_in(key, 12)
    key_base, key_pick = jax.random.split(key, 2)
    half_length = SEQ // 2
    base = half_length + jax.random.randint(key_base, (SEQS,), 0, half_length + 1)
    picked = jax.random.randint(key_pick, (), 0, SEQS)
    order = jnp.arange(SEQS)
    base = jnp.where(order == picked, SEQ, base)
    return base.astype(jnp.int32)


def draw_nu_log(key, part):
    key = jax.random.fold_in(key, 13)
    key_slow = jax.random.fold_in(key, 0)
    lower_end = math.log(0.1 / SEQ)
    upper_end = math.log(1.0 / 30.0)
    return jax.random.uniform(key_slow, (2, STATES), jnp.float32, lower_end, upper_end)


def level_of(own_key, extent, cuts, low, largest):
    def one(position, blocks):
        draws = jax.random.uniform(jax.random.fold_in(jax.random.fold_in(own_key, 6), position), (blocks,), jnp.float32, low / len(cuts), largest / len(cuts))
        return jnp.repeat(jnp.exp(draws), extent[position] // blocks).reshape((-1,) + (1,) * (len(extent) - position - 1))

    level = one(*cuts[0])
    for cut in cuts[1:]:
        level = level * one(*cut)
    return level


def gaussian(key, extent, scale, bound, shards=(), held_as=jnp.bfloat16):
    factor_of = level_of(key, extent, shards, -0.22, 0.18) if shards else 1.0
    array = jax.random.normal(key, extent, jnp.float32) * scale * factor_of
    return jnp.minimum(jnp.maximum(array, -bound), bound).astype(held_as)


def setup_inputs(seed: int = 0) -> dict:
    key_of = jax.random.split(jax.random.key(seed), 13)
    inputs = draw_inputs(jax.random.fold_in(key_of[12], 71), 0)
    lengths = draw_lengths(jax.random.fold_in(key_of[12], 71), 0)
    cotangent = gaussian(key_of[2], (SEQS, SEQ, D), 1.0, 6.0, ((1, 32),), jnp.float32)
    bn_gain = jnp.clip(1.0 + 0.1 * jax.random.normal(key_of[3], (2, D), jnp.float32), 0.5, 1.5)
    bn_bias = gaussian(key_of[4], (2, D), 0.5, 2.5, (), jnp.float32)
    running = jnp.clip(jax.random.uniform(key_of[5], (2, 2, D), jnp.float32, 0.5, 1.5), 0.5, 1.5)
    w_in = gaussian(key_of[6], (2, D, 2 * STATES), D ** -0.5, 0.25)
    nu_log = draw_nu_log(jax.random.fold_in(key_of[12], 71), 0)
    phase = jnp.clip(jax.random.uniform(key_of[8], (2, STATES), jnp.float32, 0.01, 3.0), 0.01, 3.0)
    w_out = gaussian(key_of[9], (2, 2 * STATES, D), (2 * STATES) ** -0.5, 0.25)
    skip = gaussian(key_of[10], (2, D), 1.0, 3.0, (), jnp.float32)
    w_glu = gaussian(key_of[11], (2, D, 2 * D), D ** -0.5, 0.25)
    return dict(inputs=inputs, lengths=lengths, cotangent=cotangent, bn_gain=bn_gain, bn_bias=bn_bias, running=running, w_in=w_in, nu_log=nu_log, phase=phase, w_out=w_out, skip=skip, w_glu=w_glu)


norm_epsilon = 1e-05
momentum = 0.1

@jax.custom_vjp
def low(v):
    return lax.optimization_barrier(v.astype(jnp.bfloat16)).astype(jnp.float32)

@jax.custom_vjp
def low_back(v):
    return v

def low_keep(v):
    return (low(v), None)

def low_pass(kept, grad):
    return (grad,)

def back_keep(v):
    return (v, None)

def back_low(kept, grad):
    return (low(grad),)
low.defvjp(low_keep, low_pass)
low_back.defvjp(back_keep, back_low)

def product(left, right):
    return jnp.einsum('std,dk->stk', left, right, precision=lax.Precision.HIGHEST)

def chain_states(members, backward):
    if backward:
        members = tuple((jnp.flip(member, 1) for member in members))
    blocks = SEQ // SPAN
    states = members[0].shape[-1]

    def to_blocks(member):
        return jnp.moveaxis(member.reshape(SEQS, blocks, SPAN, states), 1, 0)

    def one_block(carry, pieces):

        def one_step(inner, item):
            factor_re, factor_im, drive_re, drive_im = item
            state_re, state_im = inner
            next_re = factor_re * state_re - factor_im * state_im + drive_re
            next_im = factor_re * state_im + factor_im * state_re + drive_im
            return ((next_re, next_im), (next_re, next_im))
        inner_steps = tuple((jnp.moveaxis(piece, 1, 0) for piece in pieces))
        carry, history = lax.scan(one_step, carry, inner_steps)
        return (carry, tuple((jnp.moveaxis(member, 0, 1) for member in history)))
    start = (jnp.zeros((SEQS, states), jnp.float32), jnp.zeros((SEQS, states), jnp.float32))
    ending, history = lax.scan(jax.checkpoint(one_block), start, tuple((to_blocks(member) for member in members)))
    result = tuple((jnp.moveaxis(member, 0, 1).reshape(SEQS, SEQ, states) for member in history))
    if backward:
        result = tuple((jnp.flip(member, 1) for member in result))
    return result

def lru_block(hidden, valid, token_count, gain, bias, w_in, nu_log, phase, w_out, skip, w_glu, backward):
    width = hidden.shape[-1]
    states = nu_log.shape[0]
    valid_col = valid[:, :, None]
    batch_mean = lax.optimization_barrier(jnp.sum(valid_col * hidden, axis=(0, 1))) / token_count
    batch_var = lax.optimization_barrier(jnp.sum(valid_col * hidden * hidden, axis=(0, 1))) / token_count - batch_mean * batch_mean
    scaled = (hidden - batch_mean) * lax.rsqrt(batch_var + norm_epsilon) * gain + bias
    projected = low_back(product(low(scaled), w_in))
    decay_rate = jnp.exp(nu_log)
    radius = jnp.exp(-decay_rate)
    gamma_norm = jnp.sqrt(-jnp.expm1(-2.0 * decay_rate))
    factor_re = jnp.where(valid_col > 0, radius * jnp.cos(phase), 1.0)
    factor_im = jnp.where(valid_col > 0, radius * jnp.sin(phase), 0.0)
    drive_re = valid_col * gamma_norm * projected[..., :states]
    drive_im = valid_col * gamma_norm * projected[..., states:]
    state_re, state_im = chain_states((factor_re, factor_im, drive_re, drive_im), backward)
    both_parts = low(jnp.concatenate([state_re, state_im], -1))
    lru_out = low_back(product(both_parts, w_out) + skip * scaled)
    glu_in = low_back(product(low(jax.nn.gelu(lru_out, approximate=False)), w_glu))
    result = hidden + glu_in[..., :width] * jax.nn.sigmoid(glu_in[..., width:])
    return (result, (batch_mean, batch_var))

def reference(inputs, lengths, cotangent, bn_gain, bn_bias, running, w_in, nu_log, phase, w_out, skip, w_glu):
    valid = (jnp.arange(SEQ, dtype=jnp.int32)[None, :] < lengths[:, None]).astype(jnp.float32)
    token_count = jnp.sum(lengths).astype(jnp.float32)
    weights = (bn_gain, bn_bias, w_in.astype(jnp.float32), nu_log, phase, w_out.astype(jnp.float32), skip, w_glu.astype(jnp.float32))

    def forward(hidden, params):
        moments_all = []
        for layer_index in range(2):
            hidden, moments = lru_block(hidden, valid, token_count, params[0][layer_index], params[1][layer_index], params[2][layer_index], params[3][layer_index], params[4][layer_index], params[5][layer_index], params[6][layer_index], params[7][layer_index], layer_index == 1)
            moments_all.append(moments)
        return (hidden, moments_all)
    output, pullback, moments_all = jax.vjp(forward, inputs, weights, has_aux=True)
    grad_x, grads = pullback(cotangent)
    running_out = jnp.stack([jnp.stack([(1.0 - momentum) * running[layer_index, 0] + momentum * moments_all[layer_index][0], (1.0 - momentum) * running[layer_index, 1] + momentum * moments_all[layer_index][1] * token_count / (token_count - 1.0)]) for layer_index in range(2)])
    return (output, grad_x, grads[0], grads[1], grads[2], grads[3], grads[4], grads[5], grads[6], grads[7], running_out)
```

```python
import functools

import jax
import jax.numpy as jnp
from jax import lax
from jax.experimental import pallas as pl
from jax.experimental.pallas import tpu as pltpu
from jax.sharding import PartitionSpec as P

norm_epsilon = 1e-05
momentum = 0.1
inverse_root_two = 0.7071067811865476
density_scale = 0.3989422804014327
F32, BF16 = jnp.float32, jnp.bfloat16
LANES = 128
MIB = 1 << 20


def dot(left, right):
    return jnp.dot(left, right, preferred_element_type=F32)


def dot_nt(left, right):
    return lax.dot_general(left, right, (((1,), (1,)), ((), ())), preferred_element_type=F32)


def run(body, outs, operands, scalars=(), scratch=(), limit=40):
    vmem = pl.BlockSpec(memory_space=pltpu.VMEM)
    smem = pl.BlockSpec(memory_space=pltpu.SMEM)
    return pl.pallas_call(
        body,
        out_shape=[jax.ShapeDtypeStruct(shape, dtype) for shape, dtype in outs],
        in_specs=[smem] * len(scalars) + [vmem] * len(operands),
        out_specs=[vmem] * len(outs),
        scratch_shapes=list(scratch),
        compiler_params=pltpu.CompilerParams(vmem_limit_bytes=limit * MIB),
    )(*scalars, *operands)


def radices(count):
    out = []
    while count > 1:
        radix = 2 if not out or count % 4 else 4
        out.append(radix)
        count //= radix
    return out


def stages(count):
    stride, out = 1, []
    for radix in radices(count):
        out.append((radix, stride))
        stride *= radix
    return out


def swap(value, count, stride, mask):
    return lax.ppermute(value, "tm", [(i, i ^ (stride * mask)) for i in range(count)])


def rows_to_tile(first, second):
    pieces = [
        row[:, j : j + LANES] for row in (first, second) for j in range(0, row.shape[1], LANES)
    ]
    return jnp.concatenate(pieces, axis=0)


def tile_to_rows(tile):
    half = tile.shape[0] // 2
    return [
        jnp.concatenate([tile[base + j : base + j + 1, :] for j in range(half)], axis=1)
        for base in (0, half)
    ]


def spread(ref, first, second):
    ref[...] = jnp.broadcast_to(rows_to_tile(first, second)[None], ref.shape)


def gathered(ref):
    return tile_to_rows(jnp.sum(ref[...], axis=0))


def everywhere(tiles):
    return lax.all_to_all(tiles, "tm", 0, 0)


def mul(ar, ai, br, bi):
    return ar * br - ai * bi, ar * bi + ai * br


def members(refs, place, buffer):
    for offset, ref in enumerate(refs):
        buffer[jnp.bitwise_xor(place, offset)] = ref[...]


def pass_through(buffer, factor, place, state, backward, conj):
    radix, _, width = buffer.shape
    states = width // 2
    if state is None:
        zero = jnp.zeros(buffer.shape[1:-1] + (states,), F32)
        state = (zero, zero)
    entering = state
    for member in range(radix - 1, -1, -1) if backward else range(radix):
        entering = tuple(jnp.where(place == member, s, e) for s, e in zip(state, entering))
        fr, fi = factor[member, :, :states], factor[member, :, states:]
        moved = mul(fr, -fi if conj else fi, *state)
        state = (moved[0] + buffer[member, :, :states], moved[1] + buffer[member, :, states:])
    return entering, state


def total_body(backward, conj, place_ref, *refs):
    radix = len(refs) - 3
    factor, out, buffer = refs[radix], refs[radix + 1], refs[radix + 2]
    place = place_ref[0]
    members(refs[:radix], place, buffer)
    _, (re, im) = pass_through(buffer, factor, place, None, backward, conj)
    states = re.shape[1]
    out[:, :states] = re
    out[:, states:] = im


def exchange(summary, plan, factors, places, backward, conj):
    count = lax.axis_size("tm")
    held = []
    value = summary
    for level, (radix, stride) in enumerate(plan):
        group = [value] + [swap(value, count, stride, mask) for mask in range(1, radix)]
        held.append(group)
        if level + 1 < len(plan):
            (value,) = run(
                functools.partial(total_body, backward, conj),
                [(summary.shape, F32)],
                group + [factors[level]],
                [places[level]],
                [pltpu.VMEM((radix,) + summary.shape, F32)],
                limit=8,
            )
    return held


def entry_operands(held, factors):
    return [value for group in held for value in group] + list(factors)


def entry_scratch(plan, shape):
    return [pltpu.VMEM((radix,) + shape, F32) for radix, _ in plan]


def entering_state(plan, places, refs, buffers, backward, conj):
    total = sum(radix for radix, _ in plan)
    values, factors = refs[:total], refs[total : total + len(plan)]
    start, groups = 0, []
    for radix, _ in plan:
        groups.append(values[start : start + radix])
        start += radix
    state = None
    for level in range(len(plan) - 1, -1, -1):
        members(groups[level], places[level][0], buffers[level])
        state, _ = pass_through(
            buffers[level], factors[level], places[level][0], state, backward, conj
        )
    return state


def steps(span, backward, body, start, unroll=8):
    def one(k, carry):
        return body(span - 1 - k if backward else k, carry)

    return lax.fori_loop(0, span, one, start, unroll=unroll)


def at(t, seqs):
    return pl.ds(pl.multiple_of(t * seqs, seqs), seqs)


def state_scan(v_ref, rel, lr, li, start, span, backward, keep=None):
    seqs, states = lr.shape

    def body(t, carry):
        re, im = carry
        vr, vi = v_ref[at(t, seqs), :states], v_ref[at(t, seqs), states:]
        next_re, next_im = mul(lr, li, re, im)
        live = rel > t
        re, im = jnp.where(live, next_re + vr, re), jnp.where(live, next_im + vi, im)
        if keep is not None:
            keep(t, re, im)
        return re, im

    return steps(span, backward, body, start)


def adjoint_scan(g_ref, rel, lr, li, start, span, backward, use=None, extra=()):
    seqs, states = lr.shape

    def body(t, carry):
        (re, im), kept = carry
        ar, ai = g_ref[at(t, seqs), :states] + re, g_ref[at(t, seqs), states:] + im
        live = rel > t
        if use is not None:
            kept = use(t, ar, ai, live, kept)
        next_re, next_im = mul(lr, -li, ar, ai)
        return (jnp.where(live, next_re, ar), jnp.where(live, next_im, ai)), kept

    return steps(span, backward, body, (start, extra))


def wide(ref, row, shape):
    return jnp.broadcast_to(ref[row : row + 1, :], shape)


def to_time_major(piece):
    seqs, span, width = piece.shape
    return jnp.swapaxes(piece, 0, 1).reshape(span * seqs, width)


def from_time_major(rows, seqs):
    return jnp.swapaxes(rows.reshape(-1, seqs, rows.shape[-1]), 0, 1)


def lane_tiled(column, width):
    return jnp.concatenate([column] * (width // LANES), axis=1)


def gelu_parts(y):
    cdf = 0.5 * (1.0 + lax.erf(y * inverse_root_two))
    pdf = jnp.exp(-0.5 * y * y) * density_scale
    return y * cdf, cdf + y * pdf


def sigmoid(x):
    return 1.0 / (1.0 + jnp.exp(-x))


CHUNK = 16


def prepare_body(plan, span, rel_ref, counts_ref, x_ref, decay_ref, *outs):
    sums_ref, tm_ref, mask_ref = outs[:3]
    factor_refs = outs[3:]
    seqs, _, width = x_ref.shape
    states = decay_ref.shape[-1]
    rel = jnp.broadcast_to(rel_ref[...], (seqs, LANES))
    first = jnp.zeros((seqs, width), F32)
    second = jnp.zeros((seqs, width), F32)
    for t0 in range(0, span, 8):
        piece = jnp.swapaxes(x_ref[:, t0 : t0 + 8, :], 0, 1)
        for j in range(8):
            rows = piece[j]
            mask = jnp.where(rel > t0 + j, 1.0, 0.0)
            place = slice((t0 + j) * seqs, (t0 + j + 1) * seqs)
            mask_ref[place, :] = mask
            tm_ref[place, :] = rows
            live = rows * lane_tiled(mask, width)
            first += live
            second += live * rows
    spread(sums_ref, jnp.sum(first, 0, keepdims=True), jnp.sum(second, 0, keepdims=True))
    for k in range(2):
        row = 0
        for level, (radix, stride) in enumerate(plan):
            for member in range(radix):
                count = jnp.broadcast_to(counts_ref[row], (seqs, states))
                row += 1
                power = (decay_ref[k, 0:1, :], decay_ref[k, 1:2, :])
                re, im = jnp.ones((seqs, states), F32), jnp.zeros((seqs, states), F32)
                for bit in range((span * stride).bit_length()):
                    taken = jnp.bitwise_and(count, 1 << bit) != 0
                    next_re, next_im = mul(re, im, *power)
                    re, im = jnp.where(taken, next_re, re), jnp.where(taken, next_im, im)
                    power = mul(*power, *power)
                ref = factor_refs[k * len(plan) + level]
                ref[member, :, :states] = re
                ref[member, :, states:] = im


def project_body(
    k, span, backward, tokens, rel_ref, sums_ref, x_ref, gain_ref, bias_ref, w_ref, decay_ref,
    u_ref, v_ref, stats_ref, summary_ref,
):
    seqs = rel_ref.shape[0]
    states = decay_ref.shape[-1]
    total, squares = gathered(sums_ref)
    scale = tokens[0]
    mean = total * scale
    var = squares * scale - mean * mean
    rstd = lax.rsqrt(var + norm_epsilon)
    stats_ref[0:1, :] = mean
    stats_ref[1:2, :] = var
    stats_ref[2:3, :] = rstd
    stats_ref[3:4, :] = rstd * gain_ref[k : k + 1, :]
    slope = rstd * gain_ref[k : k + 1, :]
    bias = bias_ref[k : k + 1, :]
    step = CHUNK * seqs
    for r in range(0, span * seqs, step):
        u = ((x_ref[r : r + step, :] - mean) * slope + bias).astype(BF16)
        u_ref[r : r + step, :] = u
        v_ref[r : r + step, :] = dot(u, w_ref[k])
    shape = (seqs, states)
    rel = jnp.broadcast_to(rel_ref[...], shape)
    lr, li = wide(decay_ref.at[k], 0, shape), wide(decay_ref.at[k], 1, shape)
    zero = jnp.zeros(shape, F32)
    re, im = state_scan(v_ref, rel, lr, li, (zero, zero), span, backward)
    summary_ref[:, :states] = re
    summary_ref[:, states:] = im


def rebuild_states(k, plan, span, backward, places, refs, buffers, rel, v_ref, decay_ref, h_ref):
    seqs, states = rel.shape
    lr, li, gamma = (wide(decay_ref.at[k], row, rel.shape) for row in range(3))
    start = entering_state(plan, places, refs, buffers, backward, False)

    lead = 0 if backward else 1

    def keep(t, re, im):
        h_ref[at(t + lead, seqs), :states] = (re * gamma).astype(BF16)
        h_ref[at(t + lead, seqs), states:] = (im * gamma).astype(BF16)

    keep(span if backward else -1, *start)
    state_scan(v_ref, rel, lr, li, start, span, backward, keep)


def forward_body(
    k, plan, span, place_refs, exch, rel_ref, v_ref, x_ref, u_ref, mask_ref, stats_ref, bias_ref,
    decay_ref, w_out_ref, skip_ref, w_glu_ref,
    out_ref, h_ref, act_ref, slope_ref, gate_ref, value_ref, sums_ref, buffers,
):
    seqs = rel_ref.shape[0]
    width = x_ref.shape[1]
    states = decay_ref.shape[-1]
    rel = jnp.broadcast_to(rel_ref[...], (seqs, states))
    rebuild_states(k, plan, span, False, place_refs, exch, buffers, rel, v_ref, decay_ref, h_ref)
    mean, scale = stats_ref[0:1, :], stats_ref[3:4, :]
    bias, skip = bias_ref[k : k + 1, :], skip_ref[k : k + 1, :]
    step = CHUNK * seqs
    first = jnp.zeros((8, width), F32)
    second = jnp.zeros((8, width), F32)
    for r in range(0, span * seqs, step):
        x = x_ref[r : r + step, :]
        u = (x - mean) * scale + bias
        y = dot(h_ref[r + seqs : r + seqs + step, :], w_out_ref[k]) + skip * u
        act, slope = gelu_parts(y)
        act = act.astype(BF16)
        act_ref[r : r + step, :] = act
        slope_ref[r : r + step, :] = slope.astype(BF16)
        z = dot(act, w_glu_ref[k])
        value, gate = z[:, :width], sigmoid(z[:, width:])
        gated = value * gate
        out = x + gated
        out_ref[r : r + step, :] = out
        gate_ref[r : r + step, :] = gate.astype(BF16)
        value_ref[r : r + step, :] = (gated * (1.0 - gate)).astype(BF16)
        live = out * lane_tiled(mask_ref[r : r + step, :], width)
        first += jnp.sum(live.reshape(-1, 8, width), 0)
        second += jnp.sum((live * out).reshape(-1, 8, width), 0)
    spread(sums_ref, jnp.sum(first, 0, keepdims=True), jnp.sum(second, 0, keepdims=True))


def back_rows(k, r, step, dza, dzb, slope, width, w_glu_ref, w_out_ref, dz_ref, dy_ref, g_ref):
    dza, dzb = dza.astype(BF16), dzb.astype(BF16)
    dz_ref[r : r + step, :width] = dza
    dz_ref[r : r + step, width:] = dzb
    w = w_glu_ref[k]
    dact = dot_nt(dza, w[:, :width]) + dot_nt(dzb, w[:, width:])
    dy = (dact * slope).astype(BF16)
    dy_ref[r : r + step, :] = dy
    g_ref[r : r + step, :] = dot_nt(dy, w_out_ref[k])


def local_adjoint(k, span, backward, rel, g_ref, decay_ref, summary_ref):
    seqs, states = rel.shape
    lr, li = wide(decay_ref.at[k], 0, rel.shape), wide(decay_ref.at[k], 1, rel.shape)
    zero = jnp.zeros(rel.shape, F32)
    (re, im), _ = adjoint_scan(g_ref, rel, lr, li, (zero, zero), span, backward)
    summary_ref[:, :states] = re
    summary_ref[:, states:] = im


def turn_body(
    k, plan, span, place_refs, exch, rel_ref, v_ref, x_ref, u_ref, cot_ref, stats_ref, bias_ref,
    decay_ref, w_out_ref, skip_ref, w_glu_ref,
    out_ref, h_ref, act_ref, dz_ref, dy_ref, g_ref, summary_ref, buffers,
):
    seqs = rel_ref.shape[0]
    width = x_ref.shape[1]
    states = decay_ref.shape[-1]
    rel = jnp.broadcast_to(rel_ref[...], (seqs, states))
    rebuild_states(k, plan, span, True, place_refs, exch, buffers, rel, v_ref, decay_ref, h_ref)
    mean, scale = stats_ref[0:1, :], stats_ref[3:4, :]
    bias, skip = bias_ref[k : k + 1, :], skip_ref[k : k + 1, :]
    step = CHUNK * seqs
    for r in range(0, span * seqs, step):
        t0 = r // seqs
        x = x_ref[r : r + step, :]
        u = (x - mean) * scale + bias
        y = dot(h_ref[r : r + step, :], w_out_ref[k]) + skip * u
        act, slope = gelu_parts(y)
        act = act.astype(BF16)
        act_ref[r : r + step, :] = act
        z = dot(act, w_glu_ref[k])
        value, gate = z[:, :width], sigmoid(z[:, width:])
        gated = value * gate
        out_ref[:, t0 : t0 + CHUNK, :] = from_time_major(x + gated, seqs)
        d = to_time_major(cot_ref[:, t0 : t0 + CHUNK, :])
        back_rows(
            k, r, step, d * gate, d * (gated * (1.0 - gate)), slope, width,
            w_glu_ref, w_out_ref, dz_ref, dy_ref, g_ref,
        )
    local_adjoint(k, span, False, rel, g_ref, decay_ref, summary_ref)


def back_body(
    k, span, backward, tokens, rel_ref, sums_ref, part_ref, x_ref, mask_ref, stats_ref, slope_ref,
    gate_ref, value_ref, gain_ref, decay_ref, w_out_ref, w_glu_ref,
    d_ref, dz_ref, dy_ref, g_ref, grads_ref, summary_ref,
):
    seqs = rel_ref.shape[0]
    width = x_ref.shape[1]
    states = decay_ref.shape[-1]
    rel = jnp.broadcast_to(rel_ref[...], (seqs, states))
    shift, tilt = input_terms(k + 1, tokens, sums_ref, stats_ref, gain_ref, grads_ref)
    mean = stats_ref[0:1, :]
    step = CHUNK * seqs
    for r in range(0, span * seqs, step):
        live = lane_tiled(mask_ref[r : r + step, :], width)
        d = part_ref[r : r + step, :] + live * (shift + tilt * (x_ref[r : r + step, :] - mean))
        d_ref[r : r + step, :] = d
        back_rows(
            k, r, step, d * gate_ref[r : r + step, :].astype(F32),
            d * value_ref[r : r + step, :].astype(F32), slope_ref[r : r + step, :].astype(F32), width,
            w_glu_ref, w_out_ref, dz_ref, dy_ref, g_ref,
        )
    local_adjoint(k, span, backward, rel, g_ref, decay_ref, summary_ref)


def input_terms(k, tokens, sums_ref, stats_ref, gain_ref, grads_ref):
    bias_grad, gain_grad = gathered(sums_ref)
    grads_ref[0:1, :] = gain_grad
    grads_ref[1:2, :] = bias_grad
    rstd = stats_ref[2:3, :]
    gain = gain_ref[k : k + 1, :]
    scale = tokens[0]
    return -rstd * gain * bias_grad * scale, -rstd * rstd * gain * gain_grad * scale


def adjoint_body(
    k, plan, span, backward, seq_major, place_refs, exch, rel_ref, g_ref, h_ref, v_ref, dy_ref, x_ref,
    d_ref, stats_ref, gain_ref, bias_ref, decay_ref, w_in_ref, skip_ref,
    dv_ref, part_ref, small_ref, sums_ref, buffers,
):
    seqs = rel_ref.shape[0]
    width = x_ref.shape[1]
    states = decay_ref.shape[-1]
    rel = jnp.broadcast_to(rel_ref[...], (seqs, states))
    lr, li, gamma = (wide(decay_ref.at[k], row, rel.shape) for row in range(3))
    start = entering_state(plan, place_refs, exch, buffers, backward, True)
    before = 0 if backward else 1

    def use(t, ar, ai, live, kept):
        ar, ai = jnp.where(live, ar, 0.0), jnp.where(live, ai, 0.0)
        dv_ref[at(t, seqs), :states] = (ar * gamma).astype(BF16)
        dv_ref[at(t, seqs), states:] = (ai * gamma).astype(BF16)
        pr = h_ref[at(t + before, seqs), :states].astype(F32)
        pi = h_ref[at(t + before, seqs), states:].astype(F32)
        vr, vi = v_ref[at(t, seqs), :states], v_ref[at(t, seqs), states:]
        return (
            kept[0] + (ar * pr + ai * pi),
            kept[1] + (ai * pr - ar * pi),
            kept[2] + (ar * vr + ai * vi),
        )

    zero = jnp.zeros(rel.shape, F32)
    _, kept = adjoint_scan(g_ref, rel, lr, li, start, span, backward, use, (zero, zero, zero))
    mean, scale, rstd = stats_ref[0:1, :], stats_ref[3:4, :], stats_ref[2:3, :]
    gain, bias, skip = (ref[k : k + 1, :] for ref in (gain_ref, bias_ref, skip_ref))
    step = CHUNK * seqs
    first = jnp.zeros((8, width), F32)
    second = jnp.zeros((8, width), F32)
    third = jnp.zeros((8, width), F32)
    for r in range(0, span * seqs, step):
        xhat = (x_ref[r : r + step, :] - mean) * rstd
        dy = dy_ref[r : r + step, :].astype(F32)
        du = dot_nt(dv_ref[r : r + step, :], w_in_ref[k]) + dy * skip
        first += jnp.sum(du.reshape(-1, 8, width), 0)
        second += jnp.sum((du * xhat).reshape(-1, 8, width), 0)
        third += jnp.sum((dy * (xhat * gain + bias)).reshape(-1, 8, width), 0)
        if seq_major:
            d = to_time_major(d_ref[:, r // seqs : r // seqs + CHUNK, :])
        else:
            d = d_ref[r : r + step, :]
        part_ref[r : r + step, :] = d + du * scale
    spread(sums_ref, jnp.sum(first, 0, keepdims=True), jnp.sum(second, 0, keepdims=True))
    small_ref[...] = jnp.zeros_like(small_ref)
    for j in range(2):
        small_ref[0:1, j * states : (j + 1) * states] = jnp.sum(kept[j], 0, keepdims=True)
    small_ref[1:2, :states] = jnp.sum(kept[2], 0, keepdims=True)
    small_ref[2:3, :] = jnp.sum(third, 0, keepdims=True)


def finish_body(
    k, span, tokens, sums_ref, part_ref, x_ref, mask_ref, stats_ref, gain_ref, out_ref, grads_ref
):
    seqs = out_ref.shape[0]
    width = x_ref.shape[1]
    shift, tilt = input_terms(k, tokens, sums_ref, stats_ref, gain_ref, grads_ref)
    mean = stats_ref[0:1, :]
    step = CHUNK * seqs
    for r in range(0, span * seqs, step):
        live = lane_tiled(mask_ref[r : r + step, :], width)
        d = part_ref[r : r + step, :] + live * (shift + tilt * (x_ref[r : r + step, :] - mean))
        out_ref[:, r // seqs : r // seqs + CHUNK, :] = from_time_major(d, seqs)


def with_entry(body, plan, n_out):
    def wrapped(*refs):
        n_exch = sum(radix for radix, _ in plan) + len(plan)
        places, rest = refs[: len(plan)], refs[len(plan) :]
        exch, rest = rest[:n_exch], rest[n_exch:]
        body(places, exch, *rest[: -len(plan)], rest[-len(plan) :])

    return wrapped


def shards(
    inputs, lengths, cotangent, bn_gain, bn_bias, running, w_in, nu_log, phase, w_out, skip, w_glu
):
    seqs, span, width = inputs.shape
    states = nu_log.shape[1]
    count = lax.axis_size("tm")
    here = lax.axis_index("tm")
    rows = span * seqs
    plan = stages(count)
    token_count = jnp.sum(lengths).astype(F32)
    tokens = (1.0 / token_count).reshape(1)
    rel = (lengths - here * span).astype(jnp.int32)[:, None]
    starts, extents = [], []
    places = []
    for radix, stride in plan:
        base = here // (radix * stride) * (radix * stride)
        places.append(((here // stride) % radix).astype(jnp.int32).reshape(1))
        for member in range(radix):
            starts.append((base + member * stride) * span)
            extents.append(stride * span)
    counts = jnp.clip(
        lengths[None, :] - jnp.stack(starts)[:, None], 0, jnp.array(extents, jnp.int32)[:, None]
    )[:, :, None]
    rate = jnp.exp(nu_log)
    radius = jnp.exp(-rate)
    gamma = jnp.sqrt(-jnp.expm1(-2.0 * rate))
    cosine, sine = jnp.cos(phase), jnp.sin(phase)
    decay = jnp.stack([radius * cosine, radius * sine, gamma], axis=1)

    tile = ((count, 2 * width // LANES, LANES), F32)
    whole, whole_low = ((rows, width), F32), ((rows, width), BF16)
    pair, pair_low = ((rows, 2 * states), F32), ((rows, 2 * states), BF16)
    held_low = ((rows + seqs, 2 * states), BF16)
    summary = ((seqs, 2 * states), F32)
    eight = ((8, width), F32)
    buffers = entry_scratch(plan, summary[0])

    prepared = run(
        functools.partial(prepare_body, plan, span),
        [tile, whole, ((rows, LANES), F32)]
        + [((radix,) + summary[0], F32) for _ in range(2) for radix, _ in plan],
        [rel, counts, inputs, decay],
    )
    sums, x0, mask = prepared[:3]
    factors = [prepared[3 : 3 + len(plan)], prepared[3 + len(plan) :]]

    def project(k, sums, x):
        return run(
            functools.partial(project_body, k, span, k == 1),
            [whole_low, pair, eight, summary],
            [rel, everywhere(sums), x, bn_gain, bn_bias, w_in, decay],
            [tokens],
        )

    def entered(body, outs, held, k, operands, limit=48):
        return run(
            with_entry(body, plan, len(outs)),
            outs,
            entry_operands(held, factors[k]) + operands,
            places,
            buffers,
            limit=limit,
        )

    u0, v0, stats0, part = project(0, sums, x0)
    held = exchange(part, plan, factors[0], places, False, False)
    x1, h0, act0, slope0, gate0, value0, sums = entered(
        functools.partial(forward_body, 0, plan, span),
        [whole, held_low, whole_low, whole_low, whole_low, whole_low, tile],
        held,
        0,
        [rel, v0, x0, u0, mask, stats0, bn_bias, decay, w_out, skip, w_glu],
    )
    u1, v1, stats1, part = project(1, sums, x1)
    held = exchange(part, plan, factors[1], places, True, False)
    output, h1, act1, dz1, dy1, g1, part = entered(
        functools.partial(turn_body, 1, plan, span),
        [((seqs, span, width), F32), held_low, whole_low, ((rows, 2 * width), BF16), whole_low, pair, summary],
        held,
        1,
        [rel, v1, x1, u1, cotangent, stats1, bn_bias, decay, w_out, skip, w_glu],
    )
    held = exchange(part, plan, factors[1], places, False, True)
    dv1, part1, small1, sums = entered(
        functools.partial(adjoint_body, 1, plan, span, False, True),
        [pair_low, whole, eight, tile],
        held,
        1,
        [rel, g1, h1, v1, dy1, x1, cotangent, stats1, bn_gain, bn_bias, decay, w_in, skip],
    )
    d0, dz0, dy0, g0, grads1, part = run(
        functools.partial(back_body, 0, span, True),
        [whole, ((rows, 2 * width), BF16), whole_low, pair, eight, summary],
        [rel, everywhere(sums), part1, x1, mask, stats1, slope0, gate0, value0, bn_gain, decay, w_out, w_glu],
        [tokens],
    )
    held = exchange(part, plan, factors[0], places, True, True)
    dv0, part0, small0, sums = entered(
        functools.partial(adjoint_body, 0, plan, span, True, False),
        [pair_low, whole, eight, tile],
        held,
        0,
        [rel, g0, h0, v0, dy0, x0, d0, stats0, bn_gain, bn_bias, decay, w_in, skip],
    )
    grad_x, grads0 = run(
        functools.partial(finish_body, 0, span),
        [((seqs, span, width), F32), eight],
        [everywhere(sums), part0, x0, mask, stats0, bn_gain],
        [tokens],
    )

    def outer(left, right):
        return lax.dot_general(left, right, (((0,), (0,)), ((), ())), preferred_element_type=F32)

    h0, h1 = h0[seqs:], h1[:rows]
    g_glu, g_out, g_in, small = lax.psum(
        (
            jnp.stack([outer(act0, dz0), outer(act1, dz1)]),
            jnp.stack([outer(h0, dy0), outer(h1, dy1)]),
            jnp.stack([outer(u0, dv0), outer(u1, dv1)]),
            jnp.stack([small0, small1]),
        ),
        "tm",
    )
    sum_re, sum_im, g_gamma = small[:, 0, :states], small[:, 0, states:], small[:, 1, :states]
    g_nu = (sum_re * cosine + sum_im * sine) * (-radius * rate) + g_gamma * rate * radius * radius / gamma
    g_phase = radius * (sum_im * cosine - sum_re * sine)
    stats = jnp.stack([stats0, stats1])
    running_out = (1.0 - momentum) * running + momentum * stats[:, :2] * jnp.stack(
        [jnp.ones_like(token_count), token_count / (token_count - 1.0)]
    )[None, :, None]
    grads = jnp.stack([grads0, grads1])
    return (
        output, grad_x, grads[:, 0], grads[:, 1], g_in, g_nu, g_phase, g_out, small[:, 2], g_glu, running_out,
    )


def solution(mesh):
    placed = (P(None, "tm", None), P(), P(None, "tm", None)) + (P(),) * 9
    return jax.shard_map(
        shards,
        mesh=mesh,
        in_specs=placed,
        out_specs=(P(None, "tm", None),) * 2 + (P(),) * 9,
        check_vma=False,
    )
```

```python
import functools
import math

import jax
import jax.numpy as jnp
from jax import lax
from jax.experimental import pallas as pl
from jax.experimental.pallas import tpu as pltpu
from jax.sharding import PartitionSpec as P

norm_epsilon = 1e-05
momentum = 0.1
inverse_root_two = 0.7071067811865476
density_scale = 0.3989422804014327
F32, BF16 = jnp.float32, jnp.bfloat16
LANES = 128
MIB = 1 << 20


def dot(left, right):
    return jnp.dot(left, right, preferred_element_type=F32)


def dot_tn(left, right):
    return lax.dot_general(left, right, (((0,), (0,)), ((), ())), preferred_element_type=F32)


def dot_nt(left, right):
    return lax.dot_general(left, right, (((1,), (1,)), ((), ())), preferred_element_type=F32)


def run(body, outs, operands, after=(), scratch=(), limit=12, macs=0):
    vmem = pl.BlockSpec(memory_space=pltpu.VMEM)
    anywhere = pl.BlockSpec(memory_space=pl.ANY)
    first, second = len(operands), len(operands) + len(after)

    def kernel(*refs):
        body(*refs[:first], *refs[second:])

    return pl.pallas_call(
        kernel,
        out_shape=[jax.ShapeDtypeStruct(shape, dtype) for shape, dtype in outs],
        in_specs=[vmem] * len(operands) + [anywhere] * len(after),
        out_specs=[vmem] * len(outs),
        scratch_shapes=list(scratch),
        compiler_params=pltpu.CompilerParams(vmem_limit_bytes=limit * MIB),
        cost_estimate=pl.CostEstimate(
            flops=2 * macs,
            bytes_accessed=sum(a.size * a.dtype.itemsize for a in operands)
            + sum(math.prod(shape) * jnp.dtype(dtype).itemsize for shape, dtype in outs),
            transcendentals=0,
        ),
    )(*operands, *after)


def radices(count):
    out = []
    while count > 1:
        radix = 2 if not out or count % 4 else 4
        out.append(radix)
        count //= radix
    return out


def stages(count):
    stride, out = 1, []
    for radix in radices(count):
        out.append((radix, stride))
        stride *= radix
    return out


def swap(value, stride, mask):
    count = lax.axis_size("tm")
    return lax.ppermute(value, "tm", [(i, i ^ (stride * mask)) for i in range(count)])


def group_of(value, radix, stride):
    return [value] + [swap(value, stride, mask) for mask in range(1, radix)]


def place_in(radix, stride):
    return lax.rem(lax.div(lax.axis_index("tm"), stride), radix)


def rows_to_tile(first, second):
    pieces = [
        row[:, j : j + LANES] for row in (first, second) for j in range(0, row.shape[1], LANES)
    ]
    return jnp.concatenate(pieces, axis=0)


def tile_to_rows(tile):
    half = tile.shape[0] // 2
    return [
        jnp.concatenate([tile[base + j : base + j + 1, :] for j in range(half)], axis=1)
        for base in (0, half)
    ]


def spread(ref, first, second):
    ref[...] = jnp.broadcast_to(rows_to_tile(first, second)[None], ref.shape)


def gathered(ref):
    return tile_to_rows(jnp.sum(ref[...], axis=0))


def everywhere(tiles):
    return lax.all_to_all(tiles, "tm", 0, 0)


def mul(ar, ai, br, bi):
    return ar * br - ai * bi, ar * bi + ai * br


def members(refs, place, buffer):
    for offset, ref in enumerate(refs):
        buffer[jnp.bitwise_xor(place, offset)] = ref[...]


def pass_through(k, buffer, factor, place, state, backward, conj):
    radix, _, width = buffer.shape
    states = width // 2
    if state is None:
        zero = jnp.zeros(buffer.shape[1:-1] + (states,), F32)
        state = (zero, zero)
    entering = state
    for member in range(radix - 1, -1, -1) if backward else range(radix):
        entering = tuple(jnp.where(place == member, s, e) for s, e in zip(state, entering))
        fr, fi = factor[k, member, :, :states], factor[k, member, :, states:]
        moved = mul(fr, -fi if conj else fi, *state)
        state = (moved[0] + buffer[member, :, :states], moved[1] + buffer[member, :, states:])
    return entering, state


def total_body(k, radix, stride, backward, conj, *refs):
    factor, out, buffer = refs[radix:]
    place = place_in(radix, stride)
    members(refs[:radix], place, buffer)
    _, (re, im) = pass_through(k, buffer, factor, place, None, backward, conj)
    states = re.shape[1]
    out[:, :states] = re
    out[:, states:] = im


def group_total(k, group, level, plan, factors, backward, conj, after=()):
    radix, stride = plan[level]
    shape = group[0].shape
    (total,) = run(
        functools.partial(total_body, k, radix, stride, backward, conj),
        [(shape, F32)],
        list(group) + [factors[level]],
        after,
        [pltpu.VMEM((radix,) + shape, F32)],
        limit=4,
    )
    return total


def exchange(k, summary, plan, factors, backward, conj, between=None):
    held = []
    value = summary
    for level, (radix, stride) in enumerate(plan):
        group = group_of(value, radix, stride)
        held.append(group)
        if level + 1 < len(plan):
            after = between(level, value) if between else ()
            value = group_total(k, group, level, plan, factors, backward, conj, after)
            if between and level + 2 == len(plan):
                between(level + 1, value)
    return held


def entry_operands(held, factors):
    return [value for group in held for value in group] + list(factors)


def entry_scratch(plan, shape):
    return [pltpu.VMEM((radix,) + shape, F32) for radix, _ in plan]


def entering_state(k, plan, refs, buffers, backward, conj):
    total = sum(radix for radix, _ in plan)
    values, factors = refs[:total], refs[total:]
    start, groups = 0, []
    for radix, _ in plan:
        groups.append(values[start : start + radix])
        start += radix
    state = None
    for level in range(len(plan) - 1, -1, -1):
        place = place_in(*plan[level])
        members(groups[level], place, buffers[level])
        state, _ = pass_through(k, buffers[level], factors[level], place, state, backward, conj)
    return state


CHUNKS = 32
LEVELS = CHUNKS.bit_length() - 1


def partners(count):
    order = [(1 << b, 1 << b) for b in range(count.bit_length() - 1)]
    if len(order) > 2:
        order[1], order[2] = (2, 4), (4, 2)
    return order


def with_partner(value, bits):
    even, odd = bits
    count = lax.axis_size("tm")
    return lax.ppermute(value, "tm", [(i, i ^ (odd if i & 1 else even)) for i in range(count)])


def own_chunk(count, other_core=False):
    here = lax.axis_index("tm")
    if other_core:
        here = jnp.bitwise_xor(here, 1)
    own = 0
    for even, odd in partners(count)[:LEVELS]:
        taken = jnp.where(jnp.bitwise_and(here, 1) == 1, here & odd, here & even)
        own = own * 2 + jnp.where(taken != 0, 1, 0)
    return own


def slots(level):
    return (CHUNKS >> (level + 1), CHUNKS >> level) if level < LEVELS else (0, 1)


def outer_body(count, pairs, n_left, n_right, *refs):
    lefts, rights = refs[:n_left], refs[n_left : n_left + n_right]
    outs, products = refs[n_left + n_right : -len(pairs)], refs[-len(pairs) :]
    owns = own_chunk(count), own_chunk(count, True)
    half = CHUNKS // 2
    for q, (left, row, right, column) in enumerate(pairs):
        product = products[q]
        span = rights[right].shape[0]
        wide_left = lefts[left].shape[1]
        part = wide_left // CHUNKS
        width = product.shape[1]
        product[...] = dot_tn(
            lefts[left][row : row + span, :], rights[right][:, column : column + width]
        )
        for level in range(LEVELS + 1):
            low, high = slots(level)
            for slot in range(low, high):
                chunk = jnp.bitwise_xor(owns[slot // half], slot % half)
                chunk = pl.multiple_of(chunk * part, part)
                place = ((slot - low) * len(pairs) + q) * part
                outs[level][place : place + part, :] = product[pl.ds(chunk, part), :]


def add_body(low, *refs):
    out = refs[-1]
    total = refs[0][...]
    for ref in refs[1:-1]:
        total += ref[low : low + out.shape[0], :]
    out[...] = total


def join_body(first, second, out):
    out[: first.shape[0], :] = first[...]
    out[first.shape[0] :, :] = second[...]


class Bulk:
    def __init__(self, count, lefts, rights, pairs, after=()):
        self.bits = partners(count)
        width = 512
        part = lefts[0].shape[1] // CHUNKS
        self.rows = part * len(pairs)
        outs = [((self.rows * (hi - lo), width), F32) for lo, hi in map(slots, range(LEVELS + 1))]
        self.parts = run(
            functools.partial(outer_body, count, pairs, len(lefts), len(rights)),
            outs,
            list(lefts) + list(rights),
            after,
            [pltpu.VMEM((lefts[pair[0]].shape[1], width), F32) for pair in pairs],
            limit=16,
            macs=len(pairs) * rights[0].shape[0] * lefts[0].shape[1] * width,
        )
        self.received = []
        self.value = None

    def reduced(self, level, after=()):
        low, high = slots(level)
        if not self.received:
            return self.parts[level]
        (total,) = run(
            functools.partial(add_body, low * self.rows),
            [((self.rows * (high - low), self.parts[level].shape[1]), F32)],
            [self.parts[level]] + self.received,
            after,
            limit=8,
        )
        return total

    def send(self, after=()):
        level = len(self.received)
        total = self.reduced(level, after)
        self.received.append(with_partner(total, self.bits[level]))
        return total

    def settle(self, after=()):
        value = self.reduced(LEVELS, after)
        for even, odd in self.bits[LEVELS:]:
            other = with_partner(value, (even, odd))
            (value,) = run(
                functools.partial(add_body, 0), [(value.shape, F32)], [value, other], limit=4
            )
        self.value, self.level = value, LEVELS - 1
        return value

    def fetch(self, after=()):
        if self.level < LEVELS - 1:
            (self.value,) = run(
                join_body,
                [((2 * self.value.shape[0], self.value.shape[1]), F32)],
                [self.value, self.other],
                after,
                limit=8,
            )
        self.other = with_partner(self.value, self.bits[self.level])
        self.level -= 1
        return self.value


def unpack_body(count, width, layout, *refs):
    n_in = 2 * len(layout)
    outs, sem = refs[n_in:-1], refs[-1]
    owns = own_chunk(count), own_chunk(count, True)
    copies = []
    for piece, places in enumerate(layout):
        near, far = refs[2 * piece], refs[2 * piece + 1]
        for source, own in zip((near, far), owns):
            for j in range(CHUNKS // 2):
                chunk = jnp.bitwise_xor(own, j)
                part = source.shape[0] // (CHUNKS // 2) // len(places)
                for q, (out, k, column) in enumerate(places):
                    place = (j * len(places) + q) * part
                    rows = pl.ds(pl.multiple_of(chunk * part, part), part)
                    copies.append(
                        pltpu.make_async_copy(
                            source.at[pl.ds(place, part), :],
                            outs[out].at[k, rows, pl.ds(column, width)],
                            sem,
                        )
                    )
    for copy in copies:
        copy.start()
    for copy in copies:
        copy.wait()


def unpack(count, bulks, layout, shapes):
    operands = [value for bulk in bulks for value in (bulk.value, bulk.other)]
    anywhere = pl.BlockSpec(memory_space=pl.ANY)
    return pl.pallas_call(
        functools.partial(unpack_body, count, operands[0].shape[1], layout),
        out_shape=[jax.ShapeDtypeStruct(shape, F32) for shape in shapes],
        in_specs=[anywhere] * len(operands),
        out_specs=[anywhere] * len(shapes),
        scratch_shapes=[pltpu.SemaphoreType.DMA],
        compiler_params=pltpu.CompilerParams(vmem_limit_bytes=4 * MIB),
    )(*operands)


def steps(span, backward, body, start, unroll=8):
    def one(k, carry):
        return body(span - 1 - k if backward else k, carry)

    return lax.fori_loop(0, span, one, start, unroll=unroll)


def at(t, seqs):
    return pl.ds(pl.multiple_of(t * seqs, seqs), seqs)


def state_scan(v_ref, rel, lr, li, start, span, backward, keep=None):
    seqs, states = lr.shape

    def body(t, carry):
        re, im = carry
        vr, vi = v_ref[at(t, seqs), :states], v_ref[at(t, seqs), states:]
        next_re, next_im = mul(lr, li, re, im)
        live = rel > t
        re, im = jnp.where(live, next_re + vr, re), jnp.where(live, next_im + vi, im)
        if keep is not None:
            keep(t, re, im)
        return re, im

    return steps(span, backward, body, start)


def adjoint_scan(g_ref, rel, lr, li, start, span, backward, use=None, extra=()):
    seqs, states = lr.shape

    def body(t, carry):
        (re, im), kept = carry
        ar, ai = g_ref[at(t, seqs), :states] + re, g_ref[at(t, seqs), states:] + im
        live = rel > t
        if use is not None:
            kept = use(t, ar, ai, live, kept)
        next_re, next_im = mul(lr, -li, ar, ai)
        return (jnp.where(live, next_re, ar), jnp.where(live, next_im, ai)), kept

    return steps(span, backward, body, (start, extra))


def wide(ref, row, shape):
    return jnp.broadcast_to(ref[row : row + 1, :], shape)


def to_time_major(piece):
    seqs, span, width = piece.shape
    return jnp.swapaxes(piece, 0, 1).reshape(span * seqs, width)


def from_time_major(rows, seqs):
    return jnp.swapaxes(rows.reshape(-1, seqs, rows.shape[-1]), 0, 1)


def lane_tiled(column, width):
    return jnp.concatenate([column] * (width // LANES), axis=1)


def gelu_parts(y):
    cdf = 0.5 * (1.0 + lax.erf(y * inverse_root_two))
    pdf = jnp.exp(-0.5 * y * y) * density_scale
    return y * cdf, cdf + y * pdf


def sigmoid(x):
    return 1.0 / (1.0 + jnp.exp(-x))


CHUNK = 16


def prepare_body(plan, span, lens_ref, x_ref, nu_ref, phase_ref, gamma_ref, *outs):
    sums_ref, tm_ref, mask_ref, decay_ref = outs[:4]
    factor_refs = outs[4:]
    seqs, _, width = x_ref.shape
    states = nu_ref.shape[-1]
    here = lax.axis_index("tm")
    rel = jnp.broadcast_to(lens_ref[...] - here * span, (seqs, LANES))
    first = jnp.zeros((seqs, width), F32)
    second = jnp.zeros((seqs, width), F32)
    for t0 in range(0, span, 8):
        piece = jnp.swapaxes(x_ref[:, t0 : t0 + 8, :], 0, 1)
        for j in range(8):
            rows = piece[j]
            mask = jnp.where(rel > t0 + j, 1.0, 0.0)
            place = slice((t0 + j) * seqs, (t0 + j + 1) * seqs)
            mask_ref[place, :] = mask
            tm_ref[place, :] = rows
            live = rows * lane_tiled(mask, width)
            first += live
            second += live * rows
    spread(sums_ref, jnp.sum(first, 0, keepdims=True), jnp.sum(second, 0, keepdims=True))
    rate = jnp.exp(nu_ref[...])
    radius = jnp.exp(-rate)
    angle = phase_ref[...]
    cosine, sine = jnp.cos(angle), jnp.sin(angle)
    gamma = gamma_ref[...]
    for row, value in enumerate((radius * cosine, radius * sine, gamma, rate, radius, cosine, sine)):
        for k in range(2):
            decay_ref[k, row : row + 1, :] = value[k : k + 1, :]
    for k in range(2):
        for level, (radix, stride) in enumerate(plan):
            base = lax.div(here, radix * stride) * (radix * stride)
            for member in range(radix):
                start = (base + member * stride) * span
                count = jnp.clip(lens_ref[...] - start, 0, stride * span)
                count = jnp.broadcast_to(count, (seqs, states))
                power = (decay_ref[k, 0:1, :], decay_ref[k, 1:2, :])
                re, im = jnp.ones((seqs, states), F32), jnp.zeros((seqs, states), F32)
                for bit in range((span * stride).bit_length()):
                    taken = jnp.bitwise_and(count, 1 << bit) != 0
                    next_re, next_im = mul(re, im, *power)
                    re, im = jnp.where(taken, next_re, re), jnp.where(taken, next_im, im)
                    power = mul(*power, *power)
                factor_refs[level][k, member, :, :states] = re
                factor_refs[level][k, member, :, states:] = im


def relative(lens_ref, span, states):
    return jnp.broadcast_to(
        lens_ref[...] - lax.axis_index("tm") * span, (lens_ref.shape[0], states)
    )


def token_scale(lens_ref):
    return 1.0 / jnp.sum(lens_ref[...].astype(F32), axis=0, keepdims=True)


def project_body(
    k, span, backward, lens_ref, sums_ref, x_ref, gain_ref, bias_ref, w_ref, decay_ref,
    u_ref, v_ref, stats_ref, summary_ref,
):
    seqs = lens_ref.shape[0]
    states = decay_ref.shape[-1]
    total, squares = gathered(sums_ref)
    scale = token_scale(lens_ref)
    mean = total * scale
    var = squares * scale - mean * mean
    rstd = lax.rsqrt(var + norm_epsilon)
    stats_ref[0:1, :] = mean
    stats_ref[1:2, :] = var
    stats_ref[2:3, :] = rstd
    stats_ref[3:4, :] = rstd * gain_ref[k : k + 1, :]
    slope = rstd * gain_ref[k : k + 1, :]
    bias = bias_ref[k : k + 1, :]
    step = CHUNK * seqs
    for r in range(0, span * seqs, step):
        u = ((x_ref[r : r + step, :] - mean) * slope + bias).astype(BF16)
        u_ref[r : r + step, :] = u
        v_ref[r : r + step, :] = dot(u, w_ref[k])
    shape = (seqs, states)
    rel = relative(lens_ref, span, states)
    lr, li = wide(decay_ref.at[k], 0, shape), wide(decay_ref.at[k], 1, shape)
    zero = jnp.zeros(shape, F32)
    re, im = state_scan(v_ref, rel, lr, li, (zero, zero), span, backward)
    summary_ref[:, :states] = re
    summary_ref[:, states:] = im


def rebuild_states(k, plan, span, backward, refs, buffers, rel, v_ref, decay_ref, h_ref):
    seqs, states = rel.shape
    lr, li, gamma = (wide(decay_ref.at[k], row, rel.shape) for row in range(3))
    start = entering_state(k, plan, refs, buffers, backward, False)

    lead = 0 if backward else 1

    def keep(t, re, im):
        h_ref[at(t + lead, seqs), :states] = (re * gamma).astype(BF16)
        h_ref[at(t + lead, seqs), states:] = (im * gamma).astype(BF16)

    keep(span if backward else -1, *start)
    state_scan(v_ref, rel, lr, li, start, span, backward, keep)


def forward_body(
    k, plan, span, exch, lens_ref, v_ref, x_ref, mask_ref, stats_ref, bias_ref,
    decay_ref, w_out_ref, skip_ref, w_glu_ref,
    out_ref, h_ref, act_ref, slope_ref, gate_ref, value_ref, sums_ref, buffers,
):
    seqs = lens_ref.shape[0]
    width = x_ref.shape[1]
    states = decay_ref.shape[-1]
    rel = relative(lens_ref, span, states)
    rebuild_states(k, plan, span, False, exch, buffers, rel, v_ref, decay_ref, h_ref)
    mean, scale = stats_ref[0:1, :], stats_ref[3:4, :]
    bias, skip = bias_ref[k : k + 1, :], skip_ref[k : k + 1, :]
    step = CHUNK * seqs
    first = jnp.zeros((8, width), F32)
    second = jnp.zeros((8, width), F32)
    for r in range(0, span * seqs, step):
        x = x_ref[r : r + step, :]
        u = (x - mean) * scale + bias
        y = dot(h_ref[r + seqs : r + seqs + step, :], w_out_ref[k]) + skip * u
        act, slope = gelu_parts(y)
        act = act.astype(BF16)
        act_ref[r : r + step, :] = act
        slope_ref[r : r + step, :] = slope.astype(BF16)
        z = dot(act, w_glu_ref[k])
        value, gate = z[:, :width], sigmoid(z[:, width:])
        gated = value * gate
        out = x + gated
        out_ref[r : r + step, :] = out
        gate_ref[r : r + step, :] = gate.astype(BF16)
        value_ref[r : r + step, :] = (gated * (1.0 - gate)).astype(BF16)
        live = out * lane_tiled(mask_ref[r : r + step, :], width)
        first += jnp.sum(live.reshape(-1, 8, width), 0)
        second += jnp.sum((live * out).reshape(-1, 8, width), 0)
    spread(sums_ref, jnp.sum(first, 0, keepdims=True), jnp.sum(second, 0, keepdims=True))


def back_rows(k, r, step, dza, dzb, slope, width, w_glu_ref, w_out_ref, dz_ref, dy_ref, g_ref):
    dza, dzb = dza.astype(BF16), dzb.astype(BF16)
    dz_ref[r : r + step, :width] = dza
    dz_ref[r : r + step, width:] = dzb
    w = w_glu_ref[k]
    dact = dot_nt(dza, w[:, :width]) + dot_nt(dzb, w[:, width:])
    dy = (dact * slope).astype(BF16)
    dy_ref[r : r + step, :] = dy
    g_ref[r : r + step, :] = dot_nt(dy, w_out_ref[k])


def local_adjoint(k, span, backward, rel, g_ref, decay_ref, summary_ref):
    seqs, states = rel.shape
    lr, li = wide(decay_ref.at[k], 0, rel.shape), wide(decay_ref.at[k], 1, rel.shape)
    zero = jnp.zeros(rel.shape, F32)
    (re, im), _ = adjoint_scan(g_ref, rel, lr, li, (zero, zero), span, backward)
    summary_ref[:, :states] = re
    summary_ref[:, states:] = im


def turn_body(
    k, plan, span, exch, lens_ref, v_ref, x_ref, cot_ref, stats_ref, bias_ref,
    decay_ref, w_out_ref, skip_ref, w_glu_ref,
    out_ref, h_ref, act_ref, dz_ref, dy_ref, g_ref, summary_ref, buffers,
):
    seqs = lens_ref.shape[0]
    width = x_ref.shape[1]
    states = decay_ref.shape[-1]
    rel = relative(lens_ref, span, states)
    rebuild_states(k, plan, span, True, exch, buffers, rel, v_ref, decay_ref, h_ref)
    mean, scale = stats_ref[0:1, :], stats_ref[3:4, :]
    bias, skip = bias_ref[k : k + 1, :], skip_ref[k : k + 1, :]
    step = CHUNK * seqs
    for r in range(0, span * seqs, step):
        t0 = r // seqs
        x = x_ref[r : r + step, :]
        u = (x - mean) * scale + bias
        y = dot(h_ref[r : r + step, :], w_out_ref[k]) + skip * u
        act, slope = gelu_parts(y)
        act = act.astype(BF16)
        act_ref[r : r + step, :] = act
        z = dot(act, w_glu_ref[k])
        value, gate = z[:, :width], sigmoid(z[:, width:])
        gated = value * gate
        out_ref[:, t0 : t0 + CHUNK, :] = from_time_major(x + gated, seqs)
        d = to_time_major(cot_ref[:, t0 : t0 + CHUNK, :])
        back_rows(
            k, r, step, d * gate, d * (gated * (1.0 - gate)), slope, width,
            w_glu_ref, w_out_ref, dz_ref, dy_ref, g_ref,
        )
    local_adjoint(k, span, False, rel, g_ref, decay_ref, summary_ref)


def back_body(
    k, span, backward, lens_ref, sums_ref, part_ref, x_ref, mask_ref, stats_ref, slope_ref,
    gate_ref, value_ref, gain_ref, decay_ref, w_out_ref, w_glu_ref,
    d_ref, dz_ref, dy_ref, g_ref, grads_ref, summary_ref,
):
    seqs = lens_ref.shape[0]
    width = x_ref.shape[1]
    states = decay_ref.shape[-1]
    rel = relative(lens_ref, span, states)
    shift, tilt = input_terms(k + 1, token_scale(lens_ref), sums_ref, stats_ref, gain_ref, grads_ref)
    mean = stats_ref[0:1, :]
    step = CHUNK * seqs
    for r in range(0, span * seqs, step):
        live = lane_tiled(mask_ref[r : r + step, :], width)
        d = part_ref[r : r + step, :] + live * (shift + tilt * (x_ref[r : r + step, :] - mean))
        d_ref[r : r + step, :] = d
        back_rows(
            k, r, step, d * gate_ref[r : r + step, :].astype(F32),
            d * value_ref[r : r + step, :].astype(F32), slope_ref[r : r + step, :].astype(F32), width,
            w_glu_ref, w_out_ref, dz_ref, dy_ref, g_ref,
        )
    local_adjoint(k, span, backward, rel, g_ref, decay_ref, summary_ref)


def input_terms(k, scale, sums_ref, stats_ref, gain_ref, grads_ref):
    bias_grad, gain_grad = gathered(sums_ref)
    grads_ref[0:1, :] = gain_grad
    grads_ref[1:2, :] = bias_grad
    rstd = stats_ref[2:3, :]
    gain = gain_ref[k : k + 1, :]
    return -rstd * gain * bias_grad * scale, -rstd * rstd * gain * gain_grad * scale


def adjoint_body(
    k, plan, span, backward, exch, lens_ref, g_ref, h_ref, v_ref, decay_ref, dv_ref, small_ref, buffers
):
    seqs = lens_ref.shape[0]
    states = decay_ref.shape[-1]
    rel = relative(lens_ref, span, states)
    lr, li, gamma = (wide(decay_ref.at[k], row, rel.shape) for row in range(3))
    start = entering_state(k, plan, exch, buffers, backward, True)
    before = 0 if backward else 1

    def use(t, ar, ai, live, kept):
        ar, ai = jnp.where(live, ar, 0.0), jnp.where(live, ai, 0.0)
        dv_ref[at(t, seqs), :states] = (ar * gamma).astype(BF16)
        dv_ref[at(t, seqs), states:] = (ai * gamma).astype(BF16)
        pr = h_ref[at(t + before, seqs), :states].astype(F32)
        pi = h_ref[at(t + before, seqs), states:].astype(F32)
        vr, vi = v_ref[at(t, seqs), :states], v_ref[at(t, seqs), states:]
        return (
            kept[0] + (ar * pr + ai * pi),
            kept[1] + (ai * pr - ar * pi),
            kept[2] + (ar * vr + ai * vi),
        )

    zero = jnp.zeros(rel.shape, F32)
    _, kept = adjoint_scan(g_ref, rel, lr, li, start, span, backward, use, (zero, zero, zero))
    small_ref[...] = jnp.zeros_like(small_ref)
    for j in range(2):
        small_ref[0:1, j * states : (j + 1) * states] = jnp.sum(kept[j], 0, keepdims=True)
    small_ref[1:2, :states] = jnp.sum(kept[2], 0, keepdims=True)


def input_body(
    k, seq_major, dv_ref, dy_ref, x_ref, d_ref, stats_ref, gain_ref, bias_ref, w_in_ref, skip_ref,
    part_ref, skip_grad_ref, sums_ref,
):
    width = x_ref.shape[1]
    seqs = CHUNK
    mean, scale, rstd = stats_ref[0:1, :], stats_ref[3:4, :], stats_ref[2:3, :]
    gain, bias, skip = (ref[k : k + 1, :] for ref in (gain_ref, bias_ref, skip_ref))
    if seq_major:
        seqs = d_ref.shape[0]
    step = CHUNK * seqs
    first = jnp.zeros((8, width), F32)
    second = jnp.zeros((8, width), F32)
    third = jnp.zeros((8, width), F32)
    for r in range(0, x_ref.shape[0], step):
        xhat = (x_ref[r : r + step, :] - mean) * rstd
        dy = dy_ref[r : r + step, :].astype(F32)
        du = dot_nt(dv_ref[r : r + step, :], w_in_ref[k]) + dy * skip
        first += jnp.sum(du.reshape(-1, 8, width), 0)
        second += jnp.sum((du * xhat).reshape(-1, 8, width), 0)
        third += jnp.sum((dy * (xhat * gain + bias)).reshape(-1, 8, width), 0)
        if seq_major:
            d = to_time_major(d_ref[:, r // seqs : r // seqs + CHUNK, :])
        else:
            d = d_ref[r : r + step, :]
        part_ref[r : r + step, :] = d + du * scale
    spread(sums_ref, jnp.sum(first, 0, keepdims=True), jnp.sum(second, 0, keepdims=True))
    skip_grad_ref[...] = third


def finish_body(
    k, span, lens_ref, sums_ref, part_ref, x_ref, mask_ref, stats_ref, gain_ref, out_ref, grads_ref
):
    seqs = out_ref.shape[0]
    width = x_ref.shape[1]
    scale = token_scale(lens_ref)
    shift, tilt = input_terms(k, scale, sums_ref, stats_ref, gain_ref, grads_ref)
    mean = stats_ref[0:1, :]
    step = CHUNK * seqs
    for r in range(0, span * seqs, step):
        live = lane_tiled(mask_ref[r : r + step, :], width)
        d = part_ref[r : r + step, :] + live * (shift + tilt * (x_ref[r : r + step, :] - mean))
        out_ref[:, r // seqs : r // seqs + CHUNK, :] = from_time_major(d, seqs)


def small_body(refs_per_block, *refs):
    out = refs[-1]
    out[...] = jnp.zeros_like(out)
    for k in range(2):
        small, skip_grad = refs[2 * k], refs[2 * k + 1]
        out[8 * k : 8 * k + 2, :] = small[0:2, :]
        out[8 * k + 2 : 8 * k + 3, :] = jnp.sum(skip_grad[...], 0, keepdims=True)


def sum_body(*refs):
    total = refs[0][...]
    for ref in refs[1:-1]:
        total += ref[...]
    refs[-1][...] = total


def results_body(n_parts, *refs):
    parts, rest = refs[:n_parts], refs[n_parts:]
    lens_ref, decay_ref, running_ref = rest[:3]
    stats_refs, grads_refs = rest[3:5], rest[5:7]
    gain_ref, bias_ref, nu_ref, phase_ref, skip_ref, run_ref = rest[7:]
    small = parts[0][...]
    for ref in parts[1:]:
        small += ref[...]
    states = decay_ref.shape[-1]
    count = jnp.sum(lens_ref[...].astype(F32), axis=0, keepdims=True)
    for k in range(2):
        _, _, gamma, rate, radius, cosine, sine = (decay_ref[k, j : j + 1, :] for j in range(7))
        sum_re, sum_im = small[8 * k : 8 * k + 1, :states], small[8 * k : 8 * k + 1, states:]
        g_gamma = small[8 * k + 1 : 8 * k + 2, :states]
        nu_ref[k : k + 1, :] = (sum_re * cosine + sum_im * sine) * (
            -radius * rate
        ) + g_gamma * rate * radius * radius / gamma
        phase_ref[k : k + 1, :] = radius * (sum_im * cosine - sum_re * sine)
        skip_ref[k : k + 1, :] = small[8 * k + 2 : 8 * k + 3, :]
        gain_ref[k : k + 1, :] = grads_refs[k][0:1, :]
        bias_ref[k : k + 1, :] = grads_refs[k][1:2, :]
        mean, var = stats_refs[k][0:1, :], stats_refs[k][1:2, :]
        run_ref[k, 0:1, :] = (1.0 - momentum) * running_ref[k, 0:1, :] + momentum * mean
        run_ref[k, 1:2, :] = (1.0 - momentum) * running_ref[k, 1:2, :] + momentum * var * (
            count / (count - 1.0)
        )


def with_entry(body, plan):
    def wrapped(*refs):
        n_exch = sum(radix for radix, _ in plan) + len(plan)
        body(refs[:n_exch], *refs[n_exch : -len(plan)], refs[-len(plan) :])

    return wrapped


def shards(
    inputs, lengths, cotangent, bn_gain, bn_bias, running, w_in, nu_log, phase, w_out, skip, w_glu
):
    seqs, span, width = inputs.shape
    states = nu_log.shape[1]
    count = lax.axis_size("tm")
    rows = span * seqs
    plan = stages(count)
    lens = lengths[:, None]

    tile = ((count, 2 * width // LANES, LANES), F32)
    whole, whole_low = ((rows, width), F32), ((rows, width), BF16)
    pair, pair_low = ((rows, 2 * states), F32), ((rows, 2 * states), BF16)
    double_low = ((rows, 2 * width), BF16)
    held_low = ((rows + seqs, 2 * states), BF16)
    summary = ((seqs, 2 * states), F32)
    eight = ((8, width), F32)
    seq_major = ((seqs, span, width), F32)
    buffers = entry_scratch(plan, summary[0])

    prepared = run(
        functools.partial(prepare_body, plan, span),
        [tile, whole, ((rows, LANES), F32), ((2, 8, states), F32)]
        + [((2, radix) + summary[0], F32) for radix, _ in plan],
        [lens, inputs, nu_log, phase, jnp.sqrt(-jnp.expm1(-2.0 * jnp.exp(nu_log)))],
    )
    sums, x0, mask, decay = prepared[:4]
    factors = prepared[4:]

    def project(k, sums, x):
        return run(
            functools.partial(project_body, k, span, k == 1),
            [whole_low, pair, eight, summary],
            [lens, everywhere(sums), x, bn_gain, bn_bias, w_in, decay],
        )

    def entered(body, outs, held, operands, after=(), limit=12):
        operands = entry_operands(held, factors) + operands
        return run(with_entry(body, plan), outs, operands, after, buffers, limit)

    u0, v0, stats0, part = project(0, sums, x0)
    held = exchange(0, part, plan, factors, False, False)
    x1, h0, act0, slope0, gate0, value0, sums = entered(
        functools.partial(forward_body, 0, plan, span),
        [whole, held_low, whole_low, whole_low, whole_low, whole_low, tile],
        held,
        [lens, v0, x0, mask, stats0, bn_bias, decay, w_out, skip, w_glu],
    )
    u1, v1, stats1, part = project(1, sums, x1)
    held = exchange(1, part, plan, factors, True, False)
    output, h1, act1, dz1, dy1, g1, part = entered(
        functools.partial(turn_body, 1, plan, span),
        [seq_major, held_low, whole_low, double_low, whole_low, pair, summary],
        held,
        [lens, v1, x1, cotangent, stats1, bn_bias, decay, w_out, skip, w_glu],
    )

    flows = {}

    def beside_top(level, value):
        if level == 1:
            flows["top"] = Bulk(
                count, [act1, h1], [dz1, dy1], [(0, 0, 0, 0), (0, 0, 0, width), (1, 0, 1, 0)], [value]
            )
            flows["top"].send()
            return flows["top"].parts[-1:]
        if level == len(plan) - 1:
            flows["step"] = flows["top"].send([value])
        return ()

    held = exchange(1, part, plan, factors, False, True, beside_top)
    top = flows["top"]
    dv1, small1 = entered(
        functools.partial(adjoint_body, 1, plan, span, False),
        [pair_low, eight],
        held,
        [lens, g1, h1, v1, decay],
        [flows["step"]],
    )
    step = top.send([dv1])
    part1, skip1, sums = run(
        functools.partial(input_body, 1, True),
        [whole, eight, tile],
        [dv1, dy1, x1, cotangent, stats1, bn_gain, bn_bias, w_in, skip],
        [step],
        macs=rows * width * 2 * states,
    )
    sums = everywhere(sums)
    step = top.send([sums])
    d0, dz0, dy0, g0, grads1, part = run(
        functools.partial(back_body, 0, span, True),
        [whole, double_low, whole_low, pair, eight, summary],
        [lens, sums, part1, x1, mask, stats1, slope0, gate0, value0, bn_gain, decay, w_out, w_glu],
        [step],
        macs=rows * width * (2 * width + 2 * states),
    )

    def beside_middle(level, value):
        if level == 1:
            step = top.send([value])
            flows["middle"] = Bulk(
                count,
                [u1, act0, h0],
                [dv1, dz0, dy0],
                [(0, 0, 0, 0), (1, 0, 1, 0), (1, 0, 1, width), (2, seqs, 2, 0)],
                [step],
            )
            flows["middle"].send()
            return flows["middle"].parts[-1:]
        if level == len(plan) - 1:
            flows["step"] = flows["middle"].send([value])
        return ()

    held = exchange(0, part, plan, factors, True, True, beside_middle)
    middle = flows["middle"]
    dv0, small0 = entered(
        functools.partial(adjoint_body, 0, plan, span, True),
        [pair_low, eight],
        held,
        [lens, g0, h0, v0, decay],
        [flows["step"]],
    )
    own = top.settle([dv0])
    top.fetch()
    part0, skip0, sums = run(
        functools.partial(input_body, 0, False),
        [whole, eight, tile],
        [dv0, dy0, x0, d0, stats0, bn_gain, bn_bias, w_in, skip],
        [own],
        macs=rows * width * 2 * states,
    )
    step = middle.send([sums])
    sums = everywhere(sums)
    grad_x, grads0 = run(
        functools.partial(finish_body, 0, span),
        [seq_major, eight],
        [lens, sums, part0, x0, mask, stats0, bn_gain],
    )

    last = Bulk(count, [u0], [dv0], [(0, 0, 0, 0)], [sums])
    last.send()
    step = middle.send([last.parts[-1]])
    step = top.fetch([step])
    (small,) = run(
        functools.partial(small_body, 2), [((16, width), F32)], [small0, skip0, small1, skip1], [step]
    )
    step = last.send([small])
    step = top.fetch([step])
    step = middle.send([step])
    group = group_of(small, *plan[0])
    (small,) = run(sum_body, [((16, width), F32)], group, [step], limit=4)
    step = last.send([small])
    step = top.fetch([step])
    step = middle.settle([step])
    middle.fetch()
    step = last.send([step])
    group = group_of(small, *plan[1])
    (small,) = run(sum_body, [((16, width), F32)], group, [step], limit=4)
    step = middle.fetch([small])
    step = last.send([step])
    for stage in plan[2:]:
        group = group_of(small, *stage)
        if stage != plan[-1]:
            (small,) = run(sum_body, [((16, width), F32)], group, [step], limit=4)
    step = middle.fetch([step])
    step = top.fetch([step])
    step = last.settle([step])
    last.fetch()
    step = last.fetch([step])
    g_gain, g_bias, g_nu, g_phase, g_skip, running_out = run(
        functools.partial(results_body, len(group)),
        [((2, width), F32)] * 2 + [((2, states), F32)] * 2 + [((2, width), F32), ((2, 2, width), F32)],
        list(group) + [lens, decay, running, stats0, stats1, grads0, grads1],
        [step],
    )
    step = middle.fetch([step])
    step = last.fetch([step])
    step = last.fetch([step])
    step = middle.fetch([step])
    step = last.fetch([step])
    g_glu, g_out, g_in = unpack(
        count,
        [top, middle, last],
        [
            [(0, 1, 0), (0, 1, width), (1, 1, 0)],
            [(2, 1, 0), (0, 0, 0), (0, 0, width), (1, 0, 0)],
            [(2, 0, 0)],
        ],
        [(2, width, 2 * width), (2, 2 * states, width), (2, width, 2 * states)],
    )
    return (output, grad_x, g_gain, g_bias, g_in, g_nu, g_phase, g_out, g_skip, g_glu, running_out)


def solution(mesh):
    placed = (P(None, "tm", None), P(), P(None, "tm", None)) + (P(),) * 9
    return jax.shard_map(
        shards,
        mesh=mesh,
        in_specs=placed,
        out_specs=(P(None, "tm", None),) * 2 + (P(),) * 9,
        check_vma=False,
    )
```

```python
import functools
import math

import jax
import jax.numpy as jnp
from jax import lax
from jax.experimental import pallas as pl
from jax.experimental.pallas import tpu as pltpu
from jax.sharding import PartitionSpec as P

norm_epsilon = 1e-05
momentum = 0.1
inverse_root_two = 0.7071067811865476
density_scale = 0.3989422804014327
F32, BF16 = jnp.float32, jnp.bfloat16
LANES = 128
MIB = 1 << 20


def dot(left, right):
    return jnp.dot(left, right, preferred_element_type=F32)


def dot_tn(left, right):
    return lax.dot_general(left, right, (((0,), (0,)), ((), ())), preferred_element_type=F32)


def dot_nt(left, right):
    return lax.dot_general(left, right, (((1,), (1,)), ((), ())), preferred_element_type=F32)


def run(body, outs, operands, after=(), scratch=(), limit=12, weight=1 << 33):
    vmem = pl.BlockSpec(memory_space=pltpu.VMEM)
    anywhere = pl.BlockSpec(memory_space=pl.ANY)
    first, second = len(operands), len(operands) + len(after)

    def kernel(*refs):
        body(*refs[:first], *refs[second:])

    return pl.pallas_call(
        kernel,
        out_shape=[jax.ShapeDtypeStruct(shape, dtype) for shape, dtype in outs],
        in_specs=[vmem] * len(operands) + [anywhere] * len(after),
        out_specs=[vmem] * len(outs),
        scratch_shapes=list(scratch),
        compiler_params=pltpu.CompilerParams(vmem_limit_bytes=limit * MIB),
        cost_estimate=pl.CostEstimate(flops=weight, bytes_accessed=0, transcendentals=0),
    )(*operands, *after)


def radices(count):
    out = []
    while count > 1:
        radix = 2 if not out or count % 4 else 4
        out.append(radix)
        count //= radix
    return out


def stages(count):
    stride, out = 1, []
    for radix in radices(count):
        out.append((radix, stride))
        stride *= radix
    return out


def swap(value, stride, mask):
    count = lax.axis_size("tm")
    return lax.ppermute(value, "tm", [(i, i ^ (stride * mask)) for i in range(count)])


def group_of(value, radix, stride):
    return [value] + [swap(value, stride, mask) for mask in range(1, radix)]


def place_in(radix, stride):
    return lax.rem(lax.div(lax.axis_index("tm"), stride), radix)


def rows_to_tile(first, second):
    pieces = [
        row[:, j : j + LANES] for row in (first, second) for j in range(0, row.shape[1], LANES)
    ]
    return jnp.concatenate(pieces, axis=0)


def tile_to_rows(tile):
    half = tile.shape[0] // 2
    return [
        jnp.concatenate([tile[base + j : base + j + 1, :] for j in range(half)], axis=1)
        for base in (0, half)
    ]


def spread(ref, first, second):
    ref[...] = jnp.broadcast_to(rows_to_tile(first, second)[None], ref.shape)


def gathered(ref):
    return tile_to_rows(jnp.sum(ref[...], axis=0))


def everywhere(tiles):
    return lax.all_to_all(tiles, "tm", 0, 0)


def mul(ar, ai, br, bi):
    return ar * br - ai * bi, ar * bi + ai * br


def members(refs, place, buffer):
    for offset, ref in enumerate(refs):
        buffer[jnp.bitwise_xor(place, offset)] = ref[...]


def pass_through(k, buffer, factor, place, state, backward, conj):
    radix, _, width = buffer.shape
    states = width // 2
    if state is None:
        zero = jnp.zeros(buffer.shape[1:-1] + (states,), F32)
        state = (zero, zero)
    entering = state
    for member in range(radix - 1, -1, -1) if backward else range(radix):
        entering = tuple(jnp.where(place == member, s, e) for s, e in zip(state, entering))
        fr, fi = factor[k, member, :, :states], factor[k, member, :, states:]
        moved = mul(fr, -fi if conj else fi, *state)
        state = (moved[0] + buffer[member, :, :states], moved[1] + buffer[member, :, states:])
    return entering, state


def total_body(k, radix, stride, backward, conj, *refs):
    factor, out, buffer = refs[radix:]
    place = place_in(radix, stride)
    members(refs[:radix], place, buffer)
    _, (re, im) = pass_through(k, buffer, factor, place, None, backward, conj)
    states = re.shape[1]
    out[:, :states] = re
    out[:, states:] = im


def group_total(k, group, level, plan, factors, backward, conj, after=()):
    radix, stride = plan[level]
    shape = group[0].shape
    (total,) = run(
        functools.partial(total_body, k, radix, stride, backward, conj),
        [(shape, F32)],
        list(group) + [factors[level]],
        after,
        [pltpu.VMEM((radix,) + shape, F32)],
        limit=4,
    )
    return total


def exchange(k, summary, plan, factors, backward, conj, between=None):
    held = []
    value = summary
    for level, (radix, stride) in enumerate(plan):
        group = group_of(value, radix, stride)
        held.append(group)
        if level + 1 < len(plan):
            after = between(level, group) if between else ()
            value = group_total(k, group, level, plan, factors, backward, conj, after)
            if between and level + 2 == len(plan):
                between(level + 1, [value])
    return held


def entry_operands(held, factors):
    return [value for group in held for value in group] + list(factors)


def entry_scratch(plan, shape):
    return [pltpu.VMEM((radix,) + shape, F32) for radix, _ in plan]


def entering_state(k, plan, refs, buffers, backward, conj):
    total = sum(radix for radix, _ in plan)
    values, factors = refs[:total], refs[total:]
    start, groups = 0, []
    for radix, _ in plan:
        groups.append(values[start : start + radix])
        start += radix
    state = None
    for level in range(len(plan) - 1, -1, -1):
        place = place_in(*plan[level])
        members(groups[level], place, buffers[level])
        state, _ = pass_through(k, buffers[level], factors[level], place, state, backward, conj)
    return state


CHUNKS = 32
LEVELS = CHUNKS.bit_length() - 1


def partners(count):
    order = [(1 << b, 1 << b) for b in range(count.bit_length() - 1)]
    if len(order) > 2:
        order[1], order[2] = (2, 4), (4, 2)
    return order


def with_partner(value, bits):
    even, odd = bits
    count = lax.axis_size("tm")
    return lax.ppermute(value, "tm", [(i, i ^ (odd if i & 1 else even)) for i in range(count)])


def own_chunk(count, other_core=False):
    here = lax.axis_index("tm")
    if other_core:
        here = jnp.bitwise_xor(here, 1)
    own = 0
    for even, odd in partners(count)[:LEVELS]:
        taken = jnp.where(jnp.bitwise_and(here, 1) == 1, here & odd, here & even)
        own = own * 2 + jnp.where(taken != 0, 1, 0)
    return own


def slots(level):
    return (CHUNKS >> (level + 1), CHUNKS >> level) if level < LEVELS else (0, 1)


def outer_body(count, pairs, n_left, n_right, n_extra, *refs):
    lefts, rights = refs[:n_left], refs[n_left : n_left + n_right]
    extra, outs = refs[n_left + n_right :][:n_extra], refs[n_left + n_right + n_extra : -len(pairs)]
    products = refs[-len(pairs) :]
    if extra:
        outs[0][-extra[0].shape[0] :, :] = extra[0][...]
    owns = own_chunk(count), own_chunk(count, True)
    half = CHUNKS // 2
    for q, (left, row, right, column) in enumerate(pairs):
        product = products[q]
        span = rights[right].shape[0]
        wide_left = lefts[left].shape[1]
        part = wide_left // CHUNKS
        width = product.shape[1]
        product[...] = dot_tn(
            lefts[left][row : row + span, :], rights[right][:, column : column + width]
        )
        for level in range(LEVELS + 1):
            low, high = slots(level)
            for slot in range(low, high):
                chunk = jnp.bitwise_xor(owns[slot // half], slot % half)
                chunk = pl.multiple_of(chunk * part, part)
                place = ((slot - low) * len(pairs) + q) * part
                outs[level][place : place + part, :] = product[pl.ds(chunk, part), :]


def add_body(low, extra, *refs):
    out = refs[-1]
    rows = out.shape[0] - extra
    total = refs[0][:rows, :]
    for ref in refs[1 : -2 if extra else -1]:
        total += ref[low : low + rows, :]
    out[:rows, :] = total
    if extra:
        mine, other = refs[-2], refs[-3]
        out[rows:, :] = mine[-extra:, :] + other[-extra:, :]


def join_body(first, second, out):
    out[: first.shape[0], :] = first[...]
    out[first.shape[0] :, :] = second[...]


class Bulk:
    def __init__(self, count, lefts, rights, pairs, after=(), extra=()):
        self.bits = partners(count)
        self.extra = extra[0].shape[0] if extra else 0
        width = 512
        part = lefts[0].shape[1] // CHUNKS
        self.rows = part * len(pairs)
        outs = [((self.rows * (hi - lo), width), F32) for lo, hi in map(slots, range(LEVELS + 1))]
        outs[0] = ((outs[0][0][0] + self.extra, width), F32)
        self.parts = run(
            functools.partial(outer_body, count, pairs, len(lefts), len(rights), len(extra)),
            outs,
            list(lefts) + list(rights) + list(extra),
            after,
            [pltpu.VMEM((lefts[pair[0]].shape[1], width), F32) for pair in pairs],
            limit=16,
        )
        self.received = []
        self.sent = None

    def reduced(self, level, after=()):
        low, high = slots(level)
        if not self.received:
            return self.parts[level]
        (total,) = run(
            functools.partial(add_body, low * self.rows, self.extra),
            [((self.rows * (high - low) + self.extra, self.parts[level].shape[1]), F32)],
            [self.parts[level]] + self.received + ([self.sent] if self.extra else []),
            after,
            limit=8,
        )
        return total

    def send(self, after=()):
        level = len(self.received)
        self.sent = self.reduced(level, after)
        self.received.append(with_partner(self.sent, self.bits[level]))
        return self.sent

    def settle(self, after=()):
        value = self.reduced(LEVELS, after)
        for even, odd in self.bits[LEVELS:]:
            other = with_partner(value, (even, odd))
            (value,) = run(
                functools.partial(add_body, 0, 0), [(value.shape, F32)], [value, other], limit=4
            )
        self.total, self.value, self.level = value, value[: self.rows], LEVELS - 1
        return value

    def fetch(self, after=()):
        if self.level < LEVELS - 1:
            (self.value,) = run(
                join_body,
                [((2 * self.value.shape[0], self.value.shape[1]), F32)],
                [self.value, self.other],
                after,
                limit=8,
            )
        self.other = with_partner(self.value, self.bits[self.level])
        self.level -= 1
        return self.value


def unpack_body(count, width, layout, *refs):
    n_in = 2 * len(layout)
    outs, sem = refs[n_in:-1], refs[-1]
    owns = own_chunk(count), own_chunk(count, True)
    copies = []
    for piece, places in enumerate(layout):
        near, far = refs[2 * piece], refs[2 * piece + 1]
        for source, own in zip((near, far), owns):
            for j in range(CHUNKS // 2):
                chunk = jnp.bitwise_xor(own, j)
                part = source.shape[0] // (CHUNKS // 2) // len(places)
                for q, (out, k, column) in enumerate(places):
                    place = (j * len(places) + q) * part
                    rows = pl.ds(pl.multiple_of(chunk * part, part), part)
                    copies.append(
                        pltpu.make_async_copy(
                            source.at[pl.ds(place, part), :],
                            outs[out].at[k, rows, pl.ds(column, width)],
                            sem,
                        )
                    )
    for copy in copies:
        copy.start()
    for copy in copies:
        copy.wait()


def unpack(count, bulks, layout, shapes):
    operands = [value for bulk in bulks for value in (bulk.value, bulk.other)]
    anywhere = pl.BlockSpec(memory_space=pl.ANY)
    return pl.pallas_call(
        functools.partial(unpack_body, count, operands[0].shape[1], layout),
        out_shape=[jax.ShapeDtypeStruct(shape, F32) for shape in shapes],
        in_specs=[anywhere] * len(operands),
        out_specs=[anywhere] * len(shapes),
        scratch_shapes=[pltpu.SemaphoreType.DMA],
        compiler_params=pltpu.CompilerParams(vmem_limit_bytes=4 * MIB),
    )(*operands)


def steps(span, backward, body, start, unroll=8):
    def one(k, carry):
        return body(span - 1 - k if backward else k, carry)

    return lax.fori_loop(0, span, one, start, unroll=unroll)


def at(t, seqs):
    return pl.ds(pl.multiple_of(t * seqs, seqs), seqs)


def state_scan(v_ref, rel, lr, li, start, span, backward, keep=None):
    seqs, states = lr.shape

    def body(t, carry):
        re, im = carry
        vr, vi = v_ref[at(t, seqs), :states], v_ref[at(t, seqs), states:]
        next_re, next_im = mul(lr, li, re, im)
        live = rel > t
        re, im = jnp.where(live, next_re + vr, re), jnp.where(live, next_im + vi, im)
        if keep is not None:
            keep(t, re, im)
        return re, im

    return steps(span, backward, body, start)


def adjoint_scan(g_ref, rel, lr, li, start, span, backward, use=None, extra=()):
    seqs, states = lr.shape

    def body(t, carry):
        (re, im), kept = carry
        ar, ai = g_ref[at(t, seqs), :states] + re, g_ref[at(t, seqs), states:] + im
        live = rel > t
        if use is not None:
            kept = use(t, ar, ai, live, kept)
        next_re, next_im = mul(lr, -li, ar, ai)
        return (jnp.where(live, next_re, ar), jnp.where(live, next_im, ai)), kept

    return steps(span, backward, body, (start, extra))


def wide(ref, row, shape):
    return jnp.broadcast_to(ref[row : row + 1, :], shape)


def to_time_major(piece):
    seqs, span, width = piece.shape
    return jnp.swapaxes(piece, 0, 1).reshape(span * seqs, width)


def from_time_major(rows, seqs):
    return jnp.swapaxes(rows.reshape(-1, seqs, rows.shape[-1]), 0, 1)


def lane_tiled(column, width):
    return jnp.concatenate([column] * (width // LANES), axis=1)


def gelu_parts(y):
    cdf = 0.5 * (1.0 + lax.erf(y * inverse_root_two))
    pdf = jnp.exp(-0.5 * y * y) * density_scale
    return y * cdf, cdf + y * pdf


def sigmoid(x):
    return 1.0 / (1.0 + jnp.exp(-x))


CHUNK = 16


def prepare_body(plan, span, lens_ref, x_ref, nu_ref, phase_ref, gamma_ref, *outs):
    sums_ref, tm_ref, mask_ref, decay_ref = outs[:4]
    factor_refs = outs[4:]
    seqs, _, width = x_ref.shape
    states = nu_ref.shape[-1]
    here = lax.axis_index("tm")
    rel = jnp.broadcast_to(lens_ref[...] - here * span, (seqs, LANES))
    first = jnp.zeros((seqs, width), F32)
    second = jnp.zeros((seqs, width), F32)
    for t0 in range(0, span, 8):
        piece = jnp.swapaxes(x_ref[:, t0 : t0 + 8, :], 0, 1)
        for j in range(8):
            rows = piece[j]
            mask = jnp.where(rel > t0 + j, 1.0, 0.0)
            place = slice((t0 + j) * seqs, (t0 + j + 1) * seqs)
            mask_ref[place, :] = mask
            tm_ref[place, :] = rows
            live = rows * lane_tiled(mask, width)
            first += live
            second += live * rows
    spread(sums_ref, jnp.sum(first, 0, keepdims=True), jnp.sum(second, 0, keepdims=True))
    rate = jnp.exp(nu_ref[...])
    radius = jnp.exp(-rate)
    angle = phase_ref[...]
    cosine, sine = jnp.cos(angle), jnp.sin(angle)
    gamma = gamma_ref[...]
    for row, value in enumerate((radius * cosine, radius * sine, gamma, rate, radius, cosine, sine)):
        for k in range(2):
            decay_ref[k, row : row + 1, :] = value[k : k + 1, :]
    for k in range(2):
        for level, (radix, stride) in enumerate(plan):
            base = lax.div(here, radix * stride) * (radix * stride)
            for member in range(radix):
                start = (base + member * stride) * span
                count = jnp.clip(lens_ref[...] - start, 0, stride * span)
                count = jnp.broadcast_to(count, (seqs, states))
                power = (decay_ref[k, 0:1, :], decay_ref[k, 1:2, :])
                re, im = jnp.ones((seqs, states), F32), jnp.zeros((seqs, states), F32)
                for bit in range((span * stride).bit_length()):
                    taken = jnp.bitwise_and(count, 1 << bit) != 0
                    next_re, next_im = mul(re, im, *power)
                    re, im = jnp.where(taken, next_re, re), jnp.where(taken, next_im, im)
                    power = mul(*power, *power)
                factor_refs[level][k, member, :, :states] = re
                factor_refs[level][k, member, :, states:] = im


def relative(lens_ref, span, states):
    return jnp.broadcast_to(
        lens_ref[...] - lax.axis_index("tm") * span, (lens_ref.shape[0], states)
    )


def token_scale(lens_ref):
    return 1.0 / jnp.sum(lens_ref[...].astype(F32), axis=0, keepdims=True)


def project_body(
    k, span, backward, lens_ref, sums_ref, x_ref, gain_ref, bias_ref, w_ref, decay_ref,
    u_ref, v_ref, stats_ref, summary_ref,
):
    seqs = lens_ref.shape[0]
    states = decay_ref.shape[-1]
    total, squares = gathered(sums_ref)
    scale = token_scale(lens_ref)
    mean = total * scale
    var = squares * scale - mean * mean
    rstd = lax.rsqrt(var + norm_epsilon)
    stats_ref[0:1, :] = mean
    stats_ref[1:2, :] = var
    stats_ref[2:3, :] = rstd
    stats_ref[3:4, :] = rstd * gain_ref[k : k + 1, :]
    slope = rstd * gain_ref[k : k + 1, :]
    bias = bias_ref[k : k + 1, :]
    step = CHUNK * seqs
    for r in range(0, span * seqs, step):
        u = ((x_ref[r : r + step, :] - mean) * slope + bias).astype(BF16)
        u_ref[r : r + step, :] = u
        v_ref[r : r + step, :] = dot(u, w_ref[k])
    shape = (seqs, states)
    rel = relative(lens_ref, span, states)
    lr, li = wide(decay_ref.at[k], 0, shape), wide(decay_ref.at[k], 1, shape)
    zero = jnp.zeros(shape, F32)
    re, im = state_scan(v_ref, rel, lr, li, (zero, zero), span, backward)
    summary_ref[:, :states] = re
    summary_ref[:, states:] = im


def rebuild_states(k, plan, span, backward, refs, buffers, rel, v_ref, decay_ref, h_ref):
    seqs, states = rel.shape
    lr, li, gamma = (wide(decay_ref.at[k], row, rel.shape) for row in range(3))
    start = entering_state(k, plan, refs, buffers, backward, False)

    lead = 0 if backward else 1

    def keep(t, re, im):
        h_ref[at(t + lead, seqs), :states] = (re * gamma).astype(BF16)
        h_ref[at(t + lead, seqs), states:] = (im * gamma).astype(BF16)

    keep(span if backward else -1, *start)
    state_scan(v_ref, rel, lr, li, start, span, backward, keep)


def forward_body(
    k, plan, span, exch, lens_ref, v_ref, x_ref, mask_ref, stats_ref, bias_ref,
    decay_ref, w_out_ref, skip_ref, w_glu_ref,
    out_ref, h_ref, act_ref, slope_ref, gate_ref, value_ref, sums_ref, buffers,
):
    seqs = lens_ref.shape[0]
    width = x_ref.shape[1]
    states = decay_ref.shape[-1]
    rel = relative(lens_ref, span, states)
    rebuild_states(k, plan, span, False, exch, buffers, rel, v_ref, decay_ref, h_ref)
    mean, scale = stats_ref[0:1, :], stats_ref[3:4, :]
    bias, skip = bias_ref[k : k + 1, :], skip_ref[k : k + 1, :]
    step = CHUNK * seqs
    first = jnp.zeros((8, width), F32)
    second = jnp.zeros((8, width), F32)
    for r in range(0, span * seqs, step):
        x = x_ref[r : r + step, :]
        u = (x - mean) * scale + bias
        y = dot(h_ref[r + seqs : r + seqs + step, :], w_out_ref[k]) + skip * u
        act, slope = gelu_parts(y)
        act = act.astype(BF16)
        act_ref[r : r + step, :] = act
        slope_ref[r : r + step, :] = slope.astype(BF16)
        z = dot(act, w_glu_ref[k])
        value, gate = z[:, :width], sigmoid(z[:, width:])
        gated = value * gate
        out = x + gated
        out_ref[r : r + step, :] = out
        gate_ref[r : r + step, :] = gate.astype(BF16)
        value_ref[r : r + step, :] = (gated * (1.0 - gate)).astype(BF16)
        live = out * lane_tiled(mask_ref[r : r + step, :], width)
        first += jnp.sum(live.reshape(-1, 8, width), 0)
        second += jnp.sum((live * out).reshape(-1, 8, width), 0)
    spread(sums_ref, jnp.sum(first, 0, keepdims=True), jnp.sum(second, 0, keepdims=True))


def back_rows(k, r, step, dza, dzb, slope, width, w_glu_ref, w_out_ref, dz_ref, dy_ref, g_ref):
    dza, dzb = dza.astype(BF16), dzb.astype(BF16)
    dz_ref[r : r + step, :width] = dza
    dz_ref[r : r + step, width:] = dzb
    w = w_glu_ref[k]
    dact = dot_nt(dza, w[:, :width]) + dot_nt(dzb, w[:, width:])
    dy = (dact * slope).astype(BF16)
    dy_ref[r : r + step, :] = dy
    g_ref[r : r + step, :] = dot_nt(dy, w_out_ref[k])


def local_adjoint(k, span, backward, rel, g_ref, decay_ref, summary_ref):
    seqs, states = rel.shape
    lr, li = wide(decay_ref.at[k], 0, rel.shape), wide(decay_ref.at[k], 1, rel.shape)
    zero = jnp.zeros(rel.shape, F32)
    (re, im), _ = adjoint_scan(g_ref, rel, lr, li, (zero, zero), span, backward)
    summary_ref[:, :states] = re
    summary_ref[:, states:] = im


def turn_body(
    k, plan, span, exch, lens_ref, v_ref, x_ref, cot_ref, stats_ref, bias_ref,
    decay_ref, w_out_ref, skip_ref, w_glu_ref,
    out_ref, h_ref, act_ref, dz_ref, dy_ref, g_ref, summary_ref, buffers,
):
    seqs = lens_ref.shape[0]
    width = x_ref.shape[1]
    states = decay_ref.shape[-1]
    rel = relative(lens_ref, span, states)
    rebuild_states(k, plan, span, True, exch, buffers, rel, v_ref, decay_ref, h_ref)
    mean, scale = stats_ref[0:1, :], stats_ref[3:4, :]
    bias, skip = bias_ref[k : k + 1, :], skip_ref[k : k + 1, :]
    step = CHUNK * seqs
    for r in range(0, span * seqs, step):
        t0 = r // seqs
        x = x_ref[r : r + step, :]
        u = (x - mean) * scale + bias
        y = dot(h_ref[r : r + step, :], w_out_ref[k]) + skip * u
        act, slope = gelu_parts(y)
        act = act.astype(BF16)
        act_ref[r : r + step, :] = act
        z = dot(act, w_glu_ref[k])
        value, gate = z[:, :width], sigmoid(z[:, width:])
        gated = value * gate
        out_ref[:, t0 : t0 + CHUNK, :] = from_time_major(x + gated, seqs)
        d = to_time_major(cot_ref[:, t0 : t0 + CHUNK, :])
        back_rows(
            k, r, step, d * gate, d * (gated * (1.0 - gate)), slope, width,
            w_glu_ref, w_out_ref, dz_ref, dy_ref, g_ref,
        )
    local_adjoint(k, span, False, rel, g_ref, decay_ref, summary_ref)


def back_body(
    k, span, backward, lens_ref, sums_ref, part_ref, x_ref, mask_ref, stats_ref, slope_ref,
    gate_ref, value_ref, gain_ref, decay_ref, w_out_ref, w_glu_ref,
    d_ref, dz_ref, dy_ref, g_ref, grads_ref, summary_ref,
):
    seqs = lens_ref.shape[0]
    width = x_ref.shape[1]
    states = decay_ref.shape[-1]
    rel = relative(lens_ref, span, states)
    bias_grad, gain_grad = gathered(sums_ref)
    grads_ref[0:1, :] = gain_grad
    grads_ref[1:2, :] = bias_grad
    shift, tilt = input_terms(
        k + 1, token_scale(lens_ref), bias_grad, gain_grad, stats_ref, gain_ref
    )
    mean = stats_ref[0:1, :]
    step = CHUNK * seqs
    for r in range(0, span * seqs, step):
        live = lane_tiled(mask_ref[r : r + step, :], width)
        d = part_ref[r : r + step, :] + live * (shift + tilt * (x_ref[r : r + step, :] - mean))
        d_ref[r : r + step, :] = d
        back_rows(
            k, r, step, d * gate_ref[r : r + step, :].astype(F32),
            d * value_ref[r : r + step, :].astype(F32), slope_ref[r : r + step, :].astype(F32), width,
            w_glu_ref, w_out_ref, dz_ref, dy_ref, g_ref,
        )
    local_adjoint(k, span, backward, rel, g_ref, decay_ref, summary_ref)


def input_terms(k, scale, bias_grad, gain_grad, stats_ref, gain_ref):
    rstd = stats_ref[2:3, :]
    gain = gain_ref[k : k + 1, :]
    return -rstd * gain * bias_grad * scale, -rstd * rstd * gain * gain_grad * scale


def adjoint_body(
    k, plan, span, backward, exch, lens_ref, g_ref, h_ref, v_ref, decay_ref, dv_ref, small_ref, buffers
):
    seqs = lens_ref.shape[0]
    states = decay_ref.shape[-1]
    rel = relative(lens_ref, span, states)
    lr, li, gamma = (wide(decay_ref.at[k], row, rel.shape) for row in range(3))
    start = entering_state(k, plan, exch, buffers, backward, True)
    before = 0 if backward else 1

    def use(t, ar, ai, live, kept):
        ar, ai = jnp.where(live, ar, 0.0), jnp.where(live, ai, 0.0)
        dv_ref[at(t, seqs), :states] = (ar * gamma).astype(BF16)
        dv_ref[at(t, seqs), states:] = (ai * gamma).astype(BF16)
        pr = h_ref[at(t + before, seqs), :states].astype(F32)
        pi = h_ref[at(t + before, seqs), states:].astype(F32)
        vr, vi = v_ref[at(t, seqs), :states], v_ref[at(t, seqs), states:]
        return (
            kept[0] + (ar * pr + ai * pi),
            kept[1] + (ai * pr - ar * pi),
            kept[2] + (ar * vr + ai * vi),
        )

    zero = jnp.zeros(rel.shape, F32)
    _, kept = adjoint_scan(g_ref, rel, lr, li, start, span, backward, use, (zero, zero, zero))
    small_ref[...] = jnp.zeros_like(small_ref)
    for j in range(2):
        small_ref[0:1, j * states : (j + 1) * states] = jnp.sum(kept[j], 0, keepdims=True)
    small_ref[1:2, :states] = jnp.sum(kept[2], 0, keepdims=True)


def input_body(
    k, seqs, seq_major, dv_ref, dy_ref, x_ref, d_ref, stats_ref, gain_ref, bias_ref, w_in_ref, skip_ref,
    part_ref, skip_grad_ref, sums_ref,
):
    width = x_ref.shape[1]
    mean, scale, rstd = stats_ref[0:1, :], stats_ref[3:4, :], stats_ref[2:3, :]
    gain, bias, skip = (ref[k : k + 1, :] for ref in (gain_ref, bias_ref, skip_ref))
    step = CHUNK * seqs
    first = jnp.zeros((8, width), F32)
    second = jnp.zeros((8, width), F32)
    third = jnp.zeros((8, width), F32)
    for r in range(0, x_ref.shape[0], step):
        xhat = (x_ref[r : r + step, :] - mean) * rstd
        dy = dy_ref[r : r + step, :].astype(F32)
        du = dot_nt(dv_ref[r : r + step, :], w_in_ref[k]) + dy * skip
        first += jnp.sum(du.reshape(-1, 8, width), 0)
        second += jnp.sum((du * xhat).reshape(-1, 8, width), 0)
        third += jnp.sum((dy * (xhat * gain + bias)).reshape(-1, 8, width), 0)
        if seq_major:
            d = to_time_major(d_ref[:, r // seqs : r // seqs + CHUNK, :])
        else:
            d = d_ref[r : r + step, :]
        part_ref[r : r + step, :] = d + du * scale
    skip_grad_ref[...] = third
    if seq_major:
        spread(sums_ref, jnp.sum(first, 0, keepdims=True), jnp.sum(second, 0, keepdims=True))
    else:
        sums_ref[0] = first
        sums_ref[1] = second


def small_body(small0, skip0, sums0, small1, skip1, out):
    out[...] = jnp.zeros_like(out)
    rows = [small0[0:1, :], small0[1:2, :], skip0[...], sums0[0], sums0[1]]
    for row, value in enumerate(rows):
        out[row : row + 1, :] = jnp.sum(value, 0, keepdims=True)
    for row, value in enumerate([small1[0:1, :], small1[1:2, :], skip1[...]]):
        out[8 + row : 9 + row, :] = jnp.sum(value, 0, keepdims=True)


def finish_body(
    span, total_ref, lens_ref, part_ref, x_ref, mask_ref, gain_ref, decay_ref, running_ref, stats0_ref,
    stats1_ref, grads_ref, out_ref, g_gain_ref, g_bias_ref, nu_ref, phase_ref, skip_ref, run_ref,
):
    stats_refs = (stats0_ref, stats1_ref)
    small = total_ref[total_ref.shape[0] - 16 :, :]
    states = decay_ref.shape[-1]
    count = jnp.sum(lens_ref[...].astype(F32), axis=0, keepdims=True)
    for k in range(2):
        _, _, gamma, rate, radius, cosine, sine = (decay_ref[k, j : j + 1, :] for j in range(7))
        sum_re, sum_im = small[8 * k : 8 * k + 1, :states], small[8 * k : 8 * k + 1, states:]
        g_gamma = small[8 * k + 1 : 8 * k + 2, :states]
        nu_ref[k : k + 1, :] = (sum_re * cosine + sum_im * sine) * (
            -radius * rate
        ) + g_gamma * rate * radius * radius / gamma
        phase_ref[k : k + 1, :] = radius * (sum_im * cosine - sum_re * sine)
        skip_ref[k : k + 1, :] = small[8 * k + 2 : 8 * k + 3, :]
        mean, var = stats_refs[k][0:1, :], stats_refs[k][1:2, :]
        run_ref[k, 0:1, :] = (1.0 - momentum) * running_ref[k, 0:1, :] + momentum * mean
        run_ref[k, 1:2, :] = (1.0 - momentum) * running_ref[k, 1:2, :] + momentum * var * (
            count / (count - 1.0)
        )
    bias_grad, gain_grad = small[3:4, :], small[4:5, :]
    g_gain_ref[0:1, :], g_gain_ref[1:2, :] = gain_grad, grads_ref[0:1, :]
    g_bias_ref[0:1, :], g_bias_ref[1:2, :] = bias_grad, grads_ref[1:2, :]
    seqs = out_ref.shape[0]
    width = x_ref.shape[1]
    shift, tilt = input_terms(0, 1.0 / count, bias_grad, gain_grad, stats_refs[0], gain_ref)
    mean = stats_refs[0][0:1, :]
    step = CHUNK * seqs
    for r in range(0, span * seqs, step):
        live = lane_tiled(mask_ref[r : r + step, :], width)
        d = part_ref[r : r + step, :] + live * (shift + tilt * (x_ref[r : r + step, :] - mean))
        out_ref[:, r // seqs : r // seqs + CHUNK, :] = from_time_major(d, seqs)


def with_entry(body, plan):
    def wrapped(*refs):
        n_exch = sum(radix for radix, _ in plan) + len(plan)
        body(refs[:n_exch], *refs[n_exch : -len(plan)], refs[-len(plan) :])

    return wrapped


def shards(
    inputs, lengths, cotangent, bn_gain, bn_bias, running, w_in, nu_log, phase, w_out, skip, w_glu
):
    seqs, span, width = inputs.shape
    states = nu_log.shape[1]
    count = lax.axis_size("tm")
    rows = span * seqs
    plan = stages(count)
    lens = lengths[:, None]

    tile = ((count, 2 * width // LANES, LANES), F32)
    whole, whole_low = ((rows, width), F32), ((rows, width), BF16)
    pair, pair_low = ((rows, 2 * states), F32), ((rows, 2 * states), BF16)
    double_low = ((rows, 2 * width), BF16)
    held_low = ((rows + seqs, 2 * states), BF16)
    summary = ((seqs, 2 * states), F32)
    eight = ((8, width), F32)
    seq_major = ((seqs, span, width), F32)
    buffers = entry_scratch(plan, summary[0])

    prepared = run(
        functools.partial(prepare_body, plan, span),
        [tile, whole, ((rows, LANES), F32), ((2, 8, states), F32)]
        + [((2, radix) + summary[0], F32) for radix, _ in plan],
        [lens, inputs, nu_log, phase, jnp.sqrt(-jnp.expm1(-2.0 * jnp.exp(nu_log)))],
    )
    sums, x0, mask, decay = prepared[:4]
    factors = prepared[4:]

    def project(k, sums, x):
        return run(
            functools.partial(project_body, k, span, k == 1),
            [whole_low, pair, eight, summary],
            [lens, everywhere(sums), x, bn_gain, bn_bias, w_in, decay],
        )

    def entered(body, outs, held, operands, after=(), limit=12):
        operands = entry_operands(held, factors) + operands
        return run(with_entry(body, plan), outs, operands, after, buffers, limit)

    u0, v0, stats0, part = project(0, sums, x0)
    held = exchange(0, part, plan, factors, False, False)
    x1, h0, act0, slope0, gate0, value0, sums = entered(
        functools.partial(forward_body, 0, plan, span),
        [whole, held_low, whole_low, whole_low, whole_low, whole_low, tile],
        held,
        [lens, v0, x0, mask, stats0, bn_bias, decay, w_out, skip, w_glu],
    )
    u1, v1, stats1, part = project(1, sums, x1)
    held = exchange(1, part, plan, factors, True, False)
    output, h1, act1, dz1, dy1, g1, part = entered(
        functools.partial(turn_body, 1, plan, span),
        [seq_major, held_low, whole_low, double_low, whole_low, pair, summary],
        held,
        [lens, v1, x1, cotangent, stats1, bn_bias, decay, w_out, skip, w_glu],
    )

    flows = {}
    flows["top"] = Bulk(count, [act1, h1], [dz1, dy1], [(0, 0, 0, 0), (0, 0, 0, width), (1, 0, 1, 0)])
    flows["top"].send()

    def beside_top(level, group):
        if level == 0:
            return flows["top"].parts[-1:]
        if level == len(plan) - 2:
            return [flows["top"].send([group[1]])]
        return ()

    held = exchange(1, part, plan, factors, False, True, beside_top)
    top = flows["top"]
    dv1, small1 = entered(
        functools.partial(adjoint_body, 1, plan, span, False),
        [pair_low, eight],
        held,
        [lens, g1, h1, v1, decay],
    )
    part1, skip1, sums = run(
        functools.partial(input_body, 1, seqs, True),
        [whole, eight, tile],
        [dv1, dy1, x1, cotangent, stats1, bn_gain, bn_bias, w_in, skip],
    )
    top.send([sums])
    sums = everywhere(sums)
    step = top.send([sums])
    d0, dz0, dy0, g0, grads1, part = run(
        functools.partial(back_body, 0, span, True),
        [whole, double_low, whole_low, pair, eight, summary],
        [lens, sums, part1, x1, mask, stats1, slope0, gate0, value0, bn_gain, decay, w_out, w_glu],
        [step],
    )

    flows["middle"] = Bulk(
        count, [act0, h0], [dz0, dy0], [(0, 0, 0, 0), (0, 0, 0, width), (1, seqs, 1, 0)], [part]
    )
    flows["middle"].send()

    def beside_middle(level, group):
        if level == 0:
            return [flows["middle"].parts[-1], top.send([flows["middle"].parts[-1]])]
        if level == len(plan) - 2:
            return [flows["middle"].send([group[1]])]
        return ()

    held = exchange(0, part, plan, factors, True, True, beside_middle)
    middle = flows["middle"]
    own = top.settle([held[-1][1]])
    top.fetch()
    dv0, small0 = entered(
        functools.partial(adjoint_body, 0, plan, span, True),
        [pair_low, eight],
        held,
        [lens, g0, h0, v0, decay],
        [own],
    )
    part0, skip0, sums = run(
        functools.partial(input_body, 0, seqs, False),
        [whole, eight, ((2, 8, width), F32)],
        [dv0, dy0, x0, d0, stats0, bn_gain, bn_bias, w_in, skip],
    )

    (small,) = run(small_body, [((16, width), F32)], [small0, skip0, sums, small1, skip1], limit=4)
    last = Bulk(
        count, [u0, u1], [dv0, dv1], [(0, 0, 0, 0), (1, 0, 1, 0)], [part0], [small]
    )
    last.send()
    step = middle.send([last.parts[-1]])
    step = top.fetch([step])
    step = last.send([step])
    step = middle.send([step])
    step = last.send([step])
    step = top.fetch([step])
    step = middle.send([step])
    step = last.send([step])
    step = middle.settle([step])
    middle.fetch()
    step = top.fetch([step])
    step = last.send([step])
    step = middle.fetch([step])
    step = last.settle([step])
    last.fetch()
    step = middle.fetch([step])
    grad_x, g_gain, g_bias, g_nu, g_phase, g_skip, running_out = run(
        functools.partial(finish_body, span),
        [seq_major] + [((2, width), F32)] * 2 + [((2, states), F32)] * 2
        + [((2, width), F32), ((2, 2, width), F32)],
        [last.total, lens, part0, x0, mask, bn_gain, decay, running, stats0, stats1, grads1],
        [step],
    )
    step = last.fetch([g_gain])
    step = top.fetch([step])
    step = middle.fetch([step])
    step = last.fetch([step])
    step = last.fetch([step])
    step = middle.fetch([step])
    step = last.fetch([step])
    g_glu, g_out, g_in = unpack(
        count,
        [top, middle, last],
        [
            [(0, 1, 0), (0, 1, width), (1, 1, 0)],
            [(0, 0, 0), (0, 0, width), (1, 0, 0)],
            [(2, 0, 0), (2, 1, 0)],
        ],
        [(2, width, 2 * width), (2, 2 * states, width), (2, width, 2 * states)],
    )
    return (output, grad_x, g_gain, g_bias, g_in, g_nu, g_phase, g_out, g_skip, g_glu, running_out)


def solution(mesh):
    placed = (P(None, "tm", None), P(), P(None, "tm", None)) + (P(),) * 9
    return jax.shard_map(
        shards,
        mesh=mesh,
        in_specs=placed,
        out_specs=(P(None, "tm", None),) * 2 + (P(),) * 9,
        check_vma=False,
    )
```

```python
import functools
import math

import jax
import jax.numpy as jnp
from jax import lax
from jax.experimental import pallas as pl
from jax.experimental.pallas import tpu as pltpu
from jax.sharding import PartitionSpec as P

norm_epsilon = 1e-05
momentum = 0.1
inverse_root_two = 0.7071067811865476
density_scale = 0.3989422804014327
F32, BF16 = jnp.float32, jnp.bfloat16
LANES = 128
MIB = 1 << 20


def dot(left, right):
    return jnp.dot(left, right, preferred_element_type=F32)


def dot_tn(left, right):
    return lax.dot_general(left, right, (((0,), (0,)), ((), ())), preferred_element_type=F32)


def dot_nt(left, right):
    return lax.dot_general(left, right, (((1,), (1,)), ((), ())), preferred_element_type=F32)


def run(body, outs, operands, after=(), scratch=(), limit=24, weight=1 << 33):
    vmem = pl.BlockSpec(memory_space=pltpu.VMEM)
    anywhere = pl.BlockSpec(memory_space=pl.ANY)
    first, second = len(operands), len(operands) + len(after)

    def kernel(*refs):
        body(*refs[:first], *refs[second:])

    return pl.pallas_call(
        kernel,
        out_shape=[jax.ShapeDtypeStruct(shape, dtype) for shape, dtype in outs],
        in_specs=[vmem] * len(operands) + [anywhere] * len(after),
        out_specs=[vmem] * len(outs),
        scratch_shapes=list(scratch),
        compiler_params=pltpu.CompilerParams(vmem_limit_bytes=limit * MIB),
        cost_estimate=pl.CostEstimate(flops=weight, bytes_accessed=0, transcendentals=0),
    )(*operands, *after)


def radices(count):
    out = []
    while count > 1:
        radix = 2 if not out or count % 4 else 4
        out.append(radix)
        count //= radix
    return out


def stages(count):
    stride, out = 1, []
    for radix in radices(count):
        out.append((radix, stride))
        stride *= radix
    return out


def swap(value, stride, mask):
    count = lax.axis_size("tm")
    return lax.ppermute(value, "tm", [(i, i ^ (stride * mask)) for i in range(count)])


def group_of(value, radix, stride):
    return [value] + [swap(value, stride, mask) for mask in range(1, radix)]


def place_in(radix, stride):
    return lax.rem(lax.div(lax.axis_index("tm"), stride), radix)


def rows_to_tile(first, second):
    pieces = [
        row[:, j : j + LANES] for row in (first, second) for j in range(0, row.shape[1], LANES)
    ]
    return jnp.concatenate(pieces, axis=0)


def tile_to_rows(tile):
    half = tile.shape[0] // 2
    return [
        jnp.concatenate([tile[base + j : base + j + 1, :] for j in range(half)], axis=1)
        for base in (0, half)
    ]


def spread(ref, first, second):
    ref[...] = jnp.broadcast_to(rows_to_tile(first, second)[None], ref.shape)


def gathered(ref):
    return tile_to_rows(jnp.sum(ref[...], axis=0))


def everywhere(tiles):
    return lax.all_to_all(tiles, "tm", 0, 0)


def mul(ar, ai, br, bi):
    return ar * br - ai * bi, ar * bi + ai * br


def members(refs, place, buffer):
    for offset, ref in enumerate(refs):
        buffer[jnp.bitwise_xor(place, offset)] = ref[...]


def pass_through(k, buffer, factor, place, state, backward, conj):
    radix, _, width = buffer.shape
    states = width // 2
    if state is None:
        zero = jnp.zeros(buffer.shape[1:-1] + (states,), F32)
        state = (zero, zero)
    entering = state
    for member in range(radix - 1, -1, -1) if backward else range(radix):
        entering = tuple(jnp.where(place == member, s, e) for s, e in zip(state, entering))
        fr, fi = factor[k, member, :, :states], factor[k, member, :, states:]
        moved = mul(fr, -fi if conj else fi, *state)
        state = (moved[0] + buffer[member, :, :states], moved[1] + buffer[member, :, states:])
    return entering, state


def total_body(k, radix, stride, backward, conj, *refs):
    factor, out, buffer = refs[radix:]
    place = place_in(radix, stride)
    members(refs[:radix], place, buffer)
    _, (re, im) = pass_through(k, buffer, factor, place, None, backward, conj)
    states = re.shape[1]
    out[:, :states] = re
    out[:, states:] = im


def group_total(k, group, level, plan, factors, backward, conj, after=()):
    radix, stride = plan[level]
    shape = group[0].shape
    (total,) = run(
        functools.partial(total_body, k, radix, stride, backward, conj),
        [(shape, F32)],
        list(group) + [factors[level]],
        after,
        [pltpu.VMEM((radix,) + shape, F32)],
        limit=4,
    )
    return total


def exchange(k, summary, plan, factors, backward, conj, between=None):
    held = []
    value = summary
    for level, (radix, stride) in enumerate(plan):
        group = group_of(value, radix, stride)
        held.append(group)
        if level + 1 < len(plan):
            after = between(level, group) if between else ()
            value = group_total(k, group, level, plan, factors, backward, conj, after)
            if between and level + 2 == len(plan):
                between(level + 1, [value])
    return held


def entry_operands(held, factors):
    return [value for group in held for value in group] + list(factors)


def entry_scratch(plan, shape):
    return [pltpu.VMEM((radix,) + shape, F32) for radix, _ in plan]


def entering_state(k, plan, refs, buffers, backward, conj):
    total = sum(radix for radix, _ in plan)
    values, factors = refs[:total], refs[total:]
    start, groups = 0, []
    for radix, _ in plan:
        groups.append(values[start : start + radix])
        start += radix
    state = None
    for level in range(len(plan) - 1, -1, -1):
        place = place_in(*plan[level])
        members(groups[level], place, buffers[level])
        state, _ = pass_through(k, buffers[level], factors[level], place, state, backward, conj)
    return state


CHUNKS = 32
LEVELS = CHUNKS.bit_length() - 1


def partners(count):
    order = [(1 << b, 1 << b) for b in range(count.bit_length() - 1)]
    if len(order) > 2:
        order[1], order[2] = (2, 4), (4, 2)
    return order


def with_partner(value, bits):
    even, odd = bits
    count = lax.axis_size("tm")
    return lax.ppermute(value, "tm", [(i, i ^ (odd if i & 1 else even)) for i in range(count)])


def own_chunk(count, other_core=False):
    here = lax.axis_index("tm")
    if other_core:
        here = jnp.bitwise_xor(here, 1)
    own = 0
    for even, odd in partners(count)[:LEVELS]:
        taken = jnp.where(jnp.bitwise_and(here, 1) == 1, here & odd, here & even)
        own = own * 2 + jnp.where(taken != 0, 1, 0)
    return own


def slots(level):
    return (CHUNKS >> (level + 1), CHUNKS >> level) if level < LEVELS else (0, 1)


def outer_body(count, pairs, n_left, n_right, n_extra, *refs):
    lefts, rights = refs[:n_left], refs[n_left : n_left + n_right]
    extra, outs = refs[n_left + n_right :][:n_extra], refs[n_left + n_right + n_extra : -len(pairs)]
    products = refs[-len(pairs) :]
    if extra:
        outs[0][-extra[0].shape[0] :, :] = extra[0][...]
    owns = own_chunk(count), own_chunk(count, True)
    half = CHUNKS // 2
    for q, (left, row, right, column) in enumerate(pairs):
        product = products[q]
        span = rights[right].shape[0]
        wide_left = lefts[left].shape[1]
        part = wide_left // CHUNKS
        width = product.shape[1]
        product[...] = dot_tn(
            lefts[left][row : row + span, :], rights[right][:, column : column + width]
        )
        for level in range(LEVELS + 1):
            low, high = slots(level)
            for slot in range(low, high):
                chunk = jnp.bitwise_xor(owns[slot // half], slot % half)
                chunk = pl.multiple_of(chunk * part, part)
                place = ((slot - low) * len(pairs) + q) * part
                outs[level][place : place + part, :] = product[pl.ds(chunk, part), :]


def add_body(low, extra, *refs):
    out = refs[-1]
    rows = out.shape[0] - extra
    total = refs[0][:rows, :]
    for ref in refs[1 : -2 if extra else -1]:
        total += ref[low : low + rows, :]
    out[:rows, :] = total
    if extra:
        mine, other = refs[-2], refs[-3]
        out[rows:, :] = mine[-extra:, :] + other[-extra:, :]


def spokes_body(rows, extra, *refs):
    near, far = refs[:2]
    received, mine, outs = refs[2:-4], refs[-4], refs[-3:]
    for slot, out in enumerate(outs, 1):
        total = near[...] if slot == 1 else far[(slot - 2) * rows : (slot - 1) * rows, :]
        for ref in received:
            total += ref[slot * rows : (slot + 1) * rows, :]
        out[:rows, :] = total
        if extra:
            out[rows:, :] = mine[-extra:, :] + received[-1][-extra:, :]


def hub_body(rows, extra, *refs):
    kept, received, mine, spokes, out = refs[0], refs[1:-5], refs[-5], refs[-4:-1], refs[-1]
    total = kept[...]
    for ref in received + spokes:
        total += ref[:rows, :]
    out[:rows, :] = total
    if extra:
        total = mine[-extra:, :]
        for ref in spokes:
            total += ref[-extra:, :]
        out[rows:, :] = total


def join_body(*refs):
    out = refs[-1]
    rows = refs[0].shape[0]
    for j, ref in enumerate(refs[:-1]):
        out[j * rows : (j + 1) * rows] = ref[...]


class Bulk:
    def __init__(self, count, lefts, rights, pairs, after=(), extra=(), hub=False, weight=1 << 33):
        self.hub = hub
        self.bits = partners(count)
        self.extra = extra[0].shape[0] if extra else 0
        width = 512
        part = lefts[0].shape[1] // CHUNKS
        self.rows = part * len(pairs)
        outs = [((self.rows * (hi - lo), width), F32) for lo, hi in map(slots, range(LEVELS + 1))]
        outs[0] = ((outs[0][0][0] + self.extra, width), F32)
        self.parts = run(
            functools.partial(outer_body, count, pairs, len(lefts), len(rights), len(extra)),
            outs,
            list(lefts) + list(rights) + list(extra),
            after,
            [pltpu.VMEM((lefts[pair[0]].shape[1], width), F32) for pair in pairs],
            limit=16,
            weight=weight,
        )
        self.received = []
        self.sent = None

    def reduced(self, level, after=()):
        low, high = slots(level)
        if not self.received:
            return self.parts[level]
        (total,) = run(
            functools.partial(add_body, low * self.rows, self.extra),
            [((self.rows * (high - low) + self.extra, self.parts[level].shape[1]), F32)],
            [self.parts[level]] + self.received + ([self.sent] if self.extra else []),
            after,
            limit=8,
        )
        return total

    def send(self, after=()):
        level = len(self.received)
        if self.hub and level == LEVELS - 2:
            shape = (self.rows + self.extra, self.parts[LEVELS].shape[1])
            sent = run(
                functools.partial(spokes_body, self.rows, self.extra),
                [(shape, F32)] * 3,
                [self.parts[LEVELS - 1], self.parts[LEVELS - 2]] + self.received + [self.sent],
                after,
                limit=8,
            )
            self.sent, self.spokes = sent[0], self.with_partners(sent)
            return self.sent
        self.sent = self.reduced(level, after)
        self.received.append(with_partner(self.sent, self.bits[level]))
        return self.sent

    def with_partners(self, values):
        far, near = self.bits[LEVELS - 2][0], self.bits[LEVELS - 1][0]
        masks = (near, far, near | far)
        return [swap(value, 1, mask) for value, mask in zip(values, masks)]

    def settle(self, after=()):
        if self.hub:
            (value,) = run(
                functools.partial(hub_body, self.rows, self.extra),
                [((self.rows + self.extra, self.parts[LEVELS].shape[1]), F32)],
                [self.parts[LEVELS]] + self.received + [self.sent] + self.spokes,
                after,
                limit=8,
            )
        else:
            value = self.reduced(LEVELS, after)
        for even, odd in self.bits[LEVELS:]:
            other = with_partner(value, (even, odd))
            (value,) = run(
                functools.partial(add_body, 0, 0), [(value.shape, F32)], [value, other], limit=4
            )
        self.total, self.value, self.level = value, value[: self.rows], LEVELS - 1
        return value

    def fetch(self, after=()):
        if self.level < LEVELS - 1:
            parts = [self.value] + self.others
            (self.value,) = run(
                join_body,
                [((len(parts) * self.value.shape[0], self.value.shape[1]), F32)],
                parts,
                after,
                limit=8,
            )
        if self.hub and self.level == LEVELS - 1:
            self.others = self.with_partners([self.value] * 3)
            self.level -= 2
        else:
            self.others = [with_partner(self.value, self.bits[self.level])]
            self.level -= 1
        return self.value


def unpack_body(count, width, layout, n_after, *refs):
    outs, sem = refs[2 * len(layout) + n_after : -1], refs[-1]
    owns = own_chunk(count), own_chunk(count, True)
    copies = []
    for piece, places in enumerate(layout):
        near, far = refs[2 * piece], refs[2 * piece + 1]
        for source, own in zip((near, far), owns):
            for j in range(CHUNKS // 2):
                chunk = jnp.bitwise_xor(own, j)
                part = source.shape[0] // (CHUNKS // 2) // len(places)
                for q, (out, k, column) in enumerate(places):
                    place = (j * len(places) + q) * part
                    rows = pl.ds(pl.multiple_of(chunk * part, part), part)
                    copies.append(
                        pltpu.make_async_copy(
                            source.at[pl.ds(place, part), :],
                            outs[out].at[k, rows, pl.ds(column, width)],
                            sem,
                        )
                    )
    for copy in copies:
        copy.start()
    for copy in copies:
        copy.wait()


def unpack(count, bulks, layout, shapes, after=()):
    operands = [value for bulk in bulks for value in (bulk.value, bulk.others[0])]
    anywhere = pl.BlockSpec(memory_space=pl.ANY)
    return pl.pallas_call(
        functools.partial(unpack_body, count, operands[0].shape[1], layout, len(after)),
        out_shape=[jax.ShapeDtypeStruct(shape, F32) for shape in shapes],
        in_specs=[anywhere] * (len(operands) + len(after)),
        out_specs=[anywhere] * len(shapes),
        scratch_shapes=[pltpu.SemaphoreType.DMA],
        compiler_params=pltpu.CompilerParams(vmem_limit_bytes=4 * MIB),
    )(*operands, *after)


def steps(span, backward, body, start, unroll=8):
    def one(k, carry):
        return body(span - 1 - k if backward else k, carry)

    return lax.fori_loop(0, span, one, start, unroll=unroll)


def at(t, seqs):
    return pl.ds(pl.multiple_of(t * seqs, seqs), seqs)


def state_scan(v_ref, rel, lr, li, start, span, backward, keep=None):
    seqs, states = lr.shape

    def body(t, carry):
        re, im = carry
        vr, vi = v_ref[at(t, seqs), :states], v_ref[at(t, seqs), states:]
        next_re, next_im = mul(lr, li, re, im)
        live = rel > t
        re, im = jnp.where(live, next_re + vr, re), jnp.where(live, next_im + vi, im)
        if keep is not None:
            keep(t, re, im)
        return re, im

    return steps(span, backward, body, start)


def adjoint_scan(g_ref, rel, lr, li, start, span, backward, use=None, extra=()):
    seqs, states = lr.shape

    def body(t, carry):
        (re, im), kept = carry
        ar, ai = g_ref[at(t, seqs), :states] + re, g_ref[at(t, seqs), states:] + im
        live = rel > t
        if use is not None:
            kept = use(t, ar, ai, live, kept)
        next_re, next_im = mul(lr, -li, ar, ai)
        return (jnp.where(live, next_re, ar), jnp.where(live, next_im, ai)), kept

    return steps(span, backward, body, (start, extra))


def wide(ref, row, shape):
    return jnp.broadcast_to(ref[row : row + 1, :], shape)


def to_time_major(piece):
    seqs, span, width = piece.shape
    return jnp.swapaxes(piece, 0, 1).reshape(span * seqs, width)


def from_time_major(rows, seqs):
    return jnp.swapaxes(rows.reshape(-1, seqs, rows.shape[-1]), 0, 1)


def lane_tiled(column, width):
    return jnp.concatenate([column] * (width // LANES), axis=1)


def gelu_parts(y):
    cdf = 0.5 * (1.0 + lax.erf(y * inverse_root_two))
    pdf = jnp.exp(-0.5 * y * y) * density_scale
    return y * cdf, cdf + y * pdf


sigmoid = jax.nn.sigmoid


CHUNK = 64
PIECE = 8


def prepare_body(plan, span, lengths_any, x_any, nu_any, phase_any, *outs):
    lens_ref, sums_ref, tm_ref, mask_ref, decay_ref = outs[:5]
    factor_refs = outs[5 : 5 + len(plan)]
    lengths_ref, x_ref, nu_ref, phase_ref, sems = outs[5 + len(plan) :]
    seqs, _, width = x_ref.shape
    states = nu_ref.shape[-1]
    copies = [
        pltpu.make_async_copy(
            x_any.at[:, pl.ds(t0, PIECE), :], x_ref.at[:, pl.ds(t0, PIECE), :], sems.at[t0 // PIECE]
        )
        for t0 in range(0, span, PIECE)
    ]
    small = [
        pltpu.make_async_copy(nu_any, nu_ref, sems.at[len(copies)]),
        pltpu.make_async_copy(phase_any, phase_ref, sems.at[len(copies) + 1]),
        pltpu.make_async_copy(lengths_any, lengths_ref, sems.at[len(copies) + 2]),
    ]
    for copy in small + copies:
        copy.start()
    for copy in small:
        copy.wait()
    here = lax.axis_index("tm")
    row = lax.broadcasted_iota(jnp.int32, (seqs, LANES), 0)
    lens = jnp.zeros((seqs, LANES), jnp.int32)
    for seq in range(seqs):
        lens = jnp.where(row == seq, lengths_ref[seq], lens)
    lens_ref[...] = lens
    rel = lens - here * span
    rate = jnp.exp(nu_ref[...])
    radius = jnp.exp(-rate)
    angle = phase_ref[...]
    cosine, sine = jnp.cos(angle), jnp.sin(angle)
    gamma = jnp.sqrt(one_less_exp(2.0 * rate))
    for row, value in enumerate((radius * cosine, radius * sine, gamma, rate, radius, cosine, sine)):
        for k in range(2):
            decay_ref[k, row : row + 1, :] = value[k : k + 1, :]
    for k in range(2):
        for level, (radix, stride) in enumerate(plan):
            base = lax.div(here, radix * stride) * (radix * stride)
            for member in range(radix):
                start = (base + member * stride) * span
                count = jnp.concatenate(
                    [jnp.clip(lens - start, 0, stride * span)] * (states // LANES), axis=1
                )
                power = (decay_ref[k, 0:1, :], decay_ref[k, 1:2, :])
                re, im = jnp.ones((seqs, states), F32), jnp.zeros((seqs, states), F32)
                for bit in range((span * stride).bit_length()):
                    taken = jnp.bitwise_and(count, 1 << bit) != 0
                    next_re, next_im = mul(re, im, *power)
                    re, im = jnp.where(taken, next_re, re), jnp.where(taken, next_im, im)
                    power = mul(*power, *power)
                factor_refs[level][k, member, :, :states] = re
                factor_refs[level][k, member, :, states:] = im
    first = jnp.zeros((seqs, width), F32)
    second = jnp.zeros((seqs, width), F32)
    for t0 in range(0, span, PIECE):
        copies[t0 // PIECE].wait()
        piece = jnp.swapaxes(x_ref[:, t0 : t0 + PIECE, :], 0, 1)
        for j in range(PIECE):
            rows = piece[j]
            mask = jnp.where(rel > t0 + j, 1.0, 0.0)
            place = slice((t0 + j) * seqs, (t0 + j + 1) * seqs)
            mask_ref[place, :] = mask
            tm_ref[place, :] = rows
            live = rows * lane_tiled(mask, width)
            first += live
            second += live * rows
    spread(sums_ref, jnp.sum(first, 0, keepdims=True), jnp.sum(second, 0, keepdims=True))


def one_less_exp(x):
    total = 1.0
    for n in range(8, 1, -1):
        total = 1.0 - total * x * (1.0 / n)
    return total * x


def relative(lens_ref, span, states):
    rel = lens_ref[...] - lax.axis_index("tm") * span
    return jnp.concatenate([rel] * (states // LANES), axis=1)


def token_scale(lens_ref):
    return 1.0 / jnp.sum(lens_ref[:, 0:1].astype(F32), axis=0, keepdims=True)


def project_body(
    k, span, backward, lens_ref, sums_ref, x_ref, gain_ref, bias_ref, w_ref, decay_ref,
    u_ref, v_ref, stats_ref, summary_ref,
):
    seqs = lens_ref.shape[0]
    states = decay_ref.shape[-1]
    total, squares = gathered(sums_ref)
    scale = token_scale(lens_ref)
    mean = total * scale
    var = squares * scale - mean * mean
    rstd = lax.rsqrt(var + norm_epsilon)
    stats_ref[0:1, :] = mean
    stats_ref[1:2, :] = var
    stats_ref[2:3, :] = rstd
    stats_ref[3:4, :] = rstd * gain_ref[k : k + 1, :]
    slope = rstd * gain_ref[k : k + 1, :]
    bias = bias_ref[k : k + 1, :]
    step = CHUNK * seqs
    for r in range(0, span * seqs, step):
        u = ((x_ref[r : r + step, :] - mean) * slope + bias).astype(BF16)
        u_ref[r : r + step, :] = u
        v_ref[r : r + step, :] = dot(u, w_ref[k])
    shape = (seqs, states)
    rel = relative(lens_ref, span, states)
    lr, li = wide(decay_ref.at[k], 0, shape), wide(decay_ref.at[k], 1, shape)
    zero = jnp.zeros(shape, F32)
    re, im = state_scan(v_ref, rel, lr, li, (zero, zero), span, backward)
    summary_ref[:, :states] = re
    summary_ref[:, states:] = im


def rebuild_states(k, plan, span, backward, refs, buffers, rel, v_ref, decay_ref, h_ref):
    seqs, states = rel.shape
    lr, li, gamma = (wide(decay_ref.at[k], row, rel.shape) for row in range(3))
    start = entering_state(k, plan, refs, buffers, backward, False)

    lead = 0 if backward else 1

    def keep(t, re, im):
        h_ref[at(t + lead, seqs), :states] = (re * gamma).astype(BF16)
        h_ref[at(t + lead, seqs), states:] = (im * gamma).astype(BF16)

    keep(span if backward else -1, *start)
    state_scan(v_ref, rel, lr, li, start, span, backward, keep)


def forward_body(
    k, plan, span, exch, lens_ref, v_ref, x_ref, mask_ref, stats_ref, bias_ref,
    decay_ref, w_out_ref, skip_ref, w_glu_ref,
    out_ref, h_ref, act_ref, slope_ref, gate_ref, value_ref, sums_ref, buffers,
):
    seqs = lens_ref.shape[0]
    width = x_ref.shape[1]
    states = decay_ref.shape[-1]
    rel = relative(lens_ref, span, states)
    rebuild_states(k, plan, span, False, exch, buffers, rel, v_ref, decay_ref, h_ref)
    mean, scale = stats_ref[0:1, :], stats_ref[3:4, :]
    bias, skip = bias_ref[k : k + 1, :], skip_ref[k : k + 1, :]
    step = CHUNK * seqs
    first = jnp.zeros((8, width), F32)
    second = jnp.zeros((8, width), F32)
    for r in range(0, span * seqs, step):
        x = x_ref[r : r + step, :]
        u = (x - mean) * scale + bias
        y = dot(h_ref[r + seqs : r + seqs + step, :], w_out_ref[k]) + skip * u
        act, slope = gelu_parts(y)
        act = act.astype(BF16)
        act_ref[r : r + step, :] = act
        slope_ref[r : r + step, :] = slope.astype(BF16)
        z = dot(act, w_glu_ref[k])
        value, gate = z[:, :width], sigmoid(z[:, width:])
        gated = value * gate
        out = x + gated
        out_ref[r : r + step, :] = out
        gate_ref[r : r + step, :] = gate.astype(BF16)
        value_ref[r : r + step, :] = (gated * (1.0 - gate)).astype(BF16)
        live = out * lane_tiled(mask_ref[r : r + step, :], width)
        first += jnp.sum(live.reshape(-1, 8, width), 0)
        second += jnp.sum((live * out).reshape(-1, 8, width), 0)
    spread(sums_ref, jnp.sum(first, 0, keepdims=True), jnp.sum(second, 0, keepdims=True))


def back_rows(k, r, step, dza, dzb, slope, width, w_glu_ref, w_out_ref, dz_ref, dy_ref, g_ref):
    dza, dzb = dza.astype(BF16), dzb.astype(BF16)
    dz_ref[r : r + step, :width] = dza
    dz_ref[r : r + step, width:] = dzb
    w = w_glu_ref[k]
    dact = dot_nt(dza, w[:, :width]) + dot_nt(dzb, w[:, width:])
    dy = (dact * slope).astype(BF16)
    dy_ref[r : r + step, :] = dy
    g_ref[r : r + step, :] = dot_nt(dy, w_out_ref[k])


def local_adjoint(k, span, backward, rel, g_ref, decay_ref, summary_ref):
    seqs, states = rel.shape
    lr, li = wide(decay_ref.at[k], 0, rel.shape), wide(decay_ref.at[k], 1, rel.shape)
    zero = jnp.zeros(rel.shape, F32)
    (re, im), _ = adjoint_scan(g_ref, rel, lr, li, (zero, zero), span, backward)
    summary_ref[:, :states] = re
    summary_ref[:, states:] = im


def turn_body(
    k, plan, span, exch, lens_ref, v_ref, x_ref, cot_ref, stats_ref, bias_ref,
    decay_ref, w_out_ref, skip_ref, w_glu_ref,
    out_ref, h_ref, act_ref, dz_ref, dy_ref, g_ref, summary_ref, buffers,
):
    seqs = lens_ref.shape[0]
    width = x_ref.shape[1]
    states = decay_ref.shape[-1]
    rel = relative(lens_ref, span, states)
    rebuild_states(k, plan, span, True, exch, buffers, rel, v_ref, decay_ref, h_ref)
    mean, scale = stats_ref[0:1, :], stats_ref[3:4, :]
    bias, skip = bias_ref[k : k + 1, :], skip_ref[k : k + 1, :]
    step = CHUNK * seqs
    for r in range(0, span * seqs, step):
        t0 = r // seqs
        x = x_ref[r : r + step, :]
        u = (x - mean) * scale + bias
        y = dot(h_ref[r : r + step, :], w_out_ref[k]) + skip * u
        act, slope = gelu_parts(y)
        act = act.astype(BF16)
        act_ref[r : r + step, :] = act
        z = dot(act, w_glu_ref[k])
        value, gate = z[:, :width], sigmoid(z[:, width:])
        gated = value * gate
        out_ref[:, t0 : t0 + CHUNK, :] = from_time_major(x + gated, seqs)
        d = to_time_major(cot_ref[:, t0 : t0 + CHUNK, :])
        back_rows(
            k, r, step, d * gate, d * (gated * (1.0 - gate)), slope, width,
            w_glu_ref, w_out_ref, dz_ref, dy_ref, g_ref,
        )
    local_adjoint(k, span, False, rel, g_ref, decay_ref, summary_ref)


def back_body(
    k, span, backward, lens_ref, sums_ref, part_ref, x_ref, mask_ref, stats_ref, slope_ref,
    gate_ref, value_ref, gain_ref, decay_ref, w_out_ref, w_glu_ref,
    d_ref, dz_ref, dy_ref, g_ref, grads_ref, summary_ref,
):
    seqs = lens_ref.shape[0]
    width = x_ref.shape[1]
    states = decay_ref.shape[-1]
    rel = relative(lens_ref, span, states)
    bias_grad, gain_grad = gathered(sums_ref)
    grads_ref[0:1, :] = gain_grad
    grads_ref[1:2, :] = bias_grad
    shift, tilt = input_terms(
        k + 1, token_scale(lens_ref), bias_grad, gain_grad, stats_ref, gain_ref
    )
    mean = stats_ref[0:1, :]
    step = CHUNK * seqs
    for r in range(0, span * seqs, step):
        live = lane_tiled(mask_ref[r : r + step, :], width)
        d = part_ref[r : r + step, :] + live * (shift + tilt * (x_ref[r : r + step, :] - mean))
        d_ref[r : r + step, :] = d
        back_rows(
            k, r, step, d * gate_ref[r : r + step, :].astype(F32),
            d * value_ref[r : r + step, :].astype(F32), slope_ref[r : r + step, :].astype(F32), width,
            w_glu_ref, w_out_ref, dz_ref, dy_ref, g_ref,
        )
    local_adjoint(k, span, backward, rel, g_ref, decay_ref, summary_ref)


def input_terms(k, scale, bias_grad, gain_grad, stats_ref, gain_ref):
    rstd = stats_ref[2:3, :]
    gain = gain_ref[k : k + 1, :]
    return -rstd * gain * bias_grad * scale, -rstd * rstd * gain * gain_grad * scale


def adjoint_body(
    k, plan, span, backward, exch, lens_ref, g_ref, h_ref, v_ref, decay_ref, dv_ref, small_ref, buffers
):
    seqs = lens_ref.shape[0]
    states = decay_ref.shape[-1]
    rel = relative(lens_ref, span, states)
    lr, li, gamma = (wide(decay_ref.at[k], row, rel.shape) for row in range(3))
    start = entering_state(k, plan, exch, buffers, backward, True)
    before = 0 if backward else 1

    def use(t, ar, ai, live, kept):
        ar, ai = jnp.where(live, ar, 0.0), jnp.where(live, ai, 0.0)
        dv_ref[at(t, seqs), :states] = (ar * gamma).astype(BF16)
        dv_ref[at(t, seqs), states:] = (ai * gamma).astype(BF16)
        pr = h_ref[at(t + before, seqs), :states].astype(F32)
        pi = h_ref[at(t + before, seqs), states:].astype(F32)
        vr, vi = v_ref[at(t, seqs), :states], v_ref[at(t, seqs), states:]
        return (
            kept[0] + (ar * pr + ai * pi),
            kept[1] + (ai * pr - ar * pi),
            kept[2] + (ar * vr + ai * vi),
        )

    zero = jnp.zeros(rel.shape, F32)
    _, kept = adjoint_scan(g_ref, rel, lr, li, start, span, backward, use, (zero, zero, zero))
    small_ref[...] = jnp.zeros_like(small_ref)
    for j in range(2):
        small_ref[0:1, j * states : (j + 1) * states] = jnp.sum(kept[j], 0, keepdims=True)
    small_ref[1:2, :states] = jnp.sum(kept[2], 0, keepdims=True)


def input_body(
    k, seqs, seq_major, dv_ref, dy_ref, x_ref, d_ref, stats_ref, gain_ref, bias_ref, w_in_ref, skip_ref,
    part_ref, skip_grad_ref, sums_ref,
):
    width = x_ref.shape[1]
    mean, scale, rstd = stats_ref[0:1, :], stats_ref[3:4, :], stats_ref[2:3, :]
    gain, bias, skip = (ref[k : k + 1, :] for ref in (gain_ref, bias_ref, skip_ref))
    step = CHUNK * seqs
    first = jnp.zeros((8, width), F32)
    second = jnp.zeros((8, width), F32)
    third = jnp.zeros((8, width), F32)
    for r in range(0, x_ref.shape[0], step):
        xhat = (x_ref[r : r + step, :] - mean) * rstd
        dy = dy_ref[r : r + step, :].astype(F32)
        du = dot_nt(dv_ref[r : r + step, :], w_in_ref[k]) + dy * skip
        first += jnp.sum(du.reshape(-1, 8, width), 0)
        second += jnp.sum((du * xhat).reshape(-1, 8, width), 0)
        third += jnp.sum((dy * (xhat * gain + bias)).reshape(-1, 8, width), 0)
        if seq_major:
            d = to_time_major(d_ref[:, r // seqs : r // seqs + CHUNK, :])
        else:
            d = d_ref[r : r + step, :]
        part_ref[r : r + step, :] = d + du * scale
    skip_grad_ref[...] = third
    if seq_major:
        spread(sums_ref, jnp.sum(first, 0, keepdims=True), jnp.sum(second, 0, keepdims=True))
    else:
        sums_ref[0] = first
        sums_ref[1] = second


def small_body(small0, skip0, sums0, small1, skip1, out):
    out[...] = jnp.zeros_like(out)
    rows = [small0[0:1, :], small0[1:2, :], skip0[...], sums0[0], sums0[1]]
    for row, value in enumerate(rows):
        out[row : row + 1, :] = jnp.sum(value, 0, keepdims=True)
    for row, value in enumerate([small1[0:1, :], small1[1:2, :], skip1[...]]):
        out[8 + row : 9 + row, :] = jnp.sum(value, 0, keepdims=True)


def finish_body(
    span, total_ref, lens_ref, part_ref, x_ref, mask_ref, gain_ref, decay_ref, running_ref, stats0_ref,
    stats1_ref, grads_ref, out_ref, g_gain_ref, g_bias_ref, nu_ref, phase_ref, skip_ref, run_ref,
):
    stats_refs = (stats0_ref, stats1_ref)
    small = total_ref[total_ref.shape[0] - 16 :, :]
    states = decay_ref.shape[-1]
    count = jnp.sum(lens_ref[:, 0:1].astype(F32), axis=0, keepdims=True)
    for k in range(2):
        _, _, gamma, rate, radius, cosine, sine = (decay_ref[k, j : j + 1, :] for j in range(7))
        sum_re, sum_im = small[8 * k : 8 * k + 1, :states], small[8 * k : 8 * k + 1, states:]
        g_gamma = small[8 * k + 1 : 8 * k + 2, :states]
        nu_ref[k : k + 1, :] = (sum_re * cosine + sum_im * sine) * (
            -radius * rate
        ) + g_gamma * rate * radius * radius / gamma
        phase_ref[k : k + 1, :] = radius * (sum_im * cosine - sum_re * sine)
        skip_ref[k : k + 1, :] = small[8 * k + 2 : 8 * k + 3, :]
        mean, var = stats_refs[k][0:1, :], stats_refs[k][1:2, :]
        run_ref[k, 0:1, :] = (1.0 - momentum) * running_ref[k, 0:1, :] + momentum * mean
        run_ref[k, 1:2, :] = (1.0 - momentum) * running_ref[k, 1:2, :] + momentum * var * (
            count / (count - 1.0)
        )
    bias_grad, gain_grad = small[3:4, :], small[4:5, :]
    g_gain_ref[0:1, :], g_gain_ref[1:2, :] = gain_grad, grads_ref[0:1, :]
    g_bias_ref[0:1, :], g_bias_ref[1:2, :] = bias_grad, grads_ref[1:2, :]
    seqs = out_ref.shape[0]
    width = x_ref.shape[1]
    shift, tilt = input_terms(0, 1.0 / count, bias_grad, gain_grad, stats_refs[0], gain_ref)
    mean = stats_refs[0][0:1, :]
    step = CHUNK * seqs
    for r in range(0, span * seqs, step):
        live = lane_tiled(mask_ref[r : r + step, :], width)
        d = part_ref[r : r + step, :] + live * (shift + tilt * (x_ref[r : r + step, :] - mean))
        out_ref[:, r // seqs : r // seqs + CHUNK, :] = from_time_major(d, seqs)


def with_entry(body, plan):
    def wrapped(*refs):
        n_exch = sum(radix for radix, _ in plan) + len(plan)
        body(refs[:n_exch], *refs[n_exch : -len(plan)], refs[-len(plan) :])

    return wrapped


def shards(
    inputs, lengths, cotangent, bn_gain, bn_bias, running, w_in, nu_log, phase, w_out, skip, w_glu
):
    seqs, span, width = inputs.shape
    states = nu_log.shape[1]
    count = lax.axis_size("tm")
    rows = span * seqs
    plan = stages(count)

    tile = ((count, 2 * width // LANES, LANES), F32)
    whole, whole_low = ((rows, width), F32), ((rows, width), BF16)
    pair, pair_low = ((rows, 2 * states), F32), ((rows, 2 * states), BF16)
    double_low = ((rows, 2 * width), BF16)
    held_low = ((rows + seqs, 2 * states), BF16)
    summary = ((seqs, 2 * states), F32)
    eight = ((8, width), F32)
    seq_major = ((seqs, span, width), F32)
    buffers = entry_scratch(plan, summary[0])

    in_hbm = pl.BlockSpec(memory_space=pltpu.HBM)
    outs = [((seqs, LANES), jnp.int32), tile, whole, ((rows, LANES), F32), ((2, 8, states), F32)]
    outs += [((2, radix) + summary[0], F32) for radix, _ in plan]
    prepared = pl.pallas_call(
        functools.partial(prepare_body, plan, span),
        out_shape=[jax.ShapeDtypeStruct(shape, dtype) for shape, dtype in outs],
        in_specs=[in_hbm] * 4,
        out_specs=[pl.BlockSpec(memory_space=pltpu.VMEM)] * len(outs),
        scratch_shapes=[
            pltpu.SMEM(lengths.shape, jnp.int32),
            pltpu.VMEM(inputs.shape, F32),
            pltpu.VMEM(nu_log.shape, F32),
            pltpu.VMEM(phase.shape, F32),
            pltpu.SemaphoreType.DMA((span // PIECE + 3,)),
        ],
        compiler_params=pltpu.CompilerParams(vmem_limit_bytes=24 * MIB),
    )(*(pltpu.with_memory_space_constraint(a, pltpu.HBM) for a in (lengths, inputs, nu_log, phase)))
    lens, sums, x0, mask, decay = prepared[:5]
    factors = prepared[5:]

    def project(k, sums, x):
        return run(
            functools.partial(project_body, k, span, k == 1),
            [whole_low, pair, eight, summary],
            [lens, everywhere(sums), x, bn_gain, bn_bias, w_in, decay],
        )

    def entered(body, outs, held, operands, after=(), limit=24, weight=1 << 33):
        operands = entry_operands(held, factors) + operands
        return run(with_entry(body, plan), outs, operands, after, buffers, limit, weight)

    u0, v0, stats0, part = project(0, sums, x0)
    held = exchange(0, part, plan, factors, False, False)
    x1, h0, act0, slope0, gate0, value0, sums = entered(
        functools.partial(forward_body, 0, plan, span),
        [whole, held_low, whole_low, whole_low, whole_low, whole_low, tile],
        held,
        [lens, v0, x0, mask, stats0, bn_bias, decay, w_out, skip, w_glu],
    )
    u1, v1, stats1, part = project(1, sums, x1)
    held = exchange(1, part, plan, factors, True, False)
    output, h1, act1, dz1, dy1, g1, part = entered(
        functools.partial(turn_body, 1, plan, span),
        [seq_major, held_low, whole_low, double_low, whole_low, pair, summary],
        held,
        [lens, v1, x1, cotangent, stats1, bn_bias, decay, w_out, skip, w_glu],
    )

    flows = {}
    flows["top"] = Bulk(
        count, [act1, h1], [dz1, dy1], [(0, 0, 0, 0), (0, 0, 0, width), (1, 0, 1, 0)], [part]
    )
    flows["top"].send()

    def beside_top(level, group):
        if level == 0:
            return flows["top"].parts[-1:]
        if level == len(plan) - 1:
            flows["step"] = flows["top"].send(group)
        return ()

    held = exchange(1, part, plan, factors, False, True, beside_top)
    top = flows["top"]
    dv1, small1 = entered(
        functools.partial(adjoint_body, 1, plan, span, False),
        [pair_low, eight],
        held,
        [lens, g1, h1, v1, decay],
        [flows["step"]],
        weight=1 << 20,
    )
    part1, skip1, sums = run(
        functools.partial(input_body, 1, seqs, True),
        [whole, eight, tile],
        [dv1, dy1, x1, cotangent, stats1, bn_gain, bn_bias, w_in, skip],
        weight=1 << 20,
    )
    step = top.send([sums])
    (sums,) = run(join_body, [tile], [sums], [step], limit=4)
    sums = everywhere(sums)
    step = top.send([sums])
    d0, dz0, dy0, g0, grads1, part = run(
        functools.partial(back_body, 0, span, True),
        [whole, double_low, whole_low, pair, eight, summary],
        [lens, sums, part1, x1, mask, stats1, slope0, gate0, value0, bn_gain, decay, w_out, w_glu],
        [step],
    )

    flows["middle"] = Bulk(
        count, [act0], [dz0], [(0, 0, 0, 0), (0, 0, 0, width)], [part]
    )
    flows["middle"].send()

    def beside_middle(level, group):
        if level == 0:
            return flows["middle"].parts[-1:]
        if level == len(plan) - 2:
            return [top.send(group[1:2])]
        if level == len(plan) - 1:
            flows["step"] = flows["middle"].send(group)
        return ()

    held = exchange(0, part, plan, factors, True, True, beside_middle)
    middle = flows["middle"]
    other = Bulk(
        count, [u1, h0], [dv1, dy0], [(0, 0, 0, 0), (1, seqs, 1, 0)], [held[-1][1]], weight=1 << 20
    )
    other.send()
    dv0, small0 = entered(
        functools.partial(adjoint_body, 0, plan, span, True),
        [pair_low, eight],
        held,
        [lens, g0, h0, v0, decay],
        [flows["step"], other.parts[-1]],
        weight=1 << 20,
    )
    part0, skip0, sums = run(
        functools.partial(input_body, 0, seqs, False),
        [whole, eight, ((2, 8, width), F32)],
        [dv0, dy0, x0, d0, stats0, bn_gain, bn_bias, w_in, skip],
        weight=1 << 20,
    )

    (small,) = run(small_body, [((16, width), F32)], [small0, skip0, sums, small1, skip1], limit=4)
    step = top.settle([part0])
    top.fetch()
    step = other.send([step])
    step = middle.send([step])
    step = top.fetch([step])
    last = Bulk(count, [u0], [dv0], [(0, 0, 0, 0)], [step], [small], weight=1 << 20)
    last.send()
    step = last.parts[-1]
    step = other.send([step])
    step = middle.send([step])
    step = last.send([step])
    step = other.send([step])
    step = top.fetch([step])
    step = middle.send([step])
    step = last.send([step])
    step = other.send([step])
    step = middle.settle([step])
    middle.fetch()
    step = last.send([step])
    step = other.settle([step])
    other.fetch()
    step = top.fetch([step])
    step = middle.fetch([step])
    step = last.send([step])
    step = other.fetch([step])
    step = middle.fetch([step])
    step = last.settle([step])
    last.fetch()
    step = other.fetch([step])
    step = last.fetch([step])
    step = middle.fetch([step])
    step = last.fetch([step])
    grad_x, g_gain, g_bias, g_nu, g_phase, g_skip, running_out = run(
        functools.partial(finish_body, span),
        [seq_major] + [((2, width), F32)] * 2 + [((2, states), F32)] * 2
        + [((2, width), F32), ((2, 2, width), F32)],
        [last.total, lens, part0, x0, mask, bn_gain, decay, running, stats0, stats1, grads1],
        [step],
    )
    step = other.fetch([g_gain])
    step = top.fetch([step])
    step = last.fetch([step])
    step = middle.fetch([step])
    step = other.fetch([step])
    step = last.fetch([step])
    g_glu, g_out, g_in = unpack(
        count,
        [top, middle, other, last],
        [
            [(0, 1, 0), (0, 1, width), (1, 1, 0)],
            [(0, 0, 0), (0, 0, width)],
            [(2, 1, 0), (1, 0, 0)],
            [(2, 0, 0)],
        ],
        [(2, width, 2 * width), (2, 2 * states, width), (2, width, 2 * states)],
    )
    return (output, grad_x, g_gain, g_bias, g_in, g_nu, g_phase, g_out, g_skip, g_glu, running_out)


def solution(mesh):
    placed = (P(None, "tm", None), P(), P(None, "tm", None)) + (P(),) * 9
    return jax.shard_map(
        shards,
        mesh=mesh,
        in_specs=placed,
        out_specs=(P(None, "tm", None),) * 2 + (P(),) * 9,
        check_vma=False,
    )
```

```python
import functools
import math

import jax
import jax.numpy as jnp
from jax import lax
from jax.experimental import pallas as pl
from jax.experimental.pallas import tpu as pltpu
from jax.sharding import PartitionSpec as P

norm_epsilon = 1e-05
momentum = 0.1
inverse_root_two = 0.7071067811865476
density_scale = 0.3989422804014327
F32, BF16 = jnp.float32, jnp.bfloat16
LANES = 128
MIB = 1 << 20


def dot(left, right):
    return jnp.dot(left, right, preferred_element_type=F32)


def dot_tn(left, right):
    return lax.dot_general(left, right, (((0,), (0,)), ((), ())), preferred_element_type=F32)


def dot_nt(left, right):
    return lax.dot_general(left, right, (((1,), (1,)), ((), ())), preferred_element_type=F32)


def run(body, outs, operands, after=(), scratch=(), limit=24, weight=1 << 33):
    vmem = pl.BlockSpec(memory_space=pltpu.VMEM)
    anywhere = pl.BlockSpec(memory_space=pl.ANY)
    first, second = len(operands), len(operands) + len(after)

    def kernel(*refs):
        body(*refs[:first], *refs[second:])

    return pl.pallas_call(
        kernel,
        out_shape=[jax.ShapeDtypeStruct(shape, dtype) for shape, dtype in outs],
        in_specs=[vmem] * len(operands) + [anywhere] * len(after),
        out_specs=[vmem] * len(outs),
        scratch_shapes=list(scratch),
        compiler_params=pltpu.CompilerParams(vmem_limit_bytes=limit * MIB),
        cost_estimate=pl.CostEstimate(flops=weight, bytes_accessed=0, transcendentals=0),
    )(*operands, *after)


def radices(count):
    out = []
    while count > 1:
        radix = 2 if not out or count % 4 else 4
        out.append(radix)
        count //= radix
    return out


def stages(count):
    stride, out = 1, []
    for radix in radices(count):
        out.append((radix, stride))
        stride *= radix
    return out


def swap(value, stride, mask):
    count = lax.axis_size("tm")
    return lax.ppermute(value, "tm", [(i, i ^ (stride * mask)) for i in range(count)])


def group_of(value, radix, stride):
    return [value] + [swap(value, stride, mask) for mask in range(1, radix)]


def place_in(radix, stride):
    return lax.rem(lax.div(lax.axis_index("tm"), stride), radix)


def rows_to_tile(first, second):
    pieces = [
        row[:, j : j + LANES] for row in (first, second) for j in range(0, row.shape[1], LANES)
    ]
    return jnp.concatenate(pieces, axis=0)


def tile_to_rows(tile):
    half = tile.shape[0] // 2
    return [
        jnp.concatenate([tile[base + j : base + j + 1, :] for j in range(half)], axis=1)
        for base in (0, half)
    ]


def spread(ref, first, second):
    ref[...] = jnp.broadcast_to(rows_to_tile(first, second)[None], ref.shape)


def gathered(ref):
    return tile_to_rows(jnp.sum(ref[...], axis=0))


def everywhere(tiles):
    return lax.all_to_all(tiles, "tm", 0, 0)


def mul(ar, ai, br, bi):
    return ar * br - ai * bi, ar * bi + ai * br


def members(refs, place, buffer):
    for offset, ref in enumerate(refs):
        buffer[jnp.bitwise_xor(place, offset)] = ref[...]


def pass_through(k, buffer, factor, place, state, backward, conj):
    radix, _, width = buffer.shape
    states = width // 2
    if state is None:
        zero = jnp.zeros(buffer.shape[1:-1] + (states,), F32)
        state = (zero, zero)
    entering = state
    for member in range(radix - 1, -1, -1) if backward else range(radix):
        entering = tuple(jnp.where(place == member, s, e) for s, e in zip(state, entering))
        fr, fi = factor[k, member, :, :states], factor[k, member, :, states:]
        moved = mul(fr, -fi if conj else fi, *state)
        state = (moved[0] + buffer[member, :, :states], moved[1] + buffer[member, :, states:])
    return entering, state


def total_body(k, radix, stride, backward, conj, *refs):
    factor, out, buffer = refs[radix:]
    place = place_in(radix, stride)
    members(refs[:radix], place, buffer)
    _, (re, im) = pass_through(k, buffer, factor, place, None, backward, conj)
    states = re.shape[1]
    out[:, :states] = re
    out[:, states:] = im


def group_total(k, group, level, plan, factors, backward, conj, after=()):
    radix, stride = plan[level]
    shape = group[0].shape
    (total,) = run(
        functools.partial(total_body, k, radix, stride, backward, conj),
        [(shape, F32)],
        list(group) + [factors[level]],
        after,
        [pltpu.VMEM((radix,) + shape, F32)],
        limit=4,
    )
    return total


def exchange(k, summary, plan, factors, backward, conj, between=None):
    held = []
    value = summary
    for level, (radix, stride) in enumerate(plan):
        group = group_of(value, radix, stride)
        held.append(group)
        if level + 1 < len(plan):
            after = between(level, group) if between else ()
            value = group_total(k, group, level, plan, factors, backward, conj, after)
            if between and level + 2 == len(plan):
                between(level + 1, [value])
    return held


def entry_operands(held, factors):
    return [value for group in held for value in group] + list(factors)


def entry_scratch(plan, shape):
    return [pltpu.VMEM((radix,) + shape, F32) for radix, _ in plan]


def entering_state(k, plan, refs, buffers, backward, conj):
    total = sum(radix for radix, _ in plan)
    values, factors = refs[:total], refs[total:]
    start, groups = 0, []
    for radix, _ in plan:
        groups.append(values[start : start + radix])
        start += radix
    state = None
    for level in range(len(plan) - 1, -1, -1):
        place = place_in(*plan[level])
        members(groups[level], place, buffers[level])
        state, _ = pass_through(k, buffers[level], factors[level], place, state, backward, conj)
    return state


CHUNKS = 32
LEVELS = CHUNKS.bit_length() - 1


def partners(count):
    order = [(1 << b, 1 << b) for b in range(count.bit_length() - 1)]
    if len(order) > 2:
        order[1], order[2] = (2, 4), (4, 2)
    return order


def with_partner(value, bits):
    even, odd = bits
    count = lax.axis_size("tm")
    return lax.ppermute(value, "tm", [(i, i ^ (odd if i & 1 else even)) for i in range(count)])


def own_chunk(count, other_core=False):
    here = lax.axis_index("tm")
    if other_core:
        here = jnp.bitwise_xor(here, 1)
    own = 0
    for even, odd in partners(count)[:LEVELS]:
        taken = jnp.where(jnp.bitwise_and(here, 1) == 1, here & odd, here & even)
        own = own * 2 + jnp.where(taken != 0, 1, 0)
    return own


def slots(level):
    return (CHUNKS >> (level + 1), CHUNKS >> level) if level < LEVELS else (0, 1)


def outer_body(count, pairs, n_left, n_right, n_extra, *refs):
    lefts, rights = refs[:n_left], refs[n_left : n_left + n_right]
    extra, outs = refs[n_left + n_right :][:n_extra], refs[n_left + n_right + n_extra : -len(pairs)]
    products = refs[-len(pairs) :]
    if extra:
        outs[0][-extra[0].shape[0] :, :] = extra[0][...]
    owns = own_chunk(count), own_chunk(count, True)
    half = CHUNKS // 2
    for q, (left, row, right, column) in enumerate(pairs):
        product = products[q]
        span = rights[right].shape[0]
        wide_left = lefts[left].shape[1]
        part = wide_left // CHUNKS
        width = product.shape[1]
        product[...] = dot_tn(
            lefts[left][row : row + span, :], rights[right][:, column : column + width]
        )
        for level in range(LEVELS + 1):
            low, high = slots(level)
            for slot in range(low, high):
                chunk = jnp.bitwise_xor(owns[slot // half], slot % half)
                chunk = pl.multiple_of(chunk * part, part)
                place = ((slot - low) * len(pairs) + q) * part
                outs[level][place : place + part, :] = product[pl.ds(chunk, part), :]


def add_body(low, extra, *refs):
    out = refs[-1]
    rows = out.shape[0] - extra
    total = refs[0][:rows, :]
    for ref in refs[1 : -2 if extra else -1]:
        total += ref[low : low + rows, :]
    out[:rows, :] = total
    if extra:
        mine, other = refs[-2], refs[-3]
        out[rows:, :] = mine[-extra:, :] + other[-extra:, :]


def spokes_body(rows, extra, *refs):
    near, far = refs[:2]
    received, mine, outs = refs[2:-4], refs[-4], refs[-3:]
    for slot, out in enumerate(outs, 1):
        total = near[...] if slot == 1 else far[(slot - 2) * rows : (slot - 1) * rows, :]
        for ref in received:
            total += ref[slot * rows : (slot + 1) * rows, :]
        out[:rows, :] = total
        if extra:
            out[rows:, :] = mine[-extra:, :] + received[-1][-extra:, :]


def hub_body(rows, extra, *refs):
    kept, received, mine, spokes, out = refs[0], refs[1:-5], refs[-5], refs[-4:-1], refs[-1]
    total = kept[...]
    for ref in received + spokes:
        total += ref[:rows, :]
    out[:rows, :] = total
    if extra:
        total = mine[-extra:, :]
        for ref in spokes:
            total += ref[-extra:, :]
        out[rows:, :] = total


def join_body(*refs):
    out = refs[-1]
    rows = refs[0].shape[0]
    for j, ref in enumerate(refs[:-1]):
        out[j * rows : (j + 1) * rows] = ref[...]


class Bulk:
    def __init__(self, count, lefts, rights, pairs, after=(), extra=(), hub=False, weight=1 << 33):
        self.hub = hub
        self.bits = partners(count)
        self.extra = extra[0].shape[0] if extra else 0
        width = 512
        part = lefts[0].shape[1] // CHUNKS
        self.rows = part * len(pairs)
        outs = [((self.rows * (hi - lo), width), F32) for lo, hi in map(slots, range(LEVELS + 1))]
        outs[0] = ((outs[0][0][0] + self.extra, width), F32)
        self.parts = run(
            functools.partial(outer_body, count, pairs, len(lefts), len(rights), len(extra)),
            outs,
            list(lefts) + list(rights) + list(extra),
            after,
            [pltpu.VMEM((lefts[pair[0]].shape[1], width), F32) for pair in pairs],
            limit=16,
            weight=weight,
        )
        self.received = []
        self.sent = None

    def reduced(self, level, after=()):
        low, high = slots(level)
        if not self.received:
            return self.parts[level]
        (total,) = run(
            functools.partial(add_body, low * self.rows, self.extra),
            [((self.rows * (high - low) + self.extra, self.parts[level].shape[1]), F32)],
            [self.parts[level]] + self.received + ([self.sent] if self.extra else []),
            after,
            limit=8,
        )
        return total

    def send(self, after=()):
        level = len(self.received)
        if self.hub and level == LEVELS - 2:
            shape = (self.rows + self.extra, self.parts[LEVELS].shape[1])
            sent = run(
                functools.partial(spokes_body, self.rows, self.extra),
                [(shape, F32)] * 3,
                [self.parts[LEVELS - 1], self.parts[LEVELS - 2]] + self.received + [self.sent],
                after,
                limit=8,
            )
            self.sent, self.spokes = sent[0], self.with_partners(sent)
            return self.sent
        self.sent = self.reduced(level, after)
        self.received.append(with_partner(self.sent, self.bits[level]))
        return self.sent

    def with_partners(self, values):
        far, near = self.bits[LEVELS - 2][0], self.bits[LEVELS - 1][0]
        masks = (near, far, near | far)
        return [swap(value, 1, mask) for value, mask in zip(values, masks)]

    def settle(self, after=()):
        if self.hub:
            (value,) = run(
                functools.partial(hub_body, self.rows, self.extra),
                [((self.rows + self.extra, self.parts[LEVELS].shape[1]), F32)],
                [self.parts[LEVELS]] + self.received + [self.sent] + self.spokes,
                after,
                limit=8,
            )
        else:
            value = self.reduced(LEVELS, after)
        for even, odd in self.bits[LEVELS:]:
            other = with_partner(value, (even, odd))
            (value,) = run(
                functools.partial(add_body, 0, 0), [(value.shape, F32)], [value, other], limit=4
            )
        self.total, self.value, self.level = value, value[: self.rows], LEVELS - 1
        return value

    def fetch(self, after=()):
        if self.level < LEVELS - 1:
            parts = [self.value] + self.others
            (self.value,) = run(
                join_body,
                [((len(parts) * self.value.shape[0], self.value.shape[1]), F32)],
                parts,
                after,
                limit=8,
            )
        if self.hub and self.level == LEVELS - 1:
            self.others = self.with_partners([self.value] * 3)
            self.level -= 2
        else:
            self.others = [with_partner(self.value, self.bits[self.level])]
            self.level -= 1
        return self.value


def unpack_body(count, width, layout, n_into, *refs):
    outs, sem = refs[2 * len(layout) + n_into : -1], refs[-1]
    owns = own_chunk(count), own_chunk(count, True)
    copies = []
    for piece, places in enumerate(layout):
        near, far = refs[2 * piece], refs[2 * piece + 1]
        for source, own in zip((near, far), owns):
            for j in range(CHUNKS // 2):
                chunk = jnp.bitwise_xor(own, j)
                part = source.shape[0] // (CHUNKS // 2) // len(places)
                for q, (out, k, column) in enumerate(places):
                    place = (j * len(places) + q) * part
                    rows = pl.ds(pl.multiple_of(chunk * part, part), part)
                    copies.append(
                        pltpu.make_async_copy(
                            source.at[pl.ds(place, part), :],
                            outs[out].at[k, rows, pl.ds(column, width)],
                            sem,
                        )
                    )
    for copy in copies:
        copy.start()
    for copy in copies:
        copy.wait()


def unpack(count, bulks, layout, shapes, into=()):
    operands = [value for bulk in bulks for value in (bulk.value, bulk.others[0])]
    anywhere = pl.BlockSpec(memory_space=pl.ANY)
    return pl.pallas_call(
        functools.partial(unpack_body, count, operands[0].shape[1], layout, len(into)),
        out_shape=[jax.ShapeDtypeStruct(shape, F32) for shape in shapes],
        in_specs=[anywhere] * (len(operands) + len(into)),
        out_specs=[anywhere] * len(shapes),
        scratch_shapes=[pltpu.SemaphoreType.DMA],
        input_output_aliases={len(operands) + j: j for j in range(len(into))},
        compiler_params=pltpu.CompilerParams(vmem_limit_bytes=4 * MIB),
    )(*operands, *into)


def steps(span, backward, body, start, unroll=8):
    def one(k, carry):
        return body(span - 1 - k if backward else k, carry)

    return lax.fori_loop(0, span, one, start, unroll=unroll)


def at(t, seqs):
    return pl.ds(pl.multiple_of(t * seqs, seqs), seqs)


def state_scan(v_ref, rel, lr, li, start, span, backward, keep=None):
    seqs, states = lr.shape

    def body(t, carry):
        re, im = carry
        vr, vi = v_ref[at(t, seqs), :states], v_ref[at(t, seqs), states:]
        next_re, next_im = mul(lr, li, re, im)
        live = rel > t
        re, im = jnp.where(live, next_re + vr, re), jnp.where(live, next_im + vi, im)
        if keep is not None:
            keep(t, re, im)
        return re, im

    return steps(span, backward, body, start)


def adjoint_scan(g_ref, rel, lr, li, start, span, backward, use=None, extra=()):
    seqs, states = lr.shape

    def body(t, carry):
        (re, im), kept = carry
        ar, ai = g_ref[at(t, seqs), :states] + re, g_ref[at(t, seqs), states:] + im
        live = rel > t
        if use is not None:
            kept = use(t, ar, ai, live, kept)
        next_re, next_im = mul(lr, -li, ar, ai)
        return (jnp.where(live, next_re, ar), jnp.where(live, next_im, ai)), kept

    return steps(span, backward, body, (start, extra))


def wide(ref, row, shape):
    return jnp.broadcast_to(ref[row : row + 1, :], shape)


def to_time_major(piece):
    seqs, span, width = piece.shape
    return jnp.swapaxes(piece, 0, 1).reshape(span * seqs, width)


def from_time_major(rows, seqs):
    return jnp.swapaxes(rows.reshape(-1, seqs, rows.shape[-1]), 0, 1)


def lane_tiled(column, width):
    return jnp.concatenate([column] * (width // LANES), axis=1)


def gelu_parts(y):
    cdf = 0.5 * (1.0 + lax.erf(y * inverse_root_two))
    pdf = jnp.exp(-0.5 * y * y) * density_scale
    return y * cdf, cdf + y * pdf


sigmoid = jax.nn.sigmoid


CHUNK = 64
PIECE = 8


def prepare_body(plan, span, lengths_any, x_any, nu_any, phase_any, *outs):
    lens_ref, sums_ref, tm_ref, mask_ref, decay_ref = outs[:5]
    factor_refs = outs[5 : 5 + len(plan)]
    lengths_ref, x_ref, nu_ref, phase_ref, sems = outs[5 + len(plan) :]
    seqs, _, width = x_ref.shape
    states = nu_ref.shape[-1]
    copies = [
        pltpu.make_async_copy(
            x_any.at[:, pl.ds(t0, PIECE), :], x_ref.at[:, pl.ds(t0, PIECE), :], sems.at[t0 // PIECE]
        )
        for t0 in range(0, span, PIECE)
    ]
    small = [
        pltpu.make_async_copy(nu_any, nu_ref, sems.at[len(copies)]),
        pltpu.make_async_copy(phase_any, phase_ref, sems.at[len(copies) + 1]),
        pltpu.make_async_copy(lengths_any, lengths_ref, sems.at[len(copies) + 2]),
    ]
    for copy in small + copies:
        copy.start()
    for copy in small:
        copy.wait()
    here = lax.axis_index("tm")
    row = lax.broadcasted_iota(jnp.int32, (seqs, LANES), 0)
    lens = jnp.zeros((seqs, LANES), jnp.int32)
    for seq in range(seqs):
        lens = jnp.where(row == seq, lengths_ref[seq], lens)
    lens_ref[...] = lens
    rel = lens - here * span
    rate = jnp.exp(nu_ref[...])
    radius = jnp.exp(-rate)
    angle = phase_ref[...]
    cosine, sine = jnp.cos(angle), jnp.sin(angle)
    gamma = jnp.sqrt(one_less_exp(2.0 * rate))
    for row, value in enumerate((radius * cosine, radius * sine, gamma, rate, radius, cosine, sine)):
        for k in range(2):
            decay_ref[k, row : row + 1, :] = value[k : k + 1, :]
    for k in range(2):
        for level, (radix, stride) in enumerate(plan):
            base = lax.div(here, radix * stride) * (radix * stride)
            for member in range(radix):
                start = (base + member * stride) * span
                count = jnp.concatenate(
                    [jnp.clip(lens - start, 0, stride * span)] * (states // LANES), axis=1
                )
                power = (decay_ref[k, 0:1, :], decay_ref[k, 1:2, :])
                re, im = jnp.ones((seqs, states), F32), jnp.zeros((seqs, states), F32)
                for bit in range((span * stride).bit_length()):
                    taken = jnp.bitwise_and(count, 1 << bit) != 0
                    next_re, next_im = mul(re, im, *power)
                    re, im = jnp.where(taken, next_re, re), jnp.where(taken, next_im, im)
                    power = mul(*power, *power)
                factor_refs[level][k, member, :, :states] = re
                factor_refs[level][k, member, :, states:] = im
    first = jnp.zeros((seqs, width), F32)
    second = jnp.zeros((seqs, width), F32)
    for t0 in range(0, span, PIECE):
        copies[t0 // PIECE].wait()
        piece = jnp.swapaxes(x_ref[:, t0 : t0 + PIECE, :], 0, 1)
        for j in range(PIECE):
            rows = piece[j]
            mask = jnp.where(rel > t0 + j, 1.0, 0.0)
            place = slice((t0 + j) * seqs, (t0 + j + 1) * seqs)
            mask_ref[place, :] = mask
            tm_ref[place, :] = rows
            live = rows * lane_tiled(mask, width)
            first += live
            second += live * rows
    spread(sums_ref, jnp.sum(first, 0, keepdims=True), jnp.sum(second, 0, keepdims=True))


def one_less_exp(x):
    total = 1.0
    for n in range(8, 1, -1):
        total = 1.0 - total * x * (1.0 / n)
    return total * x


def relative(lens_ref, span, states):
    rel = lens_ref[...] - lax.axis_index("tm") * span
    return jnp.concatenate([rel] * (states // LANES), axis=1)


def token_scale(lens_ref):
    return 1.0 / jnp.sum(lens_ref[:, 0:1].astype(F32), axis=0, keepdims=True)


def project_body(
    k, span, backward, lens_ref, sums_ref, x_ref, gain_ref, bias_ref, w_ref, decay_ref,
    u_ref, v_ref, stats_ref, summary_ref,
):
    seqs = lens_ref.shape[0]
    states = decay_ref.shape[-1]
    total, squares = gathered(sums_ref)
    scale = token_scale(lens_ref)
    mean = total * scale
    var = squares * scale - mean * mean
    rstd = lax.rsqrt(var + norm_epsilon)
    stats_ref[0:1, :] = mean
    stats_ref[1:2, :] = var
    stats_ref[2:3, :] = rstd
    stats_ref[3:4, :] = rstd * gain_ref[k : k + 1, :]
    slope = rstd * gain_ref[k : k + 1, :]
    bias = bias_ref[k : k + 1, :]
    step = CHUNK * seqs
    for r in range(0, span * seqs, step):
        u = ((x_ref[r : r + step, :] - mean) * slope + bias).astype(BF16)
        u_ref[r : r + step, :] = u
        v_ref[r : r + step, :] = dot(u, w_ref[k])
    shape = (seqs, states)
    rel = relative(lens_ref, span, states)
    lr, li = wide(decay_ref.at[k], 0, shape), wide(decay_ref.at[k], 1, shape)
    zero = jnp.zeros(shape, F32)
    re, im = state_scan(v_ref, rel, lr, li, (zero, zero), span, backward)
    summary_ref[:, :states] = re
    summary_ref[:, states:] = im


def rebuild_states(k, plan, span, backward, refs, buffers, rel, v_ref, decay_ref, h_ref):
    seqs, states = rel.shape
    lr, li, gamma = (wide(decay_ref.at[k], row, rel.shape) for row in range(3))
    start = entering_state(k, plan, refs, buffers, backward, False)

    lead = 0 if backward else 1

    def keep(t, re, im):
        h_ref[at(t + lead, seqs), :states] = (re * gamma).astype(BF16)
        h_ref[at(t + lead, seqs), states:] = (im * gamma).astype(BF16)

    keep(span if backward else -1, *start)
    state_scan(v_ref, rel, lr, li, start, span, backward, keep)


def forward_body(
    k, plan, span, exch, lens_ref, v_ref, x_ref, mask_ref, stats_ref, bias_ref,
    decay_ref, w_out_ref, skip_ref, w_glu_ref,
    out_ref, h_ref, act_ref, slope_ref, gate_ref, value_ref, sums_ref, buffers,
):
    seqs = lens_ref.shape[0]
    width = x_ref.shape[1]
    states = decay_ref.shape[-1]
    rel = relative(lens_ref, span, states)
    rebuild_states(k, plan, span, False, exch, buffers, rel, v_ref, decay_ref, h_ref)
    mean, scale = stats_ref[0:1, :], stats_ref[3:4, :]
    bias, skip = bias_ref[k : k + 1, :], skip_ref[k : k + 1, :]
    step = CHUNK * seqs
    first = jnp.zeros((8, width), F32)
    second = jnp.zeros((8, width), F32)
    for r in range(0, span * seqs, step):
        x = x_ref[r : r + step, :]
        u = (x - mean) * scale + bias
        y = dot(h_ref[r + seqs : r + seqs + step, :], w_out_ref[k]) + skip * u
        act, slope = gelu_parts(y)
        act = act.astype(BF16)
        act_ref[r : r + step, :] = act
        slope_ref[r : r + step, :] = slope.astype(BF16)
        z = dot(act, w_glu_ref[k])
        value, gate = z[:, :width], sigmoid(z[:, width:])
        gated = value * gate
        out = x + gated
        out_ref[r : r + step, :] = out
        gate_ref[r : r + step, :] = gate.astype(BF16)
        value_ref[r : r + step, :] = (gated * (1.0 - gate)).astype(BF16)
        live = out * lane_tiled(mask_ref[r : r + step, :], width)
        first += jnp.sum(live.reshape(-1, 8, width), 0)
        second += jnp.sum((live * out).reshape(-1, 8, width), 0)
    spread(sums_ref, jnp.sum(first, 0, keepdims=True), jnp.sum(second, 0, keepdims=True))


def back_rows(k, r, step, dza, dzb, slope, width, w_glu_ref, w_out_ref, dz_ref, dy_ref, g_ref):
    dza, dzb = dza.astype(BF16), dzb.astype(BF16)
    dz_ref[r : r + step, :width] = dza
    dz_ref[r : r + step, width:] = dzb
    w = w_glu_ref[k]
    dact = dot_nt(dza, w[:, :width]) + dot_nt(dzb, w[:, width:])
    dy = (dact * slope).astype(BF16)
    dy_ref[r : r + step, :] = dy
    g_ref[r : r + step, :] = dot_nt(dy, w_out_ref[k])


def local_adjoint(k, span, backward, rel, g_ref, decay_ref, summary_ref):
    seqs, states = rel.shape
    lr, li = wide(decay_ref.at[k], 0, rel.shape), wide(decay_ref.at[k], 1, rel.shape)
    zero = jnp.zeros(rel.shape, F32)
    (re, im), _ = adjoint_scan(g_ref, rel, lr, li, (zero, zero), span, backward)
    summary_ref[:, :states] = re
    summary_ref[:, states:] = im


def turn_body(
    k, plan, span, exch, lens_ref, v_ref, x_ref, cot_ref, stats_ref, bias_ref,
    decay_ref, w_out_ref, skip_ref, w_glu_ref,
    out_ref, h_ref, act_ref, dz_ref, dy_ref, g_ref, summary_ref, buffers,
):
    seqs = lens_ref.shape[0]
    width = x_ref.shape[1]
    states = decay_ref.shape[-1]
    rel = relative(lens_ref, span, states)
    rebuild_states(k, plan, span, True, exch, buffers, rel, v_ref, decay_ref, h_ref)
    mean, scale = stats_ref[0:1, :], stats_ref[3:4, :]
    bias, skip = bias_ref[k : k + 1, :], skip_ref[k : k + 1, :]
    step = CHUNK * seqs
    for r in range(0, span * seqs, step):
        t0 = r // seqs
        x = x_ref[r : r + step, :]
        u = (x - mean) * scale + bias
        y = dot(h_ref[r : r + step, :], w_out_ref[k]) + skip * u
        act, slope = gelu_parts(y)
        act = act.astype(BF16)
        act_ref[r : r + step, :] = act
        z = dot(act, w_glu_ref[k])
        value, gate = z[:, :width], sigmoid(z[:, width:])
        gated = value * gate
        out_ref[:, t0 : t0 + CHUNK, :] = from_time_major(x + gated, seqs)
        d = to_time_major(cot_ref[:, t0 : t0 + CHUNK, :])
        back_rows(
            k, r, step, d * gate, d * (gated * (1.0 - gate)), slope, width,
            w_glu_ref, w_out_ref, dz_ref, dy_ref, g_ref,
        )
    local_adjoint(k, span, False, rel, g_ref, decay_ref, summary_ref)


def back_body(
    k, span, backward, lens_ref, sums_ref, part_ref, x_ref, mask_ref, stats_ref, slope_ref,
    gate_ref, value_ref, gain_ref, decay_ref, w_out_ref, w_glu_ref,
    d_ref, dz_ref, dy_ref, g_ref, grads_ref, summary_ref,
):
    seqs = lens_ref.shape[0]
    width = x_ref.shape[1]
    states = decay_ref.shape[-1]
    rel = relative(lens_ref, span, states)
    bias_grad, gain_grad = gathered(sums_ref)
    grads_ref[0:1, :] = gain_grad
    grads_ref[1:2, :] = bias_grad
    shift, tilt = input_terms(
        k + 1, token_scale(lens_ref), bias_grad, gain_grad, stats_ref, gain_ref
    )
    mean = stats_ref[0:1, :]
    step = CHUNK * seqs
    for r in range(0, span * seqs, step):
        live = lane_tiled(mask_ref[r : r + step, :], width)
        d = part_ref[r : r + step, :] + live * (shift + tilt * (x_ref[r : r + step, :] - mean))
        d_ref[r : r + step, :] = d
        back_rows(
            k, r, step, d * gate_ref[r : r + step, :].astype(F32),
            d * value_ref[r : r + step, :].astype(F32), slope_ref[r : r + step, :].astype(F32), width,
            w_glu_ref, w_out_ref, dz_ref, dy_ref, g_ref,
        )
    local_adjoint(k, span, backward, rel, g_ref, decay_ref, summary_ref)


def input_terms(k, scale, bias_grad, gain_grad, stats_ref, gain_ref):
    rstd = stats_ref[2:3, :]
    gain = gain_ref[k : k + 1, :]
    return -rstd * gain * bias_grad * scale, -rstd * rstd * gain * gain_grad * scale


def adjoint_body(
    k, plan, span, backward, exch, lens_ref, g_ref, h_ref, v_ref, decay_ref, dv_ref, small_ref, buffers
):
    seqs = lens_ref.shape[0]
    states = decay_ref.shape[-1]
    rel = relative(lens_ref, span, states)
    lr, li, gamma = (wide(decay_ref.at[k], row, rel.shape) for row in range(3))
    start = entering_state(k, plan, exch, buffers, backward, True)
    before = 0 if backward else 1

    def use(t, ar, ai, live, kept):
        ar, ai = jnp.where(live, ar, 0.0), jnp.where(live, ai, 0.0)
        dv_ref[at(t, seqs), :states] = (ar * gamma).astype(BF16)
        dv_ref[at(t, seqs), states:] = (ai * gamma).astype(BF16)
        pr = h_ref[at(t + before, seqs), :states].astype(F32)
        pi = h_ref[at(t + before, seqs), states:].astype(F32)
        vr, vi = v_ref[at(t, seqs), :states], v_ref[at(t, seqs), states:]
        return (
            kept[0] + (ar * pr + ai * pi),
            kept[1] + (ai * pr - ar * pi),
            kept[2] + (ar * vr + ai * vi),
        )

    zero = jnp.zeros(rel.shape, F32)
    _, kept = adjoint_scan(g_ref, rel, lr, li, start, span, backward, use, (zero, zero, zero))
    small_ref[...] = jnp.zeros_like(small_ref)
    for j in range(2):
        small_ref[0:1, j * states : (j + 1) * states] = jnp.sum(kept[j], 0, keepdims=True)
    small_ref[1:2, :states] = jnp.sum(kept[2], 0, keepdims=True)


def input_body(
    k, seqs, seq_major, dv_ref, dy_ref, x_ref, d_ref, stats_ref, gain_ref, bias_ref, w_in_ref, skip_ref,
    part_ref, skip_grad_ref, sums_ref,
):
    width = x_ref.shape[1]
    mean, scale, rstd = stats_ref[0:1, :], stats_ref[3:4, :], stats_ref[2:3, :]
    gain, bias, skip = (ref[k : k + 1, :] for ref in (gain_ref, bias_ref, skip_ref))
    step = CHUNK * seqs
    first = jnp.zeros((8, width), F32)
    second = jnp.zeros((8, width), F32)
    third = jnp.zeros((8, width), F32)
    for r in range(0, x_ref.shape[0], step):
        xhat = (x_ref[r : r + step, :] - mean) * rstd
        dy = dy_ref[r : r + step, :].astype(F32)
        du = dot_nt(dv_ref[r : r + step, :], w_in_ref[k]) + dy * skip
        first += jnp.sum(du.reshape(-1, 8, width), 0)
        second += jnp.sum((du * xhat).reshape(-1, 8, width), 0)
        third += jnp.sum((dy * (xhat * gain + bias)).reshape(-1, 8, width), 0)
        if seq_major:
            d = to_time_major(d_ref[:, r // seqs : r // seqs + CHUNK, :])
        else:
            d = d_ref[r : r + step, :]
        part_ref[r : r + step, :] = d + du * scale
    skip_grad_ref[...] = third
    if seq_major:
        spread(sums_ref, jnp.sum(first, 0, keepdims=True), jnp.sum(second, 0, keepdims=True))
    else:
        sums_ref[0] = first
        sums_ref[1] = second


def small_body(small0, skip0, sums0, small1, skip1, out):
    out[...] = jnp.zeros_like(out)
    rows = [small0[0:1, :], small0[1:2, :], skip0[...], sums0[0], sums0[1]]
    for row, value in enumerate(rows):
        out[row : row + 1, :] = jnp.sum(value, 0, keepdims=True)
    for row, value in enumerate([small1[0:1, :], small1[1:2, :], skip1[...]]):
        out[8 + row : 9 + row, :] = jnp.sum(value, 0, keepdims=True)


def finish_body(
    span, total_ref, lens_ref, part_ref, x_ref, mask_ref, gain_ref, decay_ref, running_ref, stats0_ref,
    stats1_ref, grads_ref, out_ref, g_gain_ref, g_bias_ref, nu_ref, phase_ref, skip_ref, run_ref,
):
    stats_refs = (stats0_ref, stats1_ref)
    small = total_ref[total_ref.shape[0] - 16 :, :]
    states = decay_ref.shape[-1]
    count = jnp.sum(lens_ref[:, 0:1].astype(F32), axis=0, keepdims=True)
    for k in range(2):
        _, _, gamma, rate, radius, cosine, sine = (decay_ref[k, j : j + 1, :] for j in range(7))
        sum_re, sum_im = small[8 * k : 8 * k + 1, :states], small[8 * k : 8 * k + 1, states:]
        g_gamma = small[8 * k + 1 : 8 * k + 2, :states]
        nu_ref[k : k + 1, :] = (sum_re * cosine + sum_im * sine) * (
            -radius * rate
        ) + g_gamma * rate * radius * radius / gamma
        phase_ref[k : k + 1, :] = radius * (sum_im * cosine - sum_re * sine)
        skip_ref[k : k + 1, :] = small[8 * k + 2 : 8 * k + 3, :]
        mean, var = stats_refs[k][0:1, :], stats_refs[k][1:2, :]
        run_ref[k, 0:1, :] = (1.0 - momentum) * running_ref[k, 0:1, :] + momentum * mean
        run_ref[k, 1:2, :] = (1.0 - momentum) * running_ref[k, 1:2, :] + momentum * var * (
            count / (count - 1.0)
        )
    bias_grad, gain_grad = small[3:4, :], small[4:5, :]
    g_gain_ref[0:1, :], g_gain_ref[1:2, :] = gain_grad, grads_ref[0:1, :]
    g_bias_ref[0:1, :], g_bias_ref[1:2, :] = bias_grad, grads_ref[1:2, :]
    seqs = out_ref.shape[0]
    width = x_ref.shape[1]
    shift, tilt = input_terms(0, 1.0 / count, bias_grad, gain_grad, stats_refs[0], gain_ref)
    mean = stats_refs[0][0:1, :]
    step = CHUNK * seqs
    for r in range(0, span * seqs, step):
        live = lane_tiled(mask_ref[r : r + step, :], width)
        d = part_ref[r : r + step, :] + live * (shift + tilt * (x_ref[r : r + step, :] - mean))
        out_ref[:, r // seqs : r // seqs + CHUNK, :] = from_time_major(d, seqs)


def with_entry(body, plan):
    def wrapped(*refs):
        n_exch = sum(radix for radix, _ in plan) + len(plan)
        body(refs[:n_exch], *refs[n_exch : -len(plan)], refs[-len(plan) :])

    return wrapped


def shards(
    inputs, lengths, cotangent, bn_gain, bn_bias, running, w_in, nu_log, phase, w_out, skip, w_glu
):
    seqs, span, width = inputs.shape
    states = nu_log.shape[1]
    count = lax.axis_size("tm")
    rows = span * seqs
    plan = stages(count)

    tile = ((count, 2 * width // LANES, LANES), F32)
    whole, whole_low = ((rows, width), F32), ((rows, width), BF16)
    pair, pair_low = ((rows, 2 * states), F32), ((rows, 2 * states), BF16)
    double_low = ((rows, 2 * width), BF16)
    held_low = ((rows + seqs, 2 * states), BF16)
    summary = ((seqs, 2 * states), F32)
    eight = ((8, width), F32)
    seq_major = ((seqs, span, width), F32)
    buffers = entry_scratch(plan, summary[0])

    in_hbm = pl.BlockSpec(memory_space=pltpu.HBM)
    outs = [((seqs, LANES), jnp.int32), tile, whole, ((rows, LANES), F32), ((2, 8, states), F32)]
    outs += [((2, radix) + summary[0], F32) for radix, _ in plan]
    prepared = pl.pallas_call(
        functools.partial(prepare_body, plan, span),
        out_shape=[jax.ShapeDtypeStruct(shape, dtype) for shape, dtype in outs],
        in_specs=[in_hbm] * 4,
        out_specs=[pl.BlockSpec(memory_space=pltpu.VMEM)] * len(outs),
        scratch_shapes=[
            pltpu.SMEM(lengths.shape, jnp.int32),
            pltpu.VMEM(inputs.shape, F32),
            pltpu.VMEM(nu_log.shape, F32),
            pltpu.VMEM(phase.shape, F32),
            pltpu.SemaphoreType.DMA((span // PIECE + 3,)),
        ],
        compiler_params=pltpu.CompilerParams(vmem_limit_bytes=24 * MIB),
    )(*(pltpu.with_memory_space_constraint(a, pltpu.HBM) for a in (lengths, inputs, nu_log, phase)))
    lens, sums, x0, mask, decay = prepared[:5]
    factors = prepared[5:]

    def project(k, sums, x):
        return run(
            functools.partial(project_body, k, span, k == 1),
            [whole_low, pair, eight, summary],
            [lens, everywhere(sums), x, bn_gain, bn_bias, w_in, decay],
        )

    def entered(body, outs, held, operands, after=(), limit=24, weight=1 << 33):
        operands = entry_operands(held, factors) + operands
        return run(with_entry(body, plan), outs, operands, after, buffers, limit, weight)

    u0, v0, stats0, part = project(0, sums, x0)
    held = exchange(0, part, plan, factors, False, False)
    x1, h0, act0, slope0, gate0, value0, sums = entered(
        functools.partial(forward_body, 0, plan, span),
        [whole, held_low, whole_low, whole_low, whole_low, whole_low, tile],
        held,
        [lens, v0, x0, mask, stats0, bn_bias, decay, w_out, skip, w_glu],
    )
    u1, v1, stats1, part = project(1, sums, x1)
    held = exchange(1, part, plan, factors, True, False)
    output, h1, act1, dz1, dy1, g1, part = entered(
        functools.partial(turn_body, 1, plan, span),
        [seq_major, held_low, whole_low, double_low, whole_low, pair, summary],
        held,
        [lens, v1, x1, cotangent, stats1, bn_bias, decay, w_out, skip, w_glu],
    )

    flows = {}
    flows["top"] = Bulk(
        count, [act1, h1], [dz1, dy1], [(0, 0, 0, 0), (0, 0, 0, width), (1, 0, 1, 0)], [part]
    )
    flows["top"].send()

    def beside_top(level, group):
        if level == 0:
            return flows["top"].parts[-1:]
        if level == len(plan) - 1:
            flows["step"] = flows["top"].send(group)
        return ()

    held = exchange(1, part, plan, factors, False, True, beside_top)
    top = flows["top"]
    dv1, small1 = entered(
        functools.partial(adjoint_body, 1, plan, span, False),
        [pair_low, eight],
        held,
        [lens, g1, h1, v1, decay],
        [flows["step"]],
        weight=1 << 20,
    )
    part1, skip1, sums = run(
        functools.partial(input_body, 1, seqs, True),
        [whole, eight, tile],
        [dv1, dy1, x1, cotangent, stats1, bn_gain, bn_bias, w_in, skip],
        weight=1 << 20,
    )
    step = top.send([sums])
    (sums,) = run(join_body, [tile], [sums], [step], limit=4)
    sums = everywhere(sums)
    step = top.send([sums])
    d0, dz0, dy0, g0, grads1, part = run(
        functools.partial(back_body, 0, span, True),
        [whole, double_low, whole_low, pair, eight, summary],
        [lens, sums, part1, x1, mask, stats1, slope0, gate0, value0, bn_gain, decay, w_out, w_glu],
        [step],
    )

    flows["middle"] = Bulk(
        count, [act0], [dz0], [(0, 0, 0, 0), (0, 0, 0, width)], [part]
    )
    flows["middle"].send()

    def beside_middle(level, group):
        if level == 0:
            return flows["middle"].parts[-1:]
        if level == len(plan) - 2:
            flows["other"] = Bulk(
                count, [u1, h0], [dv1, dy0], [(0, 0, 0, 0), (1, seqs, 1, 0)], group[1:2], weight=1 << 20
            )
            flows["other"].send()
            return [top.send(group[1:2]), flows["other"].parts[-1]]
        if level == len(plan) - 1:
            flows["step"] = flows["middle"].send(group)
        return ()

    held = exchange(0, part, plan, factors, True, True, beside_middle)
    middle = flows["middle"]
    other = flows["other"]
    dv0, small0 = entered(
        functools.partial(adjoint_body, 0, plan, span, True),
        [pair_low, eight],
        held,
        [lens, g0, h0, v0, decay],
        [flows["step"]],
        weight=1 << 20,
    )
    part0, skip0, sums = run(
        functools.partial(input_body, 0, seqs, False),
        [whole, eight, ((2, 8, width), F32)],
        [dv0, dy0, x0, d0, stats0, bn_gain, bn_bias, w_in, skip],
        weight=1 << 20,
    )

    (small,) = run(small_body, [((16, width), F32)], [small0, skip0, sums, small1, skip1], limit=4)
    step = middle.send([part0])
    step = other.send([step])
    step = top.settle([step])
    top.fetch()
    last = Bulk(count, [u0], [dv0], [(0, 0, 0, 0)], [step], [small], weight=1 << 20)
    last.send()
    step = last.parts[-1]
    step = top.fetch([step])
    step = last.send([step])
    step = other.send([step])
    step = middle.send([step])
    step = other.send([step])
    step = top.fetch([step])
    step = middle.send([step])
    step = last.send([step])
    step = other.send([step])
    step = middle.settle([step])
    middle.fetch()
    step = last.send([step])
    step = other.settle([step])
    other.fetch()
    step = top.fetch([step])
    step = middle.fetch([step])
    step = last.send([step])
    step = other.fetch([step])
    step = middle.fetch([step])
    step = last.settle([step])
    last.fetch()
    step = other.fetch([step])
    step = last.fetch([step])
    step = middle.fetch([step])
    step = last.fetch([step])
    step = other.fetch([step])
    step = top.fetch([step])
    step = last.fetch([step])
    grad_x, g_gain, g_bias, g_nu, g_phase, g_skip, running_out = run(
        functools.partial(finish_body, span),
        [seq_major] + [((2, width), F32)] * 2 + [((2, states), F32)] * 2
        + [((2, width), F32), ((2, 2, width), F32)],
        [last.total, lens, part0, x0, mask, bn_gain, decay, running, stats0, stats1, grads1],
        [step],
    )
    step = middle.fetch([g_gain])
    step = other.fetch([step])
    step = last.fetch([step])
    g_glu, g_out = unpack(
        count,
        [top],
        [[(0, 1, 0), (0, 1, width), (1, 1, 0)]],
        [(2, width, 2 * width), (2, 2 * states, width)],
    )
    g_glu, g_out, g_in = unpack(
        count,
        [middle, other, last],
        [
            [(0, 0, 0), (0, 0, width)],
            [(2, 1, 0), (1, 0, 0)],
            [(2, 0, 0)],
        ],
        [(2, width, 2 * width), (2, 2 * states, width), (2, width, 2 * states)],
        [g_glu, g_out],
    )
    return (output, grad_x, g_gain, g_bias, g_in, g_nu, g_phase, g_out, g_skip, g_glu, running_out)


def solution(mesh):
    placed = (P(None, "tm", None), P(), P(None, "tm", None)) + (P(),) * 9
    return jax.shard_map(
        shards,
        mesh=mesh,
        in_specs=placed,
        out_specs=(P(None, "tm", None),) * 2 + (P(),) * 9,
        check_vma=False,
    )
```

```python
import functools
import math

import jax
import jax.numpy as jnp
from jax import lax
from jax.experimental import pallas as pl
from jax.experimental.pallas import tpu as pltpu
from jax.sharding import PartitionSpec as P

norm_epsilon = 1e-05
momentum = 0.1
inverse_root_two = 0.7071067811865476
density_scale = 0.3989422804014327
F32, BF16 = jnp.float32, jnp.bfloat16
LANES = 128
MIB = 1 << 20


def dot(left, right):
    return jnp.dot(left, right, preferred_element_type=F32)


def dot_tn(left, right):
    return lax.dot_general(left, right, (((0,), (0,)), ((), ())), preferred_element_type=F32)


def dot_nt(left, right):
    return lax.dot_general(left, right, (((1,), (1,)), ((), ())), preferred_element_type=F32)


def run(body, outs, operands, after=(), scratch=(), limit=24, weight=1 << 33):
    vmem = pl.BlockSpec(memory_space=pltpu.VMEM)
    anywhere = pl.BlockSpec(memory_space=pl.ANY)
    first, second = len(operands), len(operands) + len(after)

    def kernel(*refs):
        body(*refs[:first], *refs[second:])

    return pl.pallas_call(
        kernel,
        out_shape=[jax.ShapeDtypeStruct(shape, dtype) for shape, dtype in outs],
        in_specs=[vmem] * len(operands) + [anywhere] * len(after),
        out_specs=[vmem] * len(outs),
        scratch_shapes=list(scratch),
        compiler_params=pltpu.CompilerParams(vmem_limit_bytes=limit * MIB),
        cost_estimate=pl.CostEstimate(flops=weight, bytes_accessed=0, transcendentals=0),
    )(*operands, *after)


def radices(count):
    out = []
    while count > 1:
        radix = 2 if not out or count % 4 else 4
        out.append(radix)
        count //= radix
    return out


def stages(count):
    stride, out = 1, []
    for radix in radices(count):
        out.append((radix, stride))
        stride *= radix
    return out


def swap(value, stride, mask):
    count = lax.axis_size("tm")
    return lax.ppermute(value, "tm", [(i, i ^ (stride * mask)) for i in range(count)])


def group_of(value, radix, stride):
    return [value] + [swap(value, stride, mask) for mask in range(1, radix)]


def place_in(radix, stride):
    return lax.rem(lax.div(lax.axis_index("tm"), stride), radix)


def rows_to_tile(first, second):
    pieces = [
        row[:, j : j + LANES] for row in (first, second) for j in range(0, row.shape[1], LANES)
    ]
    return jnp.concatenate(pieces, axis=0)


def tile_to_rows(tile):
    half = tile.shape[0] // 2
    return [
        jnp.concatenate([tile[base + j : base + j + 1, :] for j in range(half)], axis=1)
        for base in (0, half)
    ]


def spread(ref, first, second):
    ref[...] = jnp.broadcast_to(rows_to_tile(first, second)[None], ref.shape)


def gathered(ref):
    return tile_to_rows(jnp.sum(ref[...], axis=0))


def everywhere(tiles):
    return lax.all_to_all(tiles, "tm", 0, 0)


def mul(ar, ai, br, bi):
    return ar * br - ai * bi, ar * bi + ai * br


def members(refs, place, buffer):
    for offset, ref in enumerate(refs):
        buffer[jnp.bitwise_xor(place, offset)] = ref[...]


def pass_through(k, buffer, factor, place, state, backward, conj):
    radix, _, width = buffer.shape
    states = width // 2
    if state is None:
        zero = jnp.zeros(buffer.shape[1:-1] + (states,), F32)
        state = (zero, zero)
    entering = state
    for member in range(radix - 1, -1, -1) if backward else range(radix):
        entering = tuple(jnp.where(place == member, s, e) for s, e in zip(state, entering))
        fr, fi = factor[k, member, :, :states], factor[k, member, :, states:]
        moved = mul(fr, -fi if conj else fi, *state)
        state = (moved[0] + buffer[member, :, :states], moved[1] + buffer[member, :, states:])
    return entering, state


def total_body(k, radix, stride, backward, conj, *refs):
    factor, out, buffer = refs[radix:]
    place = place_in(radix, stride)
    members(refs[:radix], place, buffer)
    _, (re, im) = pass_through(k, buffer, factor, place, None, backward, conj)
    states = re.shape[1]
    out[:, :states] = re
    out[:, states:] = im


def group_total(k, group, level, plan, factors, backward, conj, after=()):
    radix, stride = plan[level]
    shape = group[0].shape
    (total,) = run(
        functools.partial(total_body, k, radix, stride, backward, conj),
        [(shape, F32)],
        list(group) + [factors[level]],
        after,
        [pltpu.VMEM((radix,) + shape, F32)],
        limit=4,
    )
    return total


def exchange(k, summary, plan, factors, backward, conj, between=None):
    held = []
    value = summary
    for level, (radix, stride) in enumerate(plan):
        group = group_of(value, radix, stride)
        held.append(group)
        if level + 1 < len(plan):
            after = between(level, group) if between else ()
            value = group_total(k, group, level, plan, factors, backward, conj, after)
            if between and level + 2 == len(plan):
                between(level + 1, [value])
    return held


def entry_operands(held, factors):
    return [value for group in held for value in group] + list(factors)


def entry_scratch(plan, shape):
    return [pltpu.VMEM((radix,) + shape, F32) for radix, _ in plan]


def entering_state(k, plan, refs, buffers, backward, conj):
    total = sum(radix for radix, _ in plan)
    values, factors = refs[:total], refs[total:]
    start, groups = 0, []
    for radix, _ in plan:
        groups.append(values[start : start + radix])
        start += radix
    state = None
    for level in range(len(plan) - 1, -1, -1):
        place = place_in(*plan[level])
        members(groups[level], place, buffers[level])
        state, _ = pass_through(k, buffers[level], factors[level], place, state, backward, conj)
    return state


CHUNKS = 32
LEVELS = CHUNKS.bit_length() - 1


def partners(count):
    order = [(1 << b, 1 << b) for b in range(count.bit_length() - 1)]
    if len(order) > 2:
        order[1], order[2] = (2, 4), (4, 2)
    return order


def with_partner(value, bits):
    even, odd = bits
    count = lax.axis_size("tm")
    return lax.ppermute(value, "tm", [(i, i ^ (odd if i & 1 else even)) for i in range(count)])


def own_chunk(count, other_core=False):
    here = lax.axis_index("tm")
    if other_core:
        here = jnp.bitwise_xor(here, 1)
    own = 0
    for even, odd in partners(count)[:LEVELS]:
        taken = jnp.where(jnp.bitwise_and(here, 1) == 1, here & odd, here & even)
        own = own * 2 + jnp.where(taken != 0, 1, 0)
    return own


def slots(level):
    return (CHUNKS >> (level + 1), CHUNKS >> level) if level < LEVELS else (0, 1)


def outer_body(count, pairs, n_left, n_right, n_extra, *refs):
    lefts, rights = refs[:n_left], refs[n_left : n_left + n_right]
    extra, outs = refs[n_left + n_right :][:n_extra], refs[n_left + n_right + n_extra : -len(pairs)]
    products = refs[-len(pairs) :]
    if extra:
        outs[0][-extra[0].shape[0] :, :] = extra[0][...]
    owns = own_chunk(count), own_chunk(count, True)
    half = CHUNKS // 2
    for q, (left, row, right, column) in enumerate(pairs):
        product = products[q]
        span = rights[right].shape[0]
        wide_left = lefts[left].shape[1]
        part = wide_left // CHUNKS
        width = product.shape[1]
        product[...] = dot_tn(
            lefts[left][row : row + span, :], rights[right][:, column : column + width]
        )
        for level in range(LEVELS + 1):
            low, high = slots(level)
            for slot in range(low, high):
                chunk = jnp.bitwise_xor(owns[slot // half], slot % half)
                chunk = pl.multiple_of(chunk * part, part)
                place = ((slot - low) * len(pairs) + q) * part
                outs[level][place : place + part, :] = product[pl.ds(chunk, part), :]


def add_body(low, extra, *refs):
    out = refs[-1]
    rows = out.shape[0] - extra
    total = refs[0][:rows, :]
    for ref in refs[1 : -2 if extra else -1]:
        total += ref[low : low + rows, :]
    out[:rows, :] = total
    if extra:
        mine, other = refs[-2], refs[-3]
        out[rows:, :] = mine[-extra:, :] + other[-extra:, :]


def spokes_body(rows, extra, *refs):
    near, far = refs[:2]
    received, mine, outs = refs[2:-4], refs[-4], refs[-3:]
    for slot, out in enumerate(outs, 1):
        total = near[...] if slot == 1 else far[(slot - 2) * rows : (slot - 1) * rows, :]
        for ref in received:
            total += ref[slot * rows : (slot + 1) * rows, :]
        out[:rows, :] = total
        if extra:
            out[rows:, :] = mine[-extra:, :] + received[-1][-extra:, :]


def hub_body(rows, extra, *refs):
    kept, received, mine, spokes, out = refs[0], refs[1:-5], refs[-5], refs[-4:-1], refs[-1]
    total = kept[...]
    for ref in received + spokes:
        total += ref[:rows, :]
    out[:rows, :] = total
    if extra:
        total = mine[-extra:, :]
        for ref in spokes:
            total += ref[-extra:, :]
        out[rows:, :] = total


def join_body(*refs):
    out = refs[-1]
    rows = refs[0].shape[0]
    for j, ref in enumerate(refs[:-1]):
        out[j * rows : (j + 1) * rows] = ref[...]


class Bulk:
    def __init__(self, count, lefts, rights, pairs, after=(), extra=(), hub=False, weight=1 << 33):
        self.hub = hub
        self.bits = partners(count)
        self.extra = extra[0].shape[0] if extra else 0
        width = 512
        part = lefts[0].shape[1] // CHUNKS
        self.rows = part * len(pairs)
        outs = [((self.rows * (hi - lo), width), F32) for lo, hi in map(slots, range(LEVELS + 1))]
        outs[0] = ((outs[0][0][0] + self.extra, width), F32)
        self.parts = run(
            functools.partial(outer_body, count, pairs, len(lefts), len(rights), len(extra)),
            outs,
            list(lefts) + list(rights) + list(extra),
            after,
            [pltpu.VMEM((lefts[pair[0]].shape[1], width), F32) for pair in pairs],
            limit=16,
            weight=weight,
        )
        self.received = []
        self.sent = None

    def reduced(self, level, after=()):
        low, high = slots(level)
        if not self.received:
            return self.parts[level]
        (total,) = run(
            functools.partial(add_body, low * self.rows, self.extra),
            [((self.rows * (high - low) + self.extra, self.parts[level].shape[1]), F32)],
            [self.parts[level]] + self.received + ([self.sent] if self.extra else []),
            after,
            limit=8,
        )
        return total

    def send(self, after=()):
        level = len(self.received)
        if self.hub and level == LEVELS - 2:
            shape = (self.rows + self.extra, self.parts[LEVELS].shape[1])
            sent = run(
                functools.partial(spokes_body, self.rows, self.extra),
                [(shape, F32)] * 3,
                [self.parts[LEVELS - 1], self.parts[LEVELS - 2]] + self.received + [self.sent],
                after,
                limit=8,
            )
            self.sent, self.spokes = sent[0], self.with_partners(sent)
            return self.sent
        self.sent = self.reduced(level, after)
        self.received.append(with_partner(self.sent, self.bits[level]))
        return self.sent

    def with_partners(self, values):
        far, near = self.bits[LEVELS - 2][0], self.bits[LEVELS - 1][0]
        masks = (near, far, near | far)
        return [swap(value, 1, mask) for value, mask in zip(values, masks)]

    def settle(self, after=()):
        if self.hub:
            (value,) = run(
                functools.partial(hub_body, self.rows, self.extra),
                [((self.rows + self.extra, self.parts[LEVELS].shape[1]), F32)],
                [self.parts[LEVELS]] + self.received + [self.sent] + self.spokes,
                after,
                limit=8,
            )
        else:
            value = self.reduced(LEVELS, after)
        for even, odd in self.bits[LEVELS:]:
            other = with_partner(value, (even, odd))
            (value,) = run(
                functools.partial(add_body, 0, 0), [(value.shape, F32)], [value, other], limit=4
            )
        self.total, self.value, self.level = value, value[: self.rows], LEVELS - 1
        return value

    def fetch(self, after=()):
        if self.level < LEVELS - 1:
            parts = [self.value] + self.others
            (self.value,) = run(
                join_body,
                [((len(parts) * self.value.shape[0], self.value.shape[1]), F32)],
                parts,
                after,
                limit=8,
            )
        if self.hub and self.level == LEVELS - 1:
            self.others = self.with_partners([self.value] * 3)
            self.level -= 2
        else:
            self.others = [with_partner(self.value, self.bits[self.level])]
            self.level -= 1
        return self.value


def unpack_body(count, width, layout, n_into, *refs):
    outs, sem = refs[2 * len(layout) + n_into : -1], refs[-1]
    owns = own_chunk(count), own_chunk(count, True)
    copies = []
    for piece, places in enumerate(layout):
        near, far = refs[2 * piece], refs[2 * piece + 1]
        for source, own in zip((near, far), owns):
            for j in range(CHUNKS // 2):
                chunk = jnp.bitwise_xor(own, j)
                part = source.shape[0] // (CHUNKS // 2) // len(places)
                for q, (out, k, column) in enumerate(places):
                    place = (j * len(places) + q) * part
                    rows = pl.ds(pl.multiple_of(chunk * part, part), part)
                    copies.append(
                        pltpu.make_async_copy(
                            source.at[pl.ds(place, part), :],
                            outs[out].at[k, rows, pl.ds(column, width)],
                            sem,
                        )
                    )
    for copy in copies:
        copy.start()
    for copy in copies:
        copy.wait()


def unpack(count, bulks, layout, shapes, into=()):
    operands = [value for bulk in bulks for value in (bulk.value, bulk.others[0])]
    anywhere = pl.BlockSpec(memory_space=pl.ANY)
    return pl.pallas_call(
        functools.partial(unpack_body, count, operands[0].shape[1], layout, len(into)),
        out_shape=[jax.ShapeDtypeStruct(shape, F32) for shape in shapes],
        in_specs=[anywhere] * (len(operands) + len(into)),
        out_specs=[anywhere] * len(shapes),
        scratch_shapes=[pltpu.SemaphoreType.DMA],
        input_output_aliases={len(operands) + j: j for j in range(len(into))},
        compiler_params=pltpu.CompilerParams(vmem_limit_bytes=4 * MIB),
    )(*operands, *into)


def steps(span, backward, body, start, unroll=None):
    def one(k, carry):
        return body(span - 1 - k if backward else k, carry)

    return lax.fori_loop(0, span, one, start, unroll=unroll or span)


def pieces(rows, step, backward=False):
    starts = range(0, rows, step)
    return reversed(starts) if backward else starts


def at(t, seqs):
    return pl.ds(pl.multiple_of(t * seqs, seqs), seqs)


def state_scan(v_ref, rel, lr, li, start, span, backward, keep=None):
    seqs, states = lr.shape

    def body(t, carry):
        re, im = carry
        vr, vi = v_ref[at(t, seqs), :states], v_ref[at(t, seqs), states:]
        next_re, next_im = mul(lr, li, re, im)
        live = rel > t
        re, im = jnp.where(live, next_re + vr, re), jnp.where(live, next_im + vi, im)
        if keep is not None:
            keep(t, re, im)
        return re, im

    return steps(span, backward, body, start)


def adjoint_scan(g_ref, rel, lr, li, start, span, backward, use=None, extra=(), unroll=None):
    seqs, states = lr.shape

    def body(t, carry):
        (re, im), kept = carry
        ar, ai = g_ref[at(t, seqs), :states] + re, g_ref[at(t, seqs), states:] + im
        live = rel > t
        if use is not None:
            kept = use(t, ar, ai, live, kept)
        next_re, next_im = mul(lr, -li, ar, ai)
        return (jnp.where(live, next_re, ar), jnp.where(live, next_im, ai)), kept

    return steps(span, backward, body, (start, extra), unroll)


def wide(ref, row, shape):
    return jnp.broadcast_to(ref[row : row + 1, :], shape)


def to_time_major(piece):
    seqs, span, width = piece.shape
    return jnp.swapaxes(piece, 0, 1).reshape(span * seqs, width)


def from_time_major(rows, seqs):
    return jnp.swapaxes(rows.reshape(-1, seqs, rows.shape[-1]), 0, 1)


def lane_tiled(column, width):
    return jnp.concatenate([column] * (width // LANES), axis=1)


def gelu_parts(y):
    cdf = 0.5 * (1.0 + lax.erf(y * inverse_root_two))
    pdf = jnp.exp(-0.5 * y * y) * density_scale
    return y * cdf, cdf + y * pdf


sigmoid = jax.nn.sigmoid


CHUNK = 64
PIECE = 8


def prepare_body(span, lengths_any, x_any, nu_any, phase_any, *outs):
    lens_ref, sums_ref, tm_ref, mask_ref, decay_ref = outs[:5]
    lengths_ref, x_ref, nu_ref, phase_ref, sems = outs[5:]
    seqs, _, width = x_ref.shape
    states = nu_ref.shape[-1]
    copies = [
        pltpu.make_async_copy(
            x_any.at[:, pl.ds(t0, PIECE), :], x_ref.at[:, pl.ds(t0, PIECE), :], sems.at[t0 // PIECE]
        )
        for t0 in range(0, span, PIECE)
    ]
    small = [
        pltpu.make_async_copy(nu_any, nu_ref, sems.at[len(copies)]),
        pltpu.make_async_copy(phase_any, phase_ref, sems.at[len(copies) + 1]),
        pltpu.make_async_copy(lengths_any, lengths_ref, sems.at[len(copies) + 2]),
    ]
    for copy in small + copies:
        copy.start()
    for copy in small:
        copy.wait()
    here = lax.axis_index("tm")
    row = lax.broadcasted_iota(jnp.int32, (seqs, LANES), 0)
    lens = jnp.zeros((seqs, LANES), jnp.int32)
    for seq in range(seqs):
        lens = jnp.where(row == seq, lengths_ref[seq], lens)
    lens_ref[...] = lens
    rel = lens - here * span
    rate = jnp.exp(nu_ref[...])
    radius = jnp.exp(-rate)
    angle = phase_ref[...]
    cosine, sine = jnp.cos(angle), jnp.sin(angle)
    gamma = jnp.sqrt(one_less_exp(2.0 * rate))
    for row, value in enumerate((radius * cosine, radius * sine, gamma, rate, radius, cosine, sine)):
        for k in range(2):
            decay_ref[k, row : row + 1, :] = value[k : k + 1, :]
    first = jnp.zeros((seqs, width), F32)
    second = jnp.zeros((seqs, width), F32)
    for t0 in range(0, span, PIECE):
        copies[t0 // PIECE].wait()
        piece = jnp.swapaxes(x_ref[:, t0 : t0 + PIECE, :], 0, 1)
        for j in range(PIECE):
            rows = piece[j]
            mask = jnp.where(rel > t0 + j, 1.0, 0.0)
            place = slice((t0 + j) * seqs, (t0 + j + 1) * seqs)
            mask_ref[place, :] = mask
            tm_ref[place, :] = rows
            live = rows * lane_tiled(mask, width)
            first += live
            second += live * rows
    spread(sums_ref, jnp.sum(first, 0, keepdims=True), jnp.sum(second, 0, keepdims=True))


def factors_body(plan, span, lens_ref, decay_ref, *factor_refs):
    seqs, states = lens_ref.shape[0], decay_ref.shape[-1]
    here = lax.axis_index("tm")
    lens = lens_ref[...]
    for k in range(2):
        for level, (radix, stride) in enumerate(plan):
            base = lax.div(here, radix * stride) * (radix * stride)
            for member in range(radix):
                start = (base + member * stride) * span
                count = jnp.concatenate(
                    [jnp.clip(lens - start, 0, stride * span)] * (states // LANES), axis=1
                )
                power = (decay_ref[k, 0:1, :], decay_ref[k, 1:2, :])
                re, im = jnp.ones((seqs, states), F32), jnp.zeros((seqs, states), F32)
                for bit in range((span * stride).bit_length()):
                    taken = jnp.bitwise_and(count, 1 << bit) != 0
                    next_re, next_im = mul(re, im, *power)
                    re, im = jnp.where(taken, next_re, re), jnp.where(taken, next_im, im)
                    power = mul(*power, *power)
                factor_refs[level][k, member, :, :states] = re
                factor_refs[level][k, member, :, states:] = im


def one_less_exp(x):
    total = 1.0
    for n in range(8, 1, -1):
        total = 1.0 - total * x * (1.0 / n)
    return total * x


def relative(lens_ref, span, states):
    rel = lens_ref[...] - lax.axis_index("tm") * span
    return jnp.concatenate([rel] * (states // LANES), axis=1)


def token_scale(lens_ref):
    return 1.0 / jnp.sum(lens_ref[:, 0:1].astype(F32), axis=0, keepdims=True)


def project_body(
    k, span, backward, lens_ref, sums_ref, x_ref, gain_ref, bias_ref, w_ref, decay_ref,
    u_ref, v_ref, stats_ref, summary_ref,
):
    seqs = lens_ref.shape[0]
    states = decay_ref.shape[-1]
    total, squares = gathered(sums_ref)
    scale = token_scale(lens_ref)
    mean = total * scale
    var = squares * scale - mean * mean
    rstd = lax.rsqrt(var + norm_epsilon)
    stats_ref[0:1, :] = mean
    stats_ref[1:2, :] = var
    stats_ref[2:3, :] = rstd
    stats_ref[3:4, :] = rstd * gain_ref[k : k + 1, :]
    slope = rstd * gain_ref[k : k + 1, :]
    bias = bias_ref[k : k + 1, :]
    step = 16 * seqs
    for r in pieces(span * seqs, step, backward):
        u = ((x_ref[r : r + step, :] - mean) * slope + bias).astype(BF16)
        u_ref[r : r + step, :] = u
        v_ref[r : r + step, :] = dot(u, w_ref[k])
    shape = (seqs, states)
    rel = relative(lens_ref, span, states)
    lr, li = wide(decay_ref.at[k], 0, shape), wide(decay_ref.at[k], 1, shape)
    zero = jnp.zeros(shape, F32)
    re, im = state_scan(v_ref, rel, lr, li, (zero, zero), span, backward)
    summary_ref[:, :states] = re
    summary_ref[:, states:] = im


def rebuild_states(k, plan, span, backward, refs, buffers, rel, v_ref, decay_ref, h_ref):
    seqs, states = rel.shape
    lr, li, gamma = (wide(decay_ref.at[k], row, rel.shape) for row in range(3))
    start = entering_state(k, plan, refs, buffers, backward, False)

    lead = 0 if backward else 1

    def keep(t, re, im):
        h_ref[at(t + lead, seqs), :states] = (re * gamma).astype(BF16)
        h_ref[at(t + lead, seqs), states:] = (im * gamma).astype(BF16)

    keep(span if backward else -1, *start)
    state_scan(v_ref, rel, lr, li, start, span, backward, keep)


def forward_body(
    k, plan, span, exch, lens_ref, v_ref, x_ref, mask_ref, stats_ref, bias_ref,
    decay_ref, w_out_ref, skip_ref, w_glu_ref,
    out_ref, h_ref, act_ref, slope_ref, gate_ref, value_ref, sums_ref, buffers,
):
    seqs = lens_ref.shape[0]
    width = x_ref.shape[1]
    states = decay_ref.shape[-1]
    rel = relative(lens_ref, span, states)
    rebuild_states(k, plan, span, False, exch, buffers, rel, v_ref, decay_ref, h_ref)
    mean, scale = stats_ref[0:1, :], stats_ref[3:4, :]
    bias, skip = bias_ref[k : k + 1, :], skip_ref[k : k + 1, :]
    step = 64 * seqs
    first = jnp.zeros((8, width), F32)
    second = jnp.zeros((8, width), F32)
    for r in pieces(span * seqs, step, False):
        x = x_ref[r : r + step, :]
        u = (x - mean) * scale + bias
        y = dot(h_ref[r + seqs : r + seqs + step, :], w_out_ref[k]) + skip * u
        act, slope = gelu_parts(y)
        act = act.astype(BF16)
        act_ref[r : r + step, :] = act
        slope_ref[r : r + step, :] = slope.astype(BF16)
        z = dot(act, w_glu_ref[k])
        value, gate = z[:, :width], sigmoid(z[:, width:])
        gated = value * gate
        out = x + gated
        out_ref[r : r + step, :] = out
        gate_ref[r : r + step, :] = gate.astype(BF16)
        value_ref[r : r + step, :] = (gated * (1.0 - gate)).astype(BF16)
        live = out * lane_tiled(mask_ref[r : r + step, :], width)
        first += jnp.sum(live.reshape(-1, 8, width), 0)
        second += jnp.sum((live * out).reshape(-1, 8, width), 0)
    spread(sums_ref, jnp.sum(first, 0, keepdims=True), jnp.sum(second, 0, keepdims=True))


def back_rows(k, r, step, dza, dzb, slope, width, w_glu_ref, w_out_ref, dz_ref, dy_ref, g_ref):
    dza, dzb = dza.astype(BF16), dzb.astype(BF16)
    dz_ref[r : r + step, :width] = dza
    dz_ref[r : r + step, width:] = dzb
    w = w_glu_ref[k]
    dact = dot_nt(dza, w[:, :width]) + dot_nt(dzb, w[:, width:])
    dy = (dact * slope).astype(BF16)
    dy_ref[r : r + step, :] = dy
    g_ref[r : r + step, :] = dot_nt(dy, w_out_ref[k])


def local_adjoint(k, span, backward, rel, g_ref, decay_ref, summary_ref, unroll=None):
    seqs, states = rel.shape
    lr, li = wide(decay_ref.at[k], 0, rel.shape), wide(decay_ref.at[k], 1, rel.shape)
    zero = jnp.zeros(rel.shape, F32)
    (re, im), _ = adjoint_scan(g_ref, rel, lr, li, (zero, zero), span, backward, unroll=unroll)
    summary_ref[:, :states] = re
    summary_ref[:, states:] = im


def turn_body(
    k, plan, span, exch, lens_ref, v_ref, x_ref, cot_ref, stats_ref, bias_ref,
    decay_ref, w_out_ref, skip_ref, w_glu_ref,
    out_ref, h_ref, act_ref, dz_ref, dy_ref, g_ref, summary_ref, buffers,
):
    seqs = lens_ref.shape[0]
    width = x_ref.shape[1]
    states = decay_ref.shape[-1]
    rel = relative(lens_ref, span, states)
    rebuild_states(k, plan, span, True, exch, buffers, rel, v_ref, decay_ref, h_ref)
    mean, scale = stats_ref[0:1, :], stats_ref[3:4, :]
    bias, skip = bias_ref[k : k + 1, :], skip_ref[k : k + 1, :]
    step = 64 * seqs
    for r in pieces(span * seqs, step, True):
        t0 = r // seqs
        x = x_ref[r : r + step, :]
        u = (x - mean) * scale + bias
        y = dot(h_ref[r : r + step, :], w_out_ref[k]) + skip * u
        act, slope = gelu_parts(y)
        act = act.astype(BF16)
        act_ref[r : r + step, :] = act
        z = dot(act, w_glu_ref[k])
        value, gate = z[:, :width], sigmoid(z[:, width:])
        gated = value * gate
        out_ref[:, t0 : t0 + 64, :] = from_time_major(x + gated, seqs)
        d = to_time_major(cot_ref[:, t0 : t0 + 64, :])
        back_rows(
            k, r, step, d * gate, d * (gated * (1.0 - gate)), slope, width,
            w_glu_ref, w_out_ref, dz_ref, dy_ref, g_ref,
        )
    local_adjoint(k, span, False, rel, g_ref, decay_ref, summary_ref)


def back_body(
    k, span, backward, lens_ref, sums_ref, part_ref, x_ref, mask_ref, stats_ref, slope_ref,
    gate_ref, value_ref, gain_ref, decay_ref, w_out_ref, w_glu_ref,
    d_ref, dz_ref, dy_ref, g_ref, grads_ref, summary_ref,
):
    seqs = lens_ref.shape[0]
    width = x_ref.shape[1]
    states = decay_ref.shape[-1]
    rel = relative(lens_ref, span, states)
    bias_grad, gain_grad = gathered(sums_ref)
    grads_ref[0:1, :] = gain_grad
    grads_ref[1:2, :] = bias_grad
    shift, tilt = input_terms(
        k + 1, token_scale(lens_ref), bias_grad, gain_grad, stats_ref, gain_ref
    )
    mean = stats_ref[0:1, :]
    step = 64 * seqs
    for r in pieces(span * seqs, step, backward):
        live = lane_tiled(mask_ref[r : r + step, :], width)
        d = part_ref[r : r + step, :] + live * (shift + tilt * (x_ref[r : r + step, :] - mean))
        d_ref[r : r + step, :] = d
        back_rows(
            k, r, step, d * gate_ref[r : r + step, :].astype(F32),
            d * value_ref[r : r + step, :].astype(F32), slope_ref[r : r + step, :].astype(F32), width,
            w_glu_ref, w_out_ref, dz_ref, dy_ref, g_ref,
        )
    local_adjoint(k, span, backward, rel, g_ref, decay_ref, summary_ref, 8)


def input_terms(k, scale, bias_grad, gain_grad, stats_ref, gain_ref):
    rstd = stats_ref[2:3, :]
    gain = gain_ref[k : k + 1, :]
    return -rstd * gain * bias_grad * scale, -rstd * rstd * gain * gain_grad * scale


def adjoint_body(
    k, plan, span, backward, exch, lens_ref, g_ref, h_ref, v_ref, decay_ref, dv_ref, small_ref, buffers
):
    seqs = lens_ref.shape[0]
    states = decay_ref.shape[-1]
    rel = relative(lens_ref, span, states)
    lr, li, gamma = (wide(decay_ref.at[k], row, rel.shape) for row in range(3))
    start = entering_state(k, plan, exch, buffers, backward, True)
    before = 0 if backward else 1

    def use(t, ar, ai, live, kept):
        ar, ai = jnp.where(live, ar, 0.0), jnp.where(live, ai, 0.0)
        dv_ref[at(t, seqs), :states] = (ar * gamma).astype(BF16)
        dv_ref[at(t, seqs), states:] = (ai * gamma).astype(BF16)
        pr = h_ref[at(t + before, seqs), :states].astype(F32)
        pi = h_ref[at(t + before, seqs), states:].astype(F32)
        vr, vi = v_ref[at(t, seqs), :states], v_ref[at(t, seqs), states:]
        return (
            kept[0] + (ar * pr + ai * pi),
            kept[1] + (ai * pr - ar * pi),
            kept[2] + (ar * vr + ai * vi),
        )

    zero = jnp.zeros(rel.shape, F32)
    _, kept = adjoint_scan(g_ref, rel, lr, li, start, span, backward, use, (zero, zero, zero))
    small_ref[...] = jnp.zeros_like(small_ref)
    for j in range(2):
        small_ref[0:1, j * states : (j + 1) * states] = jnp.sum(kept[j], 0, keepdims=True)
    small_ref[1:2, :states] = jnp.sum(kept[2], 0, keepdims=True)


def input_body(
    k, seqs, seq_major, dv_ref, dy_ref, x_ref, d_ref, stats_ref, gain_ref, bias_ref, w_in_ref, skip_ref,
    part_ref, skip_grad_ref, sums_ref,
):
    width = x_ref.shape[1]
    mean, scale, rstd = stats_ref[0:1, :], stats_ref[3:4, :], stats_ref[2:3, :]
    gain, bias, skip = (ref[k : k + 1, :] for ref in (gain_ref, bias_ref, skip_ref))
    step = CHUNK * seqs
    first = jnp.zeros((8, width), F32)
    second = jnp.zeros((8, width), F32)
    third = jnp.zeros((8, width), F32)
    for r in range(0, x_ref.shape[0], step):
        xhat = (x_ref[r : r + step, :] - mean) * rstd
        dy = dy_ref[r : r + step, :].astype(F32)
        du = dot_nt(dv_ref[r : r + step, :], w_in_ref[k]) + dy * skip
        first += jnp.sum(du.reshape(-1, 8, width), 0)
        second += jnp.sum((du * xhat).reshape(-1, 8, width), 0)
        third += jnp.sum((dy * (xhat * gain + bias)).reshape(-1, 8, width), 0)
        if seq_major:
            d = to_time_major(d_ref[:, r // seqs : r // seqs + CHUNK, :])
        else:
            d = d_ref[r : r + step, :]
        part_ref[r : r + step, :] = d + du * scale
    skip_grad_ref[...] = third
    if seq_major:
        spread(sums_ref, jnp.sum(first, 0, keepdims=True), jnp.sum(second, 0, keepdims=True))
    else:
        sums_ref[0] = first
        sums_ref[1] = second


def small_body(small0, skip0, sums0, small1, skip1, out):
    out[...] = jnp.zeros_like(out)
    rows = [small0[0:1, :], small0[1:2, :], skip0[...], sums0[0], sums0[1]]
    for row, value in enumerate(rows):
        out[row : row + 1, :] = jnp.sum(value, 0, keepdims=True)
    for row, value in enumerate([small1[0:1, :], small1[1:2, :], skip1[...]]):
        out[8 + row : 9 + row, :] = jnp.sum(value, 0, keepdims=True)


def finish_body(
    span, total_ref, lens_ref, part_ref, x_ref, mask_ref, gain_ref, decay_ref, running_ref, stats0_ref,
    stats1_ref, grads_ref, out_ref, g_gain_ref, g_bias_ref, nu_ref, phase_ref, skip_ref, run_ref,
):
    stats_refs = (stats0_ref, stats1_ref)
    small = total_ref[total_ref.shape[0] - 16 :, :]
    states = decay_ref.shape[-1]
    count = jnp.sum(lens_ref[:, 0:1].astype(F32), axis=0, keepdims=True)
    for k in range(2):
        _, _, gamma, rate, radius, cosine, sine = (decay_ref[k, j : j + 1, :] for j in range(7))
        sum_re, sum_im = small[8 * k : 8 * k + 1, :states], small[8 * k : 8 * k + 1, states:]
        g_gamma = small[8 * k + 1 : 8 * k + 2, :states]
        nu_ref[k : k + 1, :] = (sum_re * cosine + sum_im * sine) * (
            -radius * rate
        ) + g_gamma * rate * radius * radius / gamma
        phase_ref[k : k + 1, :] = radius * (sum_im * cosine - sum_re * sine)
        skip_ref[k : k + 1, :] = small[8 * k + 2 : 8 * k + 3, :]
        mean, var = stats_refs[k][0:1, :], stats_refs[k][1:2, :]
        run_ref[k, 0:1, :] = (1.0 - momentum) * running_ref[k, 0:1, :] + momentum * mean
        run_ref[k, 1:2, :] = (1.0 - momentum) * running_ref[k, 1:2, :] + momentum * var * (
            count / (count - 1.0)
        )
    bias_grad, gain_grad = small[3:4, :], small[4:5, :]
    g_gain_ref[0:1, :], g_gain_ref[1:2, :] = gain_grad, grads_ref[0:1, :]
    g_bias_ref[0:1, :], g_bias_ref[1:2, :] = bias_grad, grads_ref[1:2, :]
    seqs = out_ref.shape[0]
    width = x_ref.shape[1]
    shift, tilt = input_terms(0, 1.0 / count, bias_grad, gain_grad, stats_refs[0], gain_ref)
    mean = stats_refs[0][0:1, :]
    step = CHUNK * seqs
    for r in range(0, span * seqs, step):
        live = lane_tiled(mask_ref[r : r + step, :], width)
        d = part_ref[r : r + step, :] + live * (shift + tilt * (x_ref[r : r + step, :] - mean))
        out_ref[:, r // seqs : r // seqs + CHUNK, :] = from_time_major(d, seqs)


def with_entry(body, plan):
    def wrapped(*refs):
        n_exch = sum(radix for radix, _ in plan) + len(plan)
        body(refs[:n_exch], *refs[n_exch : -len(plan)], refs[-len(plan) :])

    return wrapped


def shards(
    inputs, lengths, cotangent, bn_gain, bn_bias, running, w_in, nu_log, phase, w_out, skip, w_glu
):
    seqs, span, width = inputs.shape
    states = nu_log.shape[1]
    count = lax.axis_size("tm")
    rows = span * seqs
    plan = stages(count)

    tile = ((count, 2 * width // LANES, LANES), F32)
    whole, whole_low = ((rows, width), F32), ((rows, width), BF16)
    pair, pair_low = ((rows, 2 * states), F32), ((rows, 2 * states), BF16)
    double_low = ((rows, 2 * width), BF16)
    held_low = ((rows + seqs, 2 * states), BF16)
    summary = ((seqs, 2 * states), F32)
    eight = ((8, width), F32)
    seq_major = ((seqs, span, width), F32)
    buffers = entry_scratch(plan, summary[0])

    in_hbm = pl.BlockSpec(memory_space=pltpu.HBM)
    outs = [((seqs, LANES), jnp.int32), tile, whole, ((rows, LANES), F32), ((2, 8, states), F32)]
    prepared = pl.pallas_call(
        functools.partial(prepare_body, span),
        out_shape=[jax.ShapeDtypeStruct(shape, dtype) for shape, dtype in outs],
        in_specs=[in_hbm] * 4,
        out_specs=[pl.BlockSpec(memory_space=pltpu.VMEM)] * len(outs),
        scratch_shapes=[
            pltpu.SMEM(lengths.shape, jnp.int32),
            pltpu.VMEM(inputs.shape, F32),
            pltpu.VMEM(nu_log.shape, F32),
            pltpu.VMEM(phase.shape, F32),
            pltpu.SemaphoreType.DMA((span // PIECE + 3,)),
        ],
        compiler_params=pltpu.CompilerParams(vmem_limit_bytes=24 * MIB),
    )(*(pltpu.with_memory_space_constraint(a, pltpu.HBM) for a in (lengths, inputs, nu_log, phase)))
    lens, sums, x0, mask, decay = prepared[:5]

    def project(k, sums, x):
        return run(
            functools.partial(project_body, k, span, k == 1),
            [whole_low, pair, eight, summary],
            [lens, everywhere(sums), x, bn_gain, bn_bias, w_in, decay],
        )

    def entered(body, outs, held, operands, after=(), limit=24, weight=1 << 33):
        operands = entry_operands(held, factors) + operands
        return run(with_entry(body, plan), outs, operands, after, buffers, limit, weight)

    u0, v0, stats0, part = project(0, sums, x0)
    factors = run(
        functools.partial(factors_body, plan, span),
        [((2, radix) + summary[0], F32) for radix, _ in plan],
        [lens, decay],
        [part],
    )
    held = exchange(0, part, plan, factors, False, False)
    x1, h0, act0, slope0, gate0, value0, sums = entered(
        functools.partial(forward_body, 0, plan, span),
        [whole, held_low, whole_low, whole_low, whole_low, whole_low, tile],
        held,
        [lens, v0, x0, mask, stats0, bn_bias, decay, w_out, skip, w_glu],
    )
    u1, v1, stats1, part = project(1, sums, x1)
    held = exchange(1, part, plan, factors, True, False)
    output, h1, act1, dz1, dy1, g1, part = entered(
        functools.partial(turn_body, 1, plan, span),
        [seq_major, held_low, whole_low, double_low, whole_low, pair, summary],
        held,
        [lens, v1, x1, cotangent, stats1, bn_bias, decay, w_out, skip, w_glu],
    )

    flows = {}
    flows["top"] = Bulk(
        count, [act1, h1], [dz1, dy1], [(0, 0, 0, 0), (0, 0, 0, width), (1, 0, 1, 0)], [part]
    )
    flows["top"].send()

    def beside_top(level, group):
        if level == 0:
            return flows["top"].parts[-1:]
        if level == len(plan) - 1:
            flows["step"] = flows["top"].send(group)
        return ()

    held = exchange(1, part, plan, factors, False, True, beside_top)
    top = flows["top"]
    dv1, small1 = entered(
        functools.partial(adjoint_body, 1, plan, span, False),
        [pair_low, eight],
        held,
        [lens, g1, h1, v1, decay],
        [flows["step"]],
        weight=1 << 20,
    )
    part1, skip1, sums = run(
        functools.partial(input_body, 1, seqs, True),
        [whole, eight, tile],
        [dv1, dy1, x1, cotangent, stats1, bn_gain, bn_bias, w_in, skip],
        weight=1 << 20,
    )
    step = top.send([sums])
    (sums,) = run(join_body, [tile], [sums], [step], limit=4)
    sums = everywhere(sums)
    step = top.send([sums])
    d0, dz0, dy0, g0, grads1, part = run(
        functools.partial(back_body, 0, span, True),
        [whole, double_low, whole_low, pair, eight, summary],
        [lens, sums, part1, x1, mask, stats1, slope0, gate0, value0, bn_gain, decay, w_out, w_glu],
        [step],
    )

    flows["middle"] = Bulk(
        count, [act0], [dz0], [(0, 0, 0, 0), (0, 0, 0, width)], [part]
    )
    flows["middle"].send()

    def beside_middle(level, group):
        if level == 0:
            return flows["middle"].parts[-1:]
        if level == len(plan) - 2:
            flows["other"] = Bulk(
                count, [u1, h0], [dv1, dy0], [(0, 0, 0, 0), (1, seqs, 1, 0)], group[1:2], weight=1 << 20
            )
            flows["other"].send()
            return [top.send(group[1:2]), flows["other"].parts[-1]]
        if level == len(plan) - 1:
            flows["step"] = flows["middle"].send(group)
        return ()

    held = exchange(0, part, plan, factors, True, True, beside_middle)
    middle = flows["middle"]
    other = flows["other"]
    sent = other.send([held[-1][1]])
    dv0, small0 = entered(
        functools.partial(adjoint_body, 0, plan, span, True),
        [pair_low, eight],
        held,
        [lens, g0, h0, v0, decay],
        [flows["step"], sent],
        weight=1 << 20,
    )
    part0, skip0, sums = run(
        functools.partial(input_body, 0, seqs, False),
        [whole, eight, ((2, 8, width), F32)],
        [dv0, dy0, x0, d0, stats0, bn_gain, bn_bias, w_in, skip],
        weight=1 << 20,
    )

    (small,) = run(small_body, [((16, width), F32)], [small0, skip0, sums, small1, skip1], limit=4)
    step = middle.send([part0])
    step = top.settle([step])
    top.fetch()
    last = Bulk(count, [u0], [dv0], [(0, 0, 0, 0)], [step], [small], weight=1 << 20)
    last.send()
    step = last.parts[-1]
    step = top.fetch([step])
    step = other.send([step])
    step = last.send([step])
    step = middle.send([step])
    step = other.send([step])
    step = top.fetch([step])
    step = middle.send([step])
    step = last.send([step])
    step = other.send([step])
    step = middle.settle([step])
    middle.fetch()
    step = last.send([step])
    step = other.settle([step])
    other.fetch()
    step = top.fetch([step])
    step = middle.fetch([step])
    step = last.send([step])
    step = other.fetch([step])
    step = middle.fetch([step])
    step = last.settle([step])
    last.fetch()
    step = other.fetch([step])
    step = last.fetch([step])
    step = middle.fetch([step])
    step = last.fetch([step])
    step = other.fetch([step])
    step = top.fetch([step])
    step = last.fetch([step])
    step = middle.fetch([step])
    grad_x, g_gain, g_bias, g_nu, g_phase, g_skip, running_out = run(
        functools.partial(finish_body, span),
        [seq_major] + [((2, width), F32)] * 2 + [((2, states), F32)] * 2
        + [((2, width), F32), ((2, 2, width), F32)],
        [last.total, lens, part0, x0, mask, bn_gain, decay, running, stats0, stats1, grads1],
        [step],
    )
    step = other.fetch([g_gain])
    step = last.fetch([step])
    g_glu, g_out = unpack(
        count,
        [top],
        [[(0, 1, 0), (0, 1, width), (1, 1, 0)]],
        [(2, width, 2 * width), (2, 2 * states, width)],
    )
    g_glu, g_out, g_in = unpack(
        count,
        [middle, other, last],
        [
            [(0, 0, 0), (0, 0, width)],
            [(2, 1, 0), (1, 0, 0)],
            [(2, 0, 0)],
        ],
        [(2, width, 2 * width), (2, 2 * states, width), (2, width, 2 * states)],
        [g_glu, g_out],
    )
    return (output, grad_x, g_gain, g_bias, g_in, g_nu, g_phase, g_out, g_skip, g_glu, running_out)


def solution(mesh):
    placed = (P(None, "tm", None), P(), P(None, "tm", None)) + (P(),) * 9
    return jax.shard_map(
        shards,
        mesh=mesh,
        in_specs=placed,
        out_specs=(P(None, "tm", None),) * 2 + (P(),) * 9,
        check_vma=False,
    )
```

```python
import functools
import math

import jax
import jax.numpy as jnp
from jax import lax
from jax.experimental import pallas as pl
from jax.experimental.pallas import tpu as pltpu
from jax.sharding import PartitionSpec as P

norm_epsilon = 1e-05
momentum = 0.1
inverse_root_two = 0.7071067811865476
density_scale = 0.3989422804014327
F32, BF16 = jnp.float32, jnp.bfloat16
LANES = 128
MIB = 1 << 20


def dot(left, right):
    return jnp.dot(left, right, preferred_element_type=F32)


def dot_tn(left, right):
    return lax.dot_general(left, right, (((0,), (0,)), ((), ())), preferred_element_type=F32)


def dot_nt(left, right):
    return lax.dot_general(left, right, (((1,), (1,)), ((), ())), preferred_element_type=F32)


def run(body, outs, operands, after=(), scratch=(), limit=24, weight=1 << 33):
    vmem = pl.BlockSpec(memory_space=pltpu.VMEM)
    anywhere = pl.BlockSpec(memory_space=pl.ANY)
    first, second = len(operands), len(operands) + len(after)

    def kernel(*refs):
        body(*refs[:first], *refs[second:])

    return pl.pallas_call(
        kernel,
        out_shape=[jax.ShapeDtypeStruct(shape, dtype) for shape, dtype in outs],
        in_specs=[vmem] * len(operands) + [anywhere] * len(after),
        out_specs=[vmem] * len(outs),
        scratch_shapes=list(scratch),
        compiler_params=pltpu.CompilerParams(vmem_limit_bytes=limit * MIB),
        cost_estimate=pl.CostEstimate(flops=weight, bytes_accessed=0, transcendentals=0),
    )(*operands, *after)


def radices(count):
    out = []
    while count > 1:
        radix = 2 if not out or count % 4 else 4
        out.append(radix)
        count //= radix
    return out


def stages(count):
    stride, out = 1, []
    for radix in radices(count):
        out.append((radix, stride))
        stride *= radix
    return out


def swap(value, stride, mask):
    count = lax.axis_size("tm")
    return lax.ppermute(value, "tm", [(i, i ^ (stride * mask)) for i in range(count)])


def group_of(value, radix, stride):
    return [value] + [swap(value, stride, mask) for mask in range(1, radix)]


def place_in(radix, stride):
    return lax.rem(lax.div(lax.axis_index("tm"), stride), radix)


def rows_to_tile(first, second):
    pieces = [
        row[:, j : j + LANES] for row in (first, second) for j in range(0, row.shape[1], LANES)
    ]
    return jnp.concatenate(pieces, axis=0)


def tile_to_rows(tile):
    half = tile.shape[0] // 2
    return [
        jnp.concatenate([tile[base + j : base + j + 1, :] for j in range(half)], axis=1)
        for base in (0, half)
    ]


def spread(ref, first, second):
    ref[...] = jnp.broadcast_to(rows_to_tile(first, second)[None], ref.shape)


def gathered(ref):
    return tile_to_rows(jnp.sum(ref[...], axis=0))


def everywhere(tiles):
    return lax.all_to_all(tiles, "tm", 0, 0)


def mul(ar, ai, br, bi):
    return ar * br - ai * bi, ar * bi + ai * br


def members(refs, place, buffer):
    for offset, ref in enumerate(refs):
        buffer[jnp.bitwise_xor(place, offset)] = ref[...]


def pass_through(k, buffer, factor, place, state, backward, conj):
    radix, _, width = buffer.shape
    states = width // 2
    if state is None:
        zero = jnp.zeros(buffer.shape[1:-1] + (states,), F32)
        state = (zero, zero)
    entering = state
    for member in range(radix - 1, -1, -1) if backward else range(radix):
        entering = tuple(jnp.where(place == member, s, e) for s, e in zip(state, entering))
        fr, fi = factor[k, member, :, :states], factor[k, member, :, states:]
        moved = mul(fr, -fi if conj else fi, *state)
        state = (moved[0] + buffer[member, :, :states], moved[1] + buffer[member, :, states:])
    return entering, state


def total_body(k, radix, stride, backward, conj, *refs):
    factor, out, buffer = refs[radix:]
    place = place_in(radix, stride)
    members(refs[:radix], place, buffer)
    _, (re, im) = pass_through(k, buffer, factor, place, None, backward, conj)
    states = re.shape[1]
    out[:, :states] = re
    out[:, states:] = im


def group_total(k, group, level, plan, factors, backward, conj, after=()):
    radix, stride = plan[level]
    shape = group[0].shape
    (total,) = run(
        functools.partial(total_body, k, radix, stride, backward, conj),
        [(shape, F32)],
        list(group) + [factors[level]],
        after,
        [pltpu.VMEM((radix,) + shape, F32)],
        limit=4,
    )
    return total


def exchange(k, summary, plan, factors, backward, conj, between=None):
    held = []
    value = summary
    for level, (radix, stride) in enumerate(plan):
        group = group_of(value, radix, stride)
        held.append(group)
        if level + 1 < len(plan):
            after = between(level, group) if between else ()
            value = group_total(k, group, level, plan, factors, backward, conj, after)
            if between and level + 2 == len(plan):
                between(level + 1, [value])
    return held


def entry_operands(held, factors):
    return [value for group in held for value in group] + list(factors)


def entry_scratch(plan, shape):
    return [pltpu.VMEM((radix,) + shape, F32) for radix, _ in plan]


def entering_state(k, plan, refs, buffers, backward, conj):
    total = sum(radix for radix, _ in plan)
    values, factors = refs[:total], refs[total:]
    start, groups = 0, []
    for radix, _ in plan:
        groups.append(values[start : start + radix])
        start += radix
    state = None
    for level in range(len(plan) - 1, -1, -1):
        place = place_in(*plan[level])
        members(groups[level], place, buffers[level])
        state, _ = pass_through(k, buffers[level], factors[level], place, state, backward, conj)
    return state


CHUNKS = 32
LEVELS = CHUNKS.bit_length() - 1


def partners(count):
    order = [(1 << b, 1 << b) for b in range(count.bit_length() - 1)]
    if len(order) > 2:
        order[1], order[2] = (2, 4), (4, 2)
    return order


def with_partner(value, bits):
    even, odd = bits
    count = lax.axis_size("tm")
    return lax.ppermute(value, "tm", [(i, i ^ (odd if i & 1 else even)) for i in range(count)])


def own_chunk(count, other_core=False):
    here = lax.axis_index("tm")
    if other_core:
        here = jnp.bitwise_xor(here, 1)
    own = 0
    for even, odd in partners(count)[:LEVELS]:
        taken = jnp.where(jnp.bitwise_and(here, 1) == 1, here & odd, here & even)
        own = own * 2 + jnp.where(taken != 0, 1, 0)
    return own


def slots(level):
    return (CHUNKS >> (level + 1), CHUNKS >> level) if level < LEVELS else (0, 1)


def outer_body(count, pairs, n_left, n_right, n_extra, *refs):
    lefts, rights = refs[:n_left], refs[n_left : n_left + n_right]
    extra, outs = refs[n_left + n_right :][:n_extra], refs[n_left + n_right + n_extra : -len(pairs)]
    products = refs[-len(pairs) :]
    if extra:
        outs[0][-extra[0].shape[0] :, :] = extra[0][...]
    owns = own_chunk(count), own_chunk(count, True)
    half = CHUNKS // 2
    for q, (left, row, right, column) in enumerate(pairs):
        product = products[q]
        span = rights[right].shape[0]
        wide_left = lefts[left].shape[1]
        part = wide_left // CHUNKS
        width = product.shape[1]
        product[...] = dot_tn(
            lefts[left][row : row + span, :], rights[right][:, column : column + width]
        )
        for level in range(LEVELS + 1):
            low, high = slots(level)
            for slot in range(low, high):
                chunk = jnp.bitwise_xor(owns[slot // half], slot % half)
                chunk = pl.multiple_of(chunk * part, part)
                place = ((slot - low) * len(pairs) + q) * part
                outs[level][place : place + part, :] = product[pl.ds(chunk, part), :]


def add_body(low, extra, *refs):
    out = refs[-1]
    rows = out.shape[0] - extra
    total = refs[0][:rows, :]
    for ref in refs[1 : -2 if extra else -1]:
        total += ref[low : low + rows, :]
    out[:rows, :] = total
    if extra:
        mine, other = refs[-2], refs[-3]
        out[rows:, :] = mine[-extra:, :] + other[-extra:, :]


def spokes_body(rows, extra, *refs):
    near, far = refs[:2]
    received, mine, outs = refs[2:-4], refs[-4], refs[-3:]
    for slot, out in enumerate(outs, 1):
        total = near[...] if slot == 1 else far[(slot - 2) * rows : (slot - 1) * rows, :]
        for ref in received:
            total += ref[slot * rows : (slot + 1) * rows, :]
        out[:rows, :] = total
        if extra:
            out[rows:, :] = mine[-extra:, :] + received[-1][-extra:, :]


def hub_body(rows, extra, *refs):
    kept, received, mine, spokes, out = refs[0], refs[1:-5], refs[-5], refs[-4:-1], refs[-1]
    total = kept[...]
    for ref in received + spokes:
        total += ref[:rows, :]
    out[:rows, :] = total
    if extra:
        total = mine[-extra:, :]
        for ref in spokes:
            total += ref[-extra:, :]
        out[rows:, :] = total


def join_body(*refs):
    out = refs[-1]
    rows = refs[0].shape[0]
    for j, ref in enumerate(refs[:-1]):
        out[j * rows : (j + 1) * rows] = ref[...]


class Bulk:
    def __init__(self, count, lefts, rights, pairs, after=(), extra=(), hub=False, weight=1 << 33):
        self.hub = hub
        self.bits = partners(count)
        self.extra = extra[0].shape[0] if extra else 0
        width = 512
        part = lefts[0].shape[1] // CHUNKS
        self.rows = part * len(pairs)
        outs = [((self.rows * (hi - lo), width), F32) for lo, hi in map(slots, range(LEVELS + 1))]
        outs[0] = ((outs[0][0][0] + self.extra, width), F32)
        self.parts = run(
            functools.partial(outer_body, count, pairs, len(lefts), len(rights), len(extra)),
            outs,
            list(lefts) + list(rights) + list(extra),
            after,
            [pltpu.VMEM((lefts[pair[0]].shape[1], width), F32) for pair in pairs],
            limit=16,
            weight=weight,
        )
        self.received = []
        self.sent = None

    def reduced(self, level, after=()):
        low, high = slots(level)
        if not self.received:
            return self.parts[level]
        (total,) = run(
            functools.partial(add_body, low * self.rows, self.extra),
            [((self.rows * (high - low) + self.extra, self.parts[level].shape[1]), F32)],
            [self.parts[level]] + self.received + ([self.sent] if self.extra else []),
            after,
            limit=8,
        )
        return total

    def send(self, after=()):
        level = len(self.received)
        if self.hub and level == LEVELS - 2:
            shape = (self.rows + self.extra, self.parts[LEVELS].shape[1])
            sent = run(
                functools.partial(spokes_body, self.rows, self.extra),
                [(shape, F32)] * 3,
                [self.parts[LEVELS - 1], self.parts[LEVELS - 2]] + self.received + [self.sent],
                after,
                limit=8,
            )
            self.sent, self.spokes = sent[0], self.with_partners(sent)
            return self.sent
        self.sent = self.reduced(level, after)
        self.received.append(with_partner(self.sent, self.bits[level]))
        return self.sent

    def with_partners(self, values):
        far, near = self.bits[LEVELS - 2][0], self.bits[LEVELS - 1][0]
        masks = (near, far, near | far)
        return [swap(value, 1, mask) for value, mask in zip(values, masks)]

    def settle(self, after=()):
        if self.hub:
            (value,) = run(
                functools.partial(hub_body, self.rows, self.extra),
                [((self.rows + self.extra, self.parts[LEVELS].shape[1]), F32)],
                [self.parts[LEVELS]] + self.received + [self.sent] + self.spokes,
                after,
                limit=8,
            )
        else:
            value = self.reduced(LEVELS, after)
        for even, odd in self.bits[LEVELS:]:
            other = with_partner(value, (even, odd))
            (value,) = run(
                functools.partial(add_body, 0, 0), [(value.shape, F32)], [value, other], limit=4
            )
        self.total, self.value, self.level = value, value[: self.rows], LEVELS - 1
        return value

    def fetch(self, after=()):
        if self.level < LEVELS - 1:
            parts = [self.value] + self.others
            (self.value,) = run(
                join_body,
                [((len(parts) * self.value.shape[0], self.value.shape[1]), F32)],
                parts,
                after,
                limit=8,
            )
        if self.hub and self.level == LEVELS - 1:
            self.others = self.with_partners([self.value] * 3)
            self.level -= 2
        else:
            self.others = [with_partner(self.value, self.bits[self.level])]
            self.level -= 1
        return self.value


def unpack_body(count, width, layout, n_into, *refs):
    outs, sem = refs[2 * len(layout) + n_into : -1], refs[-1]
    owns = own_chunk(count), own_chunk(count, True)
    copies = []
    for piece, places in enumerate(layout):
        near, far = refs[2 * piece], refs[2 * piece + 1]
        for source, own in zip((near, far), owns):
            for j in range(CHUNKS // 2):
                chunk = jnp.bitwise_xor(own, j)
                part = source.shape[0] // (CHUNKS // 2) // len(places)
                for q, (out, k, column) in enumerate(places):
                    place = (j * len(places) + q) * part
                    rows = pl.ds(pl.multiple_of(chunk * part, part), part)
                    copies.append(
                        pltpu.make_async_copy(
                            source.at[pl.ds(place, part), :],
                            outs[out].at[k, rows, pl.ds(column, width)],
                            sem,
                        )
                    )
    for copy in copies:
        copy.start()
    for copy in copies:
        copy.wait()


def unpack(count, bulks, layout, shapes, into=()):
    operands = [value for bulk in bulks for value in (bulk.value, bulk.others[0])]
    anywhere = pl.BlockSpec(memory_space=pl.ANY)
    return pl.pallas_call(
        functools.partial(unpack_body, count, operands[0].shape[1], layout, len(into)),
        out_shape=[jax.ShapeDtypeStruct(shape, F32) for shape in shapes],
        in_specs=[anywhere] * (len(operands) + len(into)),
        out_specs=[anywhere] * len(shapes),
        scratch_shapes=[pltpu.SemaphoreType.DMA],
        input_output_aliases={len(operands) + j: j for j in range(len(into))},
        compiler_params=pltpu.CompilerParams(vmem_limit_bytes=4 * MIB),
    )(*operands, *into)


def steps(span, backward, body, start, unroll=None):
    def one(k, carry):
        return body(span - 1 - k if backward else k, carry)

    return lax.fori_loop(0, span, one, start, unroll=unroll or span)


def pieces(rows, step, backward=False):
    starts = range(0, rows, step)
    return reversed(starts) if backward else starts


def at(t, seqs):
    return pl.ds(pl.multiple_of(t * seqs, seqs), seqs)


def state_scan(v_ref, rel, lr, li, start, span, backward, keep=None):
    seqs, states = lr.shape

    def body(t, carry):
        re, im = carry
        vr, vi = v_ref[at(t, seqs), :states], v_ref[at(t, seqs), states:]
        next_re, next_im = mul(lr, li, re, im)
        live = rel > t
        re, im = jnp.where(live, next_re + vr, re), jnp.where(live, next_im + vi, im)
        if keep is not None:
            keep(t, re, im)
        return re, im

    return steps(span, backward, body, start)


def adjoint_scan(g_ref, rel, lr, li, start, span, backward, use=None, extra=(), unroll=None):
    seqs, states = lr.shape

    def body(t, carry):
        (re, im), kept = carry
        ar, ai = g_ref[at(t, seqs), :states] + re, g_ref[at(t, seqs), states:] + im
        live = rel > t
        if use is not None:
            kept = use(t, ar, ai, live, kept)
        next_re, next_im = mul(lr, -li, ar, ai)
        return (jnp.where(live, next_re, ar), jnp.where(live, next_im, ai)), kept

    return steps(span, backward, body, (start, extra), unroll)


def wide(ref, row, shape):
    return jnp.broadcast_to(ref[row : row + 1, :], shape)


def to_time_major(piece):
    seqs, span, width = piece.shape
    return jnp.swapaxes(piece, 0, 1).reshape(span * seqs, width)


def from_time_major(rows, seqs):
    return jnp.swapaxes(rows.reshape(-1, seqs, rows.shape[-1]), 0, 1)


def lane_tiled(column, width):
    return jnp.concatenate([column] * (width // LANES), axis=1)


def gelu_parts(y):
    cdf = 0.5 * (1.0 + lax.erf(y * inverse_root_two))
    pdf = jnp.exp(-0.5 * y * y) * density_scale
    return y * cdf, cdf + y * pdf


sigmoid = jax.nn.sigmoid


CHUNK = 64
PIECE = 8


def prepare_body(span, lengths_any, x_any, nu_any, phase_any, *outs):
    lens_ref, sums_ref, tm_ref, mask_ref, decay_ref = outs[:5]
    lengths_ref, x_ref, nu_ref, phase_ref, sems = outs[5:]
    seqs, _, width = x_ref.shape
    states = nu_ref.shape[-1]
    copies = [
        pltpu.make_async_copy(
            x_any.at[:, pl.ds(t0, PIECE), :], x_ref.at[:, pl.ds(t0, PIECE), :], sems.at[t0 // PIECE]
        )
        for t0 in range(0, span, PIECE)
    ]
    small = [
        pltpu.make_async_copy(nu_any, nu_ref, sems.at[len(copies)]),
        pltpu.make_async_copy(phase_any, phase_ref, sems.at[len(copies) + 1]),
        pltpu.make_async_copy(lengths_any, lengths_ref, sems.at[len(copies) + 2]),
    ]
    for copy in small + copies:
        copy.start()
    for copy in small:
        copy.wait()
    here = lax.axis_index("tm")
    row = lax.broadcasted_iota(jnp.int32, (seqs, LANES), 0)
    lens = jnp.zeros((seqs, LANES), jnp.int32)
    for seq in range(seqs):
        lens = jnp.where(row == seq, lengths_ref[seq], lens)
    lens_ref[...] = lens
    rel = lens - here * span
    rate = jnp.exp(nu_ref[...])
    radius = jnp.exp(-rate)
    angle = phase_ref[...]
    cosine, sine = jnp.cos(angle), jnp.sin(angle)
    gamma = jnp.sqrt(one_less_exp(2.0 * rate))
    for row, value in enumerate((radius * cosine, radius * sine, gamma, rate, radius, cosine, sine)):
        for k in range(2):
            decay_ref[k, row : row + 1, :] = value[k : k + 1, :]
    first = jnp.zeros((seqs, width), F32)
    second = jnp.zeros((seqs, width), F32)
    for t0 in range(0, span, PIECE):
        copies[t0 // PIECE].wait()
        piece = jnp.swapaxes(x_ref[:, t0 : t0 + PIECE, :], 0, 1)
        for j in range(PIECE):
            rows = piece[j]
            mask = jnp.where(rel > t0 + j, 1.0, 0.0)
            place = slice((t0 + j) * seqs, (t0 + j + 1) * seqs)
            mask_ref[place, :] = mask
            tm_ref[place, :] = rows
            live = rows * lane_tiled(mask, width)
            first += live
            second += live * rows
    spread(sums_ref, jnp.sum(first, 0, keepdims=True), jnp.sum(second, 0, keepdims=True))


def factors_body(plan, span, lens_ref, decay_ref, *factor_refs):
    seqs, states = lens_ref.shape[0], decay_ref.shape[-1]
    here = lax.axis_index("tm")
    lens = lens_ref[...]
    for k in range(2):
        for level, (radix, stride) in enumerate(plan):
            base = lax.div(here, radix * stride) * (radix * stride)
            for member in range(radix):
                start = (base + member * stride) * span
                count = jnp.concatenate(
                    [jnp.clip(lens - start, 0, stride * span)] * (states // LANES), axis=1
                )
                power = (decay_ref[k, 0:1, :], decay_ref[k, 1:2, :])
                re, im = jnp.ones((seqs, states), F32), jnp.zeros((seqs, states), F32)
                for bit in range((span * stride).bit_length()):
                    taken = jnp.bitwise_and(count, 1 << bit) != 0
                    next_re, next_im = mul(re, im, *power)
                    re, im = jnp.where(taken, next_re, re), jnp.where(taken, next_im, im)
                    power = mul(*power, *power)
                factor_refs[level][k, member, :, :states] = re
                factor_refs[level][k, member, :, states:] = im


def one_less_exp(x):
    total = 1.0
    for n in range(8, 1, -1):
        total = 1.0 - total * x * (1.0 / n)
    return total * x


def relative(lens_ref, span, states):
    rel = lens_ref[...] - lax.axis_index("tm") * span
    return jnp.concatenate([rel] * (states // LANES), axis=1)


def token_scale(lens_ref):
    return 1.0 / jnp.sum(lens_ref[:, 0:1].astype(F32), axis=0, keepdims=True)


def project_body(
    k, span, backward, lens_ref, sums_ref, x_ref, gain_ref, bias_ref, w_ref, decay_ref,
    u_ref, v_ref, stats_ref, summary_ref,
):
    seqs = lens_ref.shape[0]
    states = decay_ref.shape[-1]
    total, squares = gathered(sums_ref)
    scale = token_scale(lens_ref)
    mean = total * scale
    var = squares * scale - mean * mean
    rstd = lax.rsqrt(var + norm_epsilon)
    stats_ref[0:1, :] = mean
    stats_ref[1:2, :] = var
    stats_ref[2:3, :] = rstd
    stats_ref[3:4, :] = rstd * gain_ref[k : k + 1, :]
    slope = rstd * gain_ref[k : k + 1, :]
    bias = bias_ref[k : k + 1, :]
    step = 16 * seqs
    for r in pieces(span * seqs, step, backward):
        u = ((x_ref[r : r + step, :] - mean) * slope + bias).astype(BF16)
        u_ref[r : r + step, :] = u
        v_ref[r : r + step, :] = dot(u, w_ref[k])
    shape = (seqs, states)
    rel = relative(lens_ref, span, states)
    lr, li = wide(decay_ref.at[k], 0, shape), wide(decay_ref.at[k], 1, shape)
    zero = jnp.zeros(shape, F32)
    re, im = state_scan(v_ref, rel, lr, li, (zero, zero), span, backward)
    summary_ref[:, :states] = re
    summary_ref[:, states:] = im


def rebuild_states(k, plan, span, backward, refs, buffers, rel, v_ref, decay_ref, h_ref):
    seqs, states = rel.shape
    lr, li, gamma = (wide(decay_ref.at[k], row, rel.shape) for row in range(3))
    start = entering_state(k, plan, refs, buffers, backward, False)

    lead = 0 if backward else 1

    def keep(t, re, im):
        h_ref[at(t + lead, seqs), :states] = (re * gamma).astype(BF16)
        h_ref[at(t + lead, seqs), states:] = (im * gamma).astype(BF16)

    keep(span if backward else -1, *start)
    state_scan(v_ref, rel, lr, li, start, span, backward, keep)


def forward_body(
    k, plan, span, exch, lens_ref, v_ref, x_ref, mask_ref, stats_ref, bias_ref,
    decay_ref, w_out_ref, skip_ref, w_glu_ref,
    out_ref, h_ref, act_ref, slope_ref, gate_ref, value_ref, sums_ref, buffers,
):
    seqs = lens_ref.shape[0]
    width = x_ref.shape[1]
    states = decay_ref.shape[-1]
    rel = relative(lens_ref, span, states)
    rebuild_states(k, plan, span, False, exch, buffers, rel, v_ref, decay_ref, h_ref)
    mean, scale = stats_ref[0:1, :], stats_ref[3:4, :]
    bias, skip = bias_ref[k : k + 1, :], skip_ref[k : k + 1, :]
    step = 64 * seqs
    first = jnp.zeros((8, width), F32)
    second = jnp.zeros((8, width), F32)
    for r in pieces(span * seqs, step, False):
        x = x_ref[r : r + step, :]
        u = (x - mean) * scale + bias
        y = dot(h_ref[r + seqs : r + seqs + step, :], w_out_ref[k]) + skip * u
        act, slope = gelu_parts(y)
        act = act.astype(BF16)
        act_ref[r : r + step, :] = act
        slope_ref[r : r + step, :] = slope.astype(BF16)
        z = dot(act, w_glu_ref[k])
        value, gate = z[:, :width], sigmoid(z[:, width:])
        gated = value * gate
        out = x + gated
        out_ref[r : r + step, :] = out
        gate_ref[r : r + step, :] = gate.astype(BF16)
        value_ref[r : r + step, :] = (gated * (1.0 - gate)).astype(BF16)
        live = out * lane_tiled(mask_ref[r : r + step, :], width)
        first += jnp.sum(live.reshape(-1, 8, width), 0)
        second += jnp.sum((live * out).reshape(-1, 8, width), 0)
    spread(sums_ref, jnp.sum(first, 0, keepdims=True), jnp.sum(second, 0, keepdims=True))


def back_rows(k, r, step, dza, dzb, slope, width, w_glu_ref, w_out_ref, dz_ref, dy_ref, g_ref):
    dza, dzb = dza.astype(BF16), dzb.astype(BF16)
    dz_ref[r : r + step, :width] = dza
    dz_ref[r : r + step, width:] = dzb
    w = w_glu_ref[k]
    dact = dot_nt(dza, w[:, :width]) + dot_nt(dzb, w[:, width:])
    dy = (dact * slope).astype(BF16)
    dy_ref[r : r + step, :] = dy
    g_ref[r : r + step, :] = dot_nt(dy, w_out_ref[k])


def local_adjoint(k, span, backward, rel, g_ref, decay_ref, summary_ref, unroll=None):
    seqs, states = rel.shape
    lr, li = wide(decay_ref.at[k], 0, rel.shape), wide(decay_ref.at[k], 1, rel.shape)
    zero = jnp.zeros(rel.shape, F32)
    (re, im), _ = adjoint_scan(g_ref, rel, lr, li, (zero, zero), span, backward, unroll=unroll)
    summary_ref[:, :states] = re
    summary_ref[:, states:] = im


def turn_body(
    k, plan, span, exch, lens_ref, v_ref, x_ref, cot_ref, stats_ref, bias_ref,
    decay_ref, w_out_ref, skip_ref, w_glu_ref,
    out_ref, h_ref, act_ref, dz_ref, dy_ref, g_ref, summary_ref, buffers,
):
    seqs = lens_ref.shape[0]
    width = x_ref.shape[1]
    states = decay_ref.shape[-1]
    rel = relative(lens_ref, span, states)
    rebuild_states(k, plan, span, True, exch, buffers, rel, v_ref, decay_ref, h_ref)
    mean, scale = stats_ref[0:1, :], stats_ref[3:4, :]
    bias, skip = bias_ref[k : k + 1, :], skip_ref[k : k + 1, :]
    step = 64 * seqs
    for r in pieces(span * seqs, step, True):
        t0 = r // seqs
        x = x_ref[r : r + step, :]
        u = (x - mean) * scale + bias
        y = dot(h_ref[r : r + step, :], w_out_ref[k]) + skip * u
        act, slope = gelu_parts(y)
        act = act.astype(BF16)
        act_ref[r : r + step, :] = act
        z = dot(act, w_glu_ref[k])
        value, gate = z[:, :width], sigmoid(z[:, width:])
        gated = value * gate
        out_ref[:, t0 : t0 + 64, :] = from_time_major(x + gated, seqs)
        d = to_time_major(cot_ref[:, t0 : t0 + 64, :])
        back_rows(
            k, r, step, d * gate, d * (gated * (1.0 - gate)), slope, width,
            w_glu_ref, w_out_ref, dz_ref, dy_ref, g_ref,
        )
    local_adjoint(k, span, False, rel, g_ref, decay_ref, summary_ref)


def back_body(
    k, span, backward, lens_ref, sums_ref, part_ref, x_ref, mask_ref, stats_ref, slope_ref,
    gate_ref, value_ref, gain_ref, decay_ref, w_out_ref, w_glu_ref,
    d_ref, dz_ref, dy_ref, g_ref, grads_ref, summary_ref,
):
    seqs = lens_ref.shape[0]
    width = x_ref.shape[1]
    states = decay_ref.shape[-1]
    rel = relative(lens_ref, span, states)
    bias_grad, gain_grad = gathered(sums_ref)
    grads_ref[0:1, :] = gain_grad
    grads_ref[1:2, :] = bias_grad
    shift, tilt = input_terms(
        k + 1, token_scale(lens_ref), bias_grad, gain_grad, stats_ref, gain_ref
    )
    mean = stats_ref[0:1, :]
    step = 64 * seqs
    for r in pieces(span * seqs, step, backward):
        live = lane_tiled(mask_ref[r : r + step, :], width)
        d = part_ref[r : r + step, :] + live * (shift + tilt * (x_ref[r : r + step, :] - mean))
        d_ref[r : r + step, :] = d
        back_rows(
            k, r, step, d * gate_ref[r : r + step, :].astype(F32),
            d * value_ref[r : r + step, :].astype(F32), slope_ref[r : r + step, :].astype(F32), width,
            w_glu_ref, w_out_ref, dz_ref, dy_ref, g_ref,
        )
    local_adjoint(k, span, backward, rel, g_ref, decay_ref, summary_ref, 8)


def input_terms(k, scale, bias_grad, gain_grad, stats_ref, gain_ref):
    rstd = stats_ref[2:3, :]
    gain = gain_ref[k : k + 1, :]
    return -rstd * gain * bias_grad * scale, -rstd * rstd * gain * gain_grad * scale


def adjoint_body(
    k, plan, span, backward, exch, lens_ref, g_ref, h_ref, v_ref, decay_ref, dv_ref, small_ref, buffers
):
    seqs = lens_ref.shape[0]
    states = decay_ref.shape[-1]
    rel = relative(lens_ref, span, states)
    lr, li, gamma = (wide(decay_ref.at[k], row, rel.shape) for row in range(3))
    start = entering_state(k, plan, exch, buffers, backward, True)
    before = 0 if backward else 1

    def use(t, ar, ai, live, kept):
        ar, ai = jnp.where(live, ar, 0.0), jnp.where(live, ai, 0.0)
        dv_ref[at(t, seqs), :states] = (ar * gamma).astype(BF16)
        dv_ref[at(t, seqs), states:] = (ai * gamma).astype(BF16)
        pr = h_ref[at(t + before, seqs), :states].astype(F32)
        pi = h_ref[at(t + before, seqs), states:].astype(F32)
        vr, vi = v_ref[at(t, seqs), :states], v_ref[at(t, seqs), states:]
        return (
            kept[0] + (ar * pr + ai * pi),
            kept[1] + (ai * pr - ar * pi),
            kept[2] + (ar * vr + ai * vi),
        )

    zero = jnp.zeros(rel.shape, F32)
    _, kept = adjoint_scan(g_ref, rel, lr, li, start, span, backward, use, (zero, zero, zero))
    small_ref[...] = jnp.zeros_like(small_ref)
    for j in range(2):
        small_ref[0:1, j * states : (j + 1) * states] = jnp.sum(kept[j], 0, keepdims=True)
    small_ref[1:2, :states] = jnp.sum(kept[2], 0, keepdims=True)


def input_body(
    k, seqs, seq_major, dv_ref, dy_ref, x_ref, d_ref, stats_ref, gain_ref, bias_ref, w_in_ref, skip_ref,
    part_ref, skip_grad_ref, sums_ref,
):
    width = x_ref.shape[1]
    mean, scale, rstd = stats_ref[0:1, :], stats_ref[3:4, :], stats_ref[2:3, :]
    gain, bias, skip = (ref[k : k + 1, :] for ref in (gain_ref, bias_ref, skip_ref))
    step = CHUNK * seqs
    first = jnp.zeros((8, width), F32)
    second = jnp.zeros((8, width), F32)
    third = jnp.zeros((8, width), F32)
    for r in range(0, x_ref.shape[0], step):
        xhat = (x_ref[r : r + step, :] - mean) * rstd
        dy = dy_ref[r : r + step, :].astype(F32)
        du = dot_nt(dv_ref[r : r + step, :], w_in_ref[k]) + dy * skip
        first += jnp.sum(du.reshape(-1, 8, width), 0)
        second += jnp.sum((du * xhat).reshape(-1, 8, width), 0)
        third += jnp.sum((dy * (xhat * gain + bias)).reshape(-1, 8, width), 0)
        if seq_major:
            d = to_time_major(d_ref[:, r // seqs : r // seqs + CHUNK, :])
        else:
            d = d_ref[r : r + step, :]
        part_ref[r : r + step, :] = d + du * scale
    skip_grad_ref[...] = third
    if seq_major:
        spread(sums_ref, jnp.sum(first, 0, keepdims=True), jnp.sum(second, 0, keepdims=True))
    else:
        sums_ref[0] = first
        sums_ref[1] = second


def small_body(small0, skip0, sums0, small1, skip1, out):
    out[...] = jnp.zeros_like(out)
    rows = [small0[0:1, :], small0[1:2, :], skip0[...], sums0[0], sums0[1]]
    for row, value in enumerate(rows):
        out[row : row + 1, :] = jnp.sum(value, 0, keepdims=True)
    for row, value in enumerate([small1[0:1, :], small1[1:2, :], skip1[...]]):
        out[8 + row : 9 + row, :] = jnp.sum(value, 0, keepdims=True)


def finish_body(
    span, total_ref, lens_ref, part_ref, x_ref, mask_ref, gain_ref, decay_ref, running_ref, stats0_ref,
    stats1_ref, grads_ref, out_ref, g_gain_ref, g_bias_ref, nu_ref, phase_ref, skip_ref, run_ref,
):
    stats_refs = (stats0_ref, stats1_ref)
    small = total_ref[total_ref.shape[0] - 16 :, :]
    states = decay_ref.shape[-1]
    count = jnp.sum(lens_ref[:, 0:1].astype(F32), axis=0, keepdims=True)
    for k in range(2):
        _, _, gamma, rate, radius, cosine, sine = (decay_ref[k, j : j + 1, :] for j in range(7))
        sum_re, sum_im = small[8 * k : 8 * k + 1, :states], small[8 * k : 8 * k + 1, states:]
        g_gamma = small[8 * k + 1 : 8 * k + 2, :states]
        nu_ref[k : k + 1, :] = (sum_re * cosine + sum_im * sine) * (
            -radius * rate
        ) + g_gamma * rate * radius * radius / gamma
        phase_ref[k : k + 1, :] = radius * (sum_im * cosine - sum_re * sine)
        skip_ref[k : k + 1, :] = small[8 * k + 2 : 8 * k + 3, :]
        mean, var = stats_refs[k][0:1, :], stats_refs[k][1:2, :]
        run_ref[k, 0:1, :] = (1.0 - momentum) * running_ref[k, 0:1, :] + momentum * mean
        run_ref[k, 1:2, :] = (1.0 - momentum) * running_ref[k, 1:2, :] + momentum * var * (
            count / (count - 1.0)
        )
    bias_grad, gain_grad = small[3:4, :], small[4:5, :]
    g_gain_ref[0:1, :], g_gain_ref[1:2, :] = gain_grad, grads_ref[0:1, :]
    g_bias_ref[0:1, :], g_bias_ref[1:2, :] = bias_grad, grads_ref[1:2, :]
    seqs = out_ref.shape[0]
    width = x_ref.shape[1]
    shift, tilt = input_terms(0, 1.0 / count, bias_grad, gain_grad, stats_refs[0], gain_ref)
    mean = stats_refs[0][0:1, :]
    step = CHUNK * seqs
    for r in range(0, span * seqs, step):
        live = lane_tiled(mask_ref[r : r + step, :], width)
        d = part_ref[r : r + step, :] + live * (shift + tilt * (x_ref[r : r + step, :] - mean))
        out_ref[:, r // seqs : r // seqs + CHUNK, :] = from_time_major(d, seqs)


def with_entry(body, plan):
    def wrapped(*refs):
        n_exch = sum(radix for radix, _ in plan) + len(plan)
        body(refs[:n_exch], *refs[n_exch : -len(plan)], refs[-len(plan) :])

    return wrapped


def shards(
    inputs, lengths, cotangent, bn_gain, bn_bias, running, w_in, nu_log, phase, w_out, skip, w_glu
):
    seqs, span, width = inputs.shape
    states = nu_log.shape[1]
    count = lax.axis_size("tm")
    rows = span * seqs
    plan = stages(count)

    tile = ((count, 2 * width // LANES, LANES), F32)
    whole, whole_low = ((rows, width), F32), ((rows, width), BF16)
    pair, pair_low = ((rows, 2 * states), F32), ((rows, 2 * states), BF16)
    double_low = ((rows, 2 * width), BF16)
    held_low = ((rows + seqs, 2 * states), BF16)
    summary = ((seqs, 2 * states), F32)
    eight = ((8, width), F32)
    seq_major = ((seqs, span, width), F32)
    buffers = entry_scratch(plan, summary[0])

    in_hbm = pl.BlockSpec(memory_space=pltpu.HBM)
    outs = [((seqs, LANES), jnp.int32), tile, whole, ((rows, LANES), F32), ((2, 8, states), F32)]
    prepared = pl.pallas_call(
        functools.partial(prepare_body, span),
        out_shape=[jax.ShapeDtypeStruct(shape, dtype) for shape, dtype in outs],
        in_specs=[in_hbm] * 4,
        out_specs=[pl.BlockSpec(memory_space=pltpu.VMEM)] * len(outs),
        scratch_shapes=[
            pltpu.SMEM(lengths.shape, jnp.int32),
            pltpu.VMEM(inputs.shape, F32),
            pltpu.VMEM(nu_log.shape, F32),
            pltpu.VMEM(phase.shape, F32),
            pltpu.SemaphoreType.DMA((span // PIECE + 3,)),
        ],
        compiler_params=pltpu.CompilerParams(vmem_limit_bytes=24 * MIB),
    )(*(pltpu.with_memory_space_constraint(a, pltpu.HBM) for a in (lengths, inputs, nu_log, phase)))
    lens, sums, x0, mask, decay = prepared[:5]

    def project(k, sums, x):
        return run(
            functools.partial(project_body, k, span, k == 1),
            [whole_low, pair, eight, summary],
            [lens, everywhere(sums), x, bn_gain, bn_bias, w_in, decay],
        )

    def entered(body, outs, held, operands, after=(), limit=24, weight=1 << 33):
        operands = entry_operands(held, factors) + operands
        return run(with_entry(body, plan), outs, operands, after, buffers, limit, weight)

    u0, v0, stats0, part = project(0, sums, x0)
    factors = run(
        functools.partial(factors_body, plan, span),
        [((2, radix) + summary[0], F32) for radix, _ in plan],
        [lens, decay],
        [part],
    )
    held = exchange(0, part, plan, factors, False, False)
    x1, h0, act0, slope0, gate0, value0, sums = entered(
        functools.partial(forward_body, 0, plan, span),
        [whole, held_low, whole_low, whole_low, whole_low, whole_low, tile],
        held,
        [lens, v0, x0, mask, stats0, bn_bias, decay, w_out, skip, w_glu],
    )
    u1, v1, stats1, part = project(1, sums, x1)
    held = exchange(1, part, plan, factors, True, False)
    output, h1, act1, dz1, dy1, g1, part = entered(
        functools.partial(turn_body, 1, plan, span),
        [seq_major, held_low, whole_low, double_low, whole_low, pair, summary],
        held,
        [lens, v1, x1, cotangent, stats1, bn_bias, decay, w_out, skip, w_glu],
    )

    flows = {}
    flows["top"] = Bulk(
        count, [act1, h1], [dz1, dy1], [(0, 0, 0, 0), (0, 0, 0, width), (1, 0, 1, 0)], [part]
    )
    flows["top"].send()

    def beside_top(level, group):
        if level == 0:
            return flows["top"].parts[-1:]
        if level == len(plan) - 1:
            flows["step"] = flows["top"].send(group)
        return ()

    held = exchange(1, part, plan, factors, False, True, beside_top)
    top = flows["top"]
    dv1, small1 = entered(
        functools.partial(adjoint_body, 1, plan, span, False),
        [pair_low, eight],
        held,
        [lens, g1, h1, v1, decay],
        [flows["step"]],
        weight=1 << 20,
    )
    part1, skip1, sums = run(
        functools.partial(input_body, 1, seqs, True),
        [whole, eight, tile],
        [dv1, dy1, x1, cotangent, stats1, bn_gain, bn_bias, w_in, skip],
        weight=1 << 20,
    )
    top.send([sums])
    sums = everywhere(sums)
    step = top.send([sums])
    d0, dz0, dy0, g0, grads1, part = run(
        functools.partial(back_body, 0, span, True),
        [whole, double_low, whole_low, pair, eight, summary],
        [lens, sums, part1, x1, mask, stats1, slope0, gate0, value0, bn_gain, decay, w_out, w_glu],
        [step],
    )

    flows["middle"] = Bulk(
        count, [act0], [dz0], [(0, 0, 0, 0), (0, 0, 0, width)], [part]
    )
    flows["middle"].send()

    def beside_middle(level, group):
        if level == 0:
            return flows["middle"].parts[-1:]
        if level == len(plan) - 2:
            flows["other"] = Bulk(
                count, [u1, h0], [dv1, dy0], [(0, 0, 0, 0), (1, seqs, 1, 0)], group[1:2], weight=1 << 20
            )
            flows["other"].send()
            return [top.send(group[1:2]), flows["other"].parts[-1]]
        if level == len(plan) - 1:
            flows["step"] = flows["middle"].send(group)
        return ()

    held = exchange(0, part, plan, factors, True, True, beside_middle)
    middle = flows["middle"]
    other = flows["other"]
    sent = other.send([held[-1][1]])
    dv0, small0 = entered(
        functools.partial(adjoint_body, 0, plan, span, True),
        [pair_low, eight],
        held,
        [lens, g0, h0, v0, decay],
        [flows["step"], sent],
        weight=1 << 20,
    )
    part0, skip0, sums = run(
        functools.partial(input_body, 0, seqs, False),
        [whole, eight, ((2, 8, width), F32)],
        [dv0, dy0, x0, d0, stats0, bn_gain, bn_bias, w_in, skip],
        weight=1 << 20,
    )

    (small,) = run(small_body, [((16, width), F32)], [small0, skip0, sums, small1, skip1], limit=4)
    step = middle.send([part0])
    step = top.settle([step])
    top.fetch()
    last = Bulk(count, [u0], [dv0], [(0, 0, 0, 0)], [step], [small], weight=1 << 20)
    last.send()
    step = last.parts[-1]
    step = top.fetch([step])
    step = other.send([step])
    step = last.send([step])
    step = middle.send([step])
    step = other.send([step])
    step = top.fetch([step])
    step = middle.send([step])
    step = last.send([step])
    step = other.send([step])
    step = middle.settle([step])
    middle.fetch()
    step = last.send([step])
    step = other.settle([step])
    other.fetch()
    step = top.fetch([step])
    step = middle.fetch([step])
    step = last.send([step])
    step = other.fetch([step])
    step = middle.fetch([step])
    step = last.settle([step])
    last.fetch()
    step = other.fetch([step])
    step = last.fetch([step])
    step = middle.fetch([step])
    step = last.fetch([step])
    step = other.fetch([step])
    step = top.fetch([step])
    step = last.fetch([step])
    step = middle.fetch([step])
    grad_x, g_gain, g_bias, g_nu, g_phase, g_skip, running_out = run(
        functools.partial(finish_body, span),
        [seq_major] + [((2, width), F32)] * 2 + [((2, states), F32)] * 2
        + [((2, width), F32), ((2, 2, width), F32)],
        [last.total, lens, part0, x0, mask, bn_gain, decay, running, stats0, stats1, grads1],
        [step],
    )
    step = other.fetch([g_gain])
    step = last.fetch([step])
    g_glu, g_out = unpack(
        count,
        [top],
        [[(0, 1, 0), (0, 1, width), (1, 1, 0)]],
        [(2, width, 2 * width), (2, 2 * states, width)],
    )
    g_glu, g_out, g_in = unpack(
        count,
        [middle, other, last],
        [
            [(0, 0, 0), (0, 0, width)],
            [(2, 1, 0), (1, 0, 0)],
            [(2, 0, 0)],
        ],
        [(2, width, 2 * width), (2, 2 * states, width), (2, width, 2 * states)],
        [g_glu, g_out],
    )
    return (output, grad_x, g_gain, g_bias, g_in, g_nu, g_phase, g_out, g_skip, g_glu, running_out)


def solution(mesh):
    placed = (P(None, "tm", None), P(), P(None, "tm", None)) + (P(),) * 9
    return jax.shard_map(
        shards,
        mesh=mesh,
        in_specs=placed,
        out_specs=(P(None, "tm", None),) * 2 + (P(),) * 9,
        check_vma=False,
    )
```
